512 devices in a mesh: tm: 64 (over x, z_lo, core), space: 8 (over y, z_hi).
Axes of the slice: x: 4, y: 4, z: 16 (z_hi: 2, z_lo: 8; z = z_hi * 8 + z_lo), core: 2. Of those that a mesh axis runs over, the one named last changes fastest.
Arguments:
- guess: float32 [64, 16, 192, 128], P('tm', 'space'), may hold values from -6 to 6
- source: float32 [64, 16, 192, 128], P('tm', 'space'), may hold values from -4 to 4
- diffusivity: float32 [16, 192, 128], P('space'), may hold values from 0.25 to 4
- initial: float32 [16, 192, 128], P('space'), may hold values from -6 to 6
Outputs:
- states: float32 [64, 16, 192, 128], P('tm', 'space')
The draws below stay inside these ranges and needn't reach their ends.
All inputs are finite; a program needn't handle non-finite values.
Results may differ from the reference program's by a relative error of at most 0.00002.
Values sent between devices are 32-bit elements; how exact they have to be, the bound alone decides.
No kernel may reach another device: no remote copies, remote signals or barrier semaphores. Data moves between devices by JAX's collectives and lax.ppermute only.
A program may use at most 64 MiB of HBM per device.

```python
import math
import jax
import jax.numpy as jnp
from jax import lax

SWEEPS = 2
NT = 64
NC = 8
NZ = 16
NY = 192
NX = 128


def draw_source(key, part):
    key = jax.random.fold_in(key, 11)
    values = jnp.clip(jax.random.normal(key, (NT, NZ, NY, NX), jnp.float32), -4.0, 4.0)
    return values.astype(jnp.float32)


def steps_of(key, shape, pieces, smallest, top_value):
    def one(axis_at, shards_of):
        draws = jax.random.uniform(jax.random.fold_in(jax.random.fold_in(key, 6), axis_at), (shards_of,), jnp.float32, smallest / len(pieces), top_value / len(pieces))
        return jnp.repeat(jnp.exp(draws), shape[axis_at] // shards_of).reshape((-1,) + (1,) * (len(shape) - axis_at - 1))

    loudness = one(*pieces[0])
    for cut in pieces[1:]:
        loudness = loudness * one(*cut)
    return loudness


def scatter_about(rng, dims, width, reach, split=(), held_as=jnp.bfloat16):
    values = jax.random.normal(rng, dims, jnp.float32) * width
    if len(split) > 0:
        values = steps_of(rng, dims, split, -0.22, 0.18) * values
    return jnp.clip(values, min=-reach, max=reach).astype(held_as)


def setup_inputs(seed: int = 0) -> dict:
    arg_keys = jax.random.split(jax.random.key(seed), 5)
    guess = scatter_about(arg_keys[0], (NT, NZ, NY, NX), 1.0, 6.0, ((0, 64), (1, 8)), jnp.float32)
    source = draw_source(jax.random.fold_in(arg_keys[4], 71), 0)
    diffusivity = jnp.clip(jnp.exp(math.log(4.0) - 2.7725887 * jax.random.uniform(arg_keys[2], (NZ, NY, NX), jnp.float32) ** steps_of(arg_keys[2], (NZ, NY, NX), ((0, 8),), -0.2, 0.2)), 0.25, 4.0)
    initial = scatter_about(arg_keys[3], (NZ, NY, NX), 1.0, 6.0, ((0, 8),), jnp.float32)
    return {"guess": guess, "source": source, "diffusivity": diffusivity, "initial": initial}


damping = 0.8
step_size = 0.5
coarse_size = 4.0
z_weight = 8.0


def sweep(field, target, conduct, rate):
    padded = jnp.pad(field, 1)
    cond_pad = jnp.pad(conduct, 1)
    shape_z, shape_y, shape_x = field.shape
    total = jnp.zeros_like(field)
    weighted = jnp.zeros_like(field)
    for axis_pos, weight in ((0, z_weight), (1, 1.0), (2, 1.0)):
        for offset in (0, 2):
            anchor = [1, 1, 1]
            anchor[axis_pos] = offset
            limits = [anchor[0] + shape_z, anchor[1] + shape_y, anchor[2] + shape_x]
            near_field = lax.slice(padded, anchor, limits)
            near_cond = lax.slice(cond_pad, anchor, limits)
            coeff = (rate * weight * 0.5) * (conduct + near_cond)
            total = total + coeff
            weighted = weighted + coeff * near_field
    return (1.0 - damping) * field + damping * (target + weighted) / (1.0 + total)


def reference(guess, source, diffusivity, initial):
    def fine_step(state, forcing):
        target = state + step_size * forcing
        field = state
        for sweep_index in range(SWEEPS):
            field = sweep(field, target, diffusivity, step_size)
        return field

    def coarse_step(error):
        field = error
        for sweep_index in range(SWEEPS):
            field = sweep(field, error, diffusivity, coarse_size)
        return field

    outputs = []
    residuals = []
    for block in range(NC):
        state = initial if block == 0 else guess[8 * block - 1]
        for inner in range(1, 8):
            state = fine_step(state, source[8 * block + inner - 1])
            outputs.append(state)
        residuals.append(fine_step(state, source[8 * block + 7]) - guess[8 * block + 7])
        outputs.append(guess[8 * block + 7])
    error = residuals[0]
    outputs[7] = guess[7] + error
    for block in range(1, NC):
        error = coarse_step(error) + residuals[block]
        outputs[8 * block + 7] = guess[8 * block + 7] + error
    return jnp.stack(outputs)
```

```python
import functools

import jax
import jax.numpy as jnp
from jax import lax
from jax.experimental import pallas as pl
from jax.experimental.pallas import tpu as pltpu
from jax.sharding import Mesh, PartitionSpec as P

SWEEPS = 2
F32 = jnp.float32

damping = 0.8
step_size = 0.5
coarse_size = 4.0
z_weight = 8.0

AXES = ("x", "zh", "zl", "core", "y", "zhi")
SIZES = (4, 2, 4, 2, 4, 2)
BLOCK = ("zl", "core", "y", "zhi")
BLOCKS = ("x", "zh")
NB = 8
NZ = 16
ROWS = 8
TILES = 24
CHIPS = 16
SIDE = 8
WIN = 3 * ROWS
LANES = 128


def chip_order(zl, y):
    return zl * 4 + (y if zl % 2 == 0 else 3 - y)


def block_index(zl, core, y, zhi):
    return ((zl * 2 + core) * 4 + y) * 2 + zhi


def neighbours(step):
    place = {chip_order(zl, y): zl * 4 + y for zl in range(4) for y in range(4)}
    return [(place[m], place[m + step]) for m in range(CHIPS) if 0 <= m + step < CHIPS]


def call(body, outs, *args, scratch=(), smem=0, flops=0):
    specs = [pl.BlockSpec(memory_space=pltpu.SMEM)] * smem
    specs += [pl.BlockSpec(memory_space=pltpu.VMEM)] * (len(args) - smem)
    out_specs = [pl.BlockSpec(memory_space=pltpu.VMEM)] * len(outs)
    size = sum(4 * a.size for a in args) + sum(4 * o.size for o in outs)
    return pl.pallas_call(
        body,
        out_shape=list(outs),
        in_specs=specs,
        out_specs=out_specs,
        scratch_shapes=list(scratch),
        compiler_params=pltpu.CompilerParams(vmem_limit_bytes=32 * 1024 * 1024),
        cost_estimate=pl.CostEstimate(flops=flops, bytes_accessed=size, transcendentals=0),
    )(*args)


def sds(*shape):
    return jax.ShapeDtypeStruct(shape, F32)


def scatter_body(j_ref, src_ref, guess_ref, cond_ref, init_ref, out_ref):
    place = j_ref[0]
    zero = jnp.zeros((ROWS, LANES), F32)
    for zl in range(4):
        for y in range(4):
            for zhi in range(2):
                tile = SIDE * zhi + chip_order(zl, y)
                rows = slice(tile * ROWS, (tile + 1) * ROWS)
                for core in range(2):
                    out_ref[block_index(zl, core, y, zhi), 0] = src_ref[core, rows]

    def fill(pick):
        for zl in range(4):
            for y in range(4):
                for zhi in range(2):
                    tile = SIDE * zhi + chip_order(zl, y)
                    for core in range(2):
                        out_ref[block_index(zl, core, y, zhi), 1] = pick(core, tile)

    def tile_of(ref, shift):
        def pick(core, tile):
            at = tile + shift
            if at < 0 or at >= TILES:
                return zero
            return ref[core, at * ROWS : (at + 1) * ROWS]

        return pick

    for where, ref, shift in ((0, cond_ref, 0), (1, cond_ref, 1), (2, cond_ref, -1), (3, init_ref, 0)):
        pl.when(place == where)(functools.partial(fill, tile_of(ref, shift)))
    pl.when(place > 3)(functools.partial(fill, tile_of(guess_ref, 0)))


def pack_body(first, all_ref, g_ref, up_ref, down_ref):
    row = lax.broadcasted_iota(jnp.int32, (ROWS, LANES), 0)
    for z in range(NZ):
        s, p = z // 2, z % 2
        g_ref[z] = all_ref[p, 7, s, 1]
        for phase in range(2):
            f = [all_ref[p, 4 * phase + n, s, 0] for n in range(4)]
            down_ref[2 * phase, z] = jnp.where(row < 7, f[0], pltpu.roll(f[3], 7, 0))
            down_ref[2 * phase + 1, z] = jnp.where(row < 5, f[1], pltpu.roll(f[2], 5, 0))
            up_ref[2 * phase, z] = jnp.where(row >= 1, f[0], pltpu.roll(f[3], 1, 0))
            up_ref[2 * phase + 1, z] = jnp.where(row >= 3, f[1], pltpu.roll(f[2], 3, 0))


def coefficients(rate, all_ref, k_s, co_s):
    zero = jnp.zeros((WIN, LANES), F32)
    for z in range(NZ):
        s, p = z // 2, z % 2
        k_s[z + 1, 0:8] = all_ref[p, 2, s, 1]
        k_s[z + 1, 8:16] = all_ref[p, 0, s, 1]
        k_s[z + 1, 16:24] = all_ref[p, 1, s, 1]
    k_s[0] = zero
    k_s[NZ + 1] = zero
    lane = lax.broadcasted_iota(jnp.int32, (WIN, LANES), 1)
    first = lane == 0
    last = lane == LANES - 1

    def layer(z, carry):
        k = k_s[z + 1]
        side = 0.5 * rate
        tall = 0.5 * rate * z_weight
        c = [
            tall * (k + k_s[z]),
            tall * (k + k_s[z + 2]),
            side * (k + pltpu.roll(k, 1, 0)),
            side * (k + pltpu.roll(k, WIN - 1, 0)),
            side * (k + jnp.where(first, 0.0, pltpu.roll(k, 1, 1))),
            side * (k + jnp.where(last, 0.0, pltpu.roll(k, LANES - 1, 1))),
        ]
        total = ((c[0] + c[1]) + (c[2] + c[3])) + (c[4] + c[5])
        d = jnp.where(k > 0.0, damping / (1.0 + total), 0.0)
        co_s[0, z] = c[0] * d
        co_s[1, z] = c[1] * d
        co_s[2, z] = c[2] * d
        co_s[3, z] = c[3] * d
        co_s[4, z] = jnp.where(first, 0.0, c[4] * d)
        co_s[5, z] = jnp.where(last, 0.0, c[5] * d)
        co_s[6, z] = d
        return carry

    lax.fori_loop(0, NZ, layer, 0)


def one_sweep(src, dst, co_s, db_s):
    for z in range(NZ):
        w = src[z + 1]
        acc = (db_s[z] + (1.0 - damping) * w) + (co_s[0, z] * src[z] + co_s[1, z] * src[z + 2])
        acc = acc + (co_s[2, z] * pltpu.roll(w, 1, 0) + co_s[3, z] * pltpu.roll(w, WIN - 1, 0))
        acc = acc + (co_s[4, z] * pltpu.roll(w, 1, 1) + co_s[5, z] * pltpu.roll(w, LANES - 1, 1))
        dst[z + 1] = acc


def load_window(a_s, own_ref, below_ref, above_ref, b_s):
    zero = jnp.zeros((WIN, LANES), F32)
    for ref in (a_s, b_s):
        ref[0] = zero
        ref[NZ + 1] = zero
    for z in range(NZ):
        a_s[z + 1, 0:8] = below_ref[z]
        a_s[z + 1, 8:16] = own_ref[z]
        a_s[z + 1, 16:24] = above_ref[z]


def fine_body(phase, all_ref, fb_ref, fa_ref, own_ref, below_ref, above_ref, *rest):
    if phase == 0:
        out_ref, end_ref, k_s, co_s, a_s, b_s, db_s = rest
    else:
        out_ref, end_ref, k_s, co_s, a_s, b_s, db_s = rest
    coefficients(step_size, all_ref, k_s, co_s)
    load_window(a_s, own_ref, below_ref, above_ref, b_s)
    for n in range(4):
        tile, turn = ((0, 0), (1, 0), (1, 5), (0, 7))[n]
        for z in range(NZ):
            s, p = z // 2, z % 2
            below = fb_ref[2 * phase + tile, z]
            above = fa_ref[2 * phase + tile, z]
            if turn:
                below = pltpu.roll(below, turn, 0)
                above = pltpu.roll(above, ROWS - turn, 0)
            forcing = jnp.concatenate([below, all_ref[p, 4 * phase + n, s, 0], above], axis=0)
            db_s[z] = co_s[6, z] * (a_s[z + 1] + step_size * forcing)
        one_sweep(a_s, b_s, co_s, db_s)
        one_sweep(b_s, a_s, co_s, db_s)
        for z in range(NZ):
            s, p = z // 2, z % 2
            mine = a_s[z + 1, 8:16]
            if n < 3:
                out_ref[n, z] = mine
            elif phase == 0:
                out_ref[n, z] = mine
                end_ref[z] = mine
            else:
                end_ref[z] = mine - all_ref[p, 7, s, 1]


def coarse_body(steps, all_ref, own_ref, below_ref, above_ref, out_ref, end_ref, k_s, co_s, a_s, b_s, db_s):
    coefficients(coarse_size, all_ref, k_s, co_s)
    load_window(a_s, own_ref, below_ref, above_ref, b_s)
    for n in range(steps):
        for z in range(NZ):
            db_s[z] = co_s[6, z] * a_s[z + 1]
        one_sweep(a_s, b_s, co_s, db_s)
        one_sweep(b_s, a_s, co_s, db_s)
        for z in range(NZ):
            mine = a_s[z + 1, 8:16]
            out_ref[n, z] = mine
            if n == steps - 1:
                end_ref[z] = mine


SWEEP_SCRATCH = (
    pltpu.VMEM((NZ + 2, WIN, LANES), F32),
    pltpu.VMEM((7, NZ, WIN, LANES), F32),
    pltpu.VMEM((NZ + 2, WIN, LANES), F32),
    pltpu.VMEM((NZ + 2, WIN, LANES), F32),
    pltpu.VMEM((NZ, WIN, LANES), F32),
)


def powers_body(place_ref, r_ref, z1_ref, z2_ref, out_ref):
    c, p = place_ref[0], place_ref[1]
    for b in range(NB):

        @pl.when(b == c)
        def _():
            for s in range(8):
                out_ref[b, s] = r_ref[2 * s + p]

        @pl.when((b > c) & (b <= c + 4))
        def _():
            n = jnp.clip(b - c - 1, 0, 3)
            for s in range(8):
                out_ref[b, s] = z1_ref[n, 2 * s + p]

        @pl.when(b > c + 4)
        def _():
            n = jnp.clip(b - c - 5, 0, 2)
            for s in range(8):
                out_ref[b, s] = z2_ref[n, 2 * s + p]

        @pl.when(b < c)
        def _():
            out_ref[b] = jnp.zeros((8, ROWS, LANES), F32)


def collect_body(place_ref, got_ref, v1_ref, v2_ref, out_ref):
    p = place_ref[1]
    for s in range(8):
        total = got_ref[0, s]
        for b in range(1, NB):
            total = total + got_ref[b, s]
        out_ref[7 * 8 + s] = total
        for n in range(4):
            out_ref[n * 8 + s] = v1_ref[n, 2 * s + p]
        for n in range(3):
            out_ref[(4 + n) * 8 + s] = v2_ref[n, 2 * s + p]


def home_body(j_ref, got_ref, guess_ref, out_ref):
    last = j_ref[0] == 7

    def write(add):
        for tile in range(TILES):
            zhi = 0 if tile < TILES // 2 else 1
            m = tile - SIDE * zhi
            zl, y = m // 4, m % 4
            if zl % 2 == 1:
                y = 3 - y
            rows = slice(tile * ROWS, (tile + 1) * ROWS)
            for core in range(2):
                value = got_ref[block_index(zl, core, y, zhi)]
                if add:
                    value = guess_ref[core, rows] + value
                out_ref[core, rows] = value

    pl.when(last)(functools.partial(write, True))
    pl.when(jnp.logical_not(last))(functools.partial(write, False))


def on_device(guess, source, diffusivity, initial):
    guess = guess[0]
    source = source[0]
    core = lax.axis_index("core")
    place = lax.axis_index(("zl", "core"))[None]
    block = lax.axis_index(BLOCKS)
    block_core = jnp.stack([block, core])

    (sent,) = call(scatter_body, [sds(64, 2, ROWS, LANES)], place, source, guess, diffusivity, initial, smem=1)
    strips = lax.all_to_all(sent, BLOCK, 0, 0, tiled=True)
    both = lax.all_gather(strips, "core").reshape(2, 8, 8, 2, ROWS, LANES)

    own_g, f_up, f_down = call(
        functools.partial(pack_body, 0),
        [sds(NZ, ROWS, LANES), sds(4, NZ, ROWS, LANES), sds(4, NZ, ROWS, LANES)],
        both,
    )
    shifted = lax.ppermute(own_g, BLOCKS, [(b, b + 1) for b in range(NB - 1)])

    def exchange(mine):
        below = lax.ppermute(mine, ("zl", "y"), neighbours(1))
        above = lax.ppermute(mine, ("zl", "y"), neighbours(-1))
        return below, above

    f_below = lax.ppermute(f_up, ("zl", "y"), neighbours(1))
    f_above = lax.ppermute(f_down, ("zl", "y"), neighbours(-1))
    first = both[:, 3, :, 1].transpose(1, 0, 2, 3).reshape(NZ, ROWS, LANES)
    v0 = jnp.where(block == 0, first, shifted)
    below, above = exchange(v0)
    sweep_flops = 8 * NZ * WIN * LANES * 15
    v_first, v4 = call(
        functools.partial(fine_body, 0),
        [sds(4, NZ, ROWS, LANES), sds(NZ, ROWS, LANES)],
        both, f_below, f_above, v0, below, above,
        scratch=SWEEP_SCRATCH, flops=sweep_flops,
    )
    below, above = exchange(v4)
    v_second, residual = call(
        functools.partial(fine_body, 1),
        [sds(3, NZ, ROWS, LANES), sds(NZ, ROWS, LANES)],
        both, f_below, f_above, v4, below, above,
        scratch=SWEEP_SCRATCH, flops=sweep_flops,
    )
    below, above = exchange(residual)
    z_first, z4 = call(
        functools.partial(coarse_body, 4),
        [sds(4, NZ, ROWS, LANES), sds(NZ, ROWS, LANES)],
        both, residual, below, above,
        scratch=SWEEP_SCRATCH, flops=sweep_flops,
    )
    below, above = exchange(z4)
    z_second, _ = call(
        functools.partial(coarse_body, 3),
        [sds(3, NZ, ROWS, LANES), sds(NZ, ROWS, LANES)],
        both, z4, below, above,
        scratch=SWEEP_SCRATCH, flops=sweep_flops,
    )
    (outgoing,) = call(powers_body, [sds(NB, 8, ROWS, LANES)], block_core, residual, z_first, z_second, smem=1)
    arrived = lax.all_to_all(outgoing, BLOCKS, 0, 0, tiled=True)
    (back,) = call(collect_body, [sds(64, ROWS, LANES)], block_core, arrived, v_first, v_second, smem=1)
    returned = lax.all_to_all(back, BLOCK, 0, 0, tiled=True)
    (result,) = call(home_body, [sds(2, TILES * ROWS, LANES)], place, returned, guess, smem=1)
    return result[None]


def solution(mesh):
    fine = Mesh(mesh.devices.reshape(SIZES), AXES)
    tm = ("x", "zh", "zl", "core")
    space = ("y", "zhi")
    in_specs = (P(tm, space, None, None), P(tm, space, None, None), P(space, None, None), P(space, None, None))
    out_specs = P(tm, space, None, None)
    return jax.shard_map(on_device, mesh=fine, in_specs=in_specs, out_specs=out_specs, check_vma=False)
```

```python
import functools

import jax
import jax.numpy as jnp
from jax import lax
from jax.experimental import pallas as pl
from jax.experimental.pallas import tpu as pltpu
from jax.sharding import Mesh, PartitionSpec as P

SWEEPS = 2
F32 = jnp.float32

damping = 0.8
step_size = 0.5
coarse_size = 4.0
z_weight = 8.0

AXES = ("x", "zh", "zl", "core", "y", "zhi")
SIZES = (4, 2, 4, 2, 4, 2)
BLOCK = ("zl", "core", "y", "zhi")
BLOCKS = ("x", "zh")
NB = 8
NZ = 16
ROWS = 8
TILES = 24
CHIPS = 16
SIDE = 8
WIN = 3 * ROWS
LANES = 128


def chip_order(zl, y):
    return zl * 4 + (y if zl % 2 == 0 else 3 - y)


def block_index(zl, core, y, zhi):
    return ((zl * 2 + core) * 4 + y) * 2 + zhi


def neighbours(step):
    place = {chip_order(zl, y): zl * 4 + y for zl in range(4) for y in range(4)}
    return [(place[m], place[m + step]) for m in range(CHIPS) if 0 <= m + step < CHIPS]


def call(body, outs, *args, scratch=(), smem=0, flops=0):
    specs = [pl.BlockSpec(memory_space=pltpu.SMEM)] * smem
    specs += [pl.BlockSpec(memory_space=pltpu.VMEM)] * (len(args) - smem)
    out_specs = [pl.BlockSpec(memory_space=pltpu.VMEM)] * len(outs)
    size = sum(4 * a.size for a in args) + sum(4 * o.size for o in outs)
    return pl.pallas_call(
        body,
        out_shape=list(outs),
        in_specs=specs,
        out_specs=out_specs,
        scratch_shapes=list(scratch),
        compiler_params=pltpu.CompilerParams(vmem_limit_bytes=32 * 1024 * 1024),
        cost_estimate=pl.CostEstimate(flops=flops, bytes_accessed=size, transcendentals=0),
    )(*args)


def sds(*shape):
    return jax.ShapeDtypeStruct(shape, F32)


def scatter_body(j_ref, src_hbm, guess_hbm, cond_hbm, init_hbm, out_ref, src_ref, extra_ref, sems):
    place = j_ref[0]
    zero = jnp.zeros((ROWS, LANES), F32)
    source_copy = pltpu.make_async_copy(src_hbm, src_ref, sems.at[0])
    source_copy.start()

    @pl.when(place < 3)
    def _():
        pltpu.make_async_copy(cond_hbm, extra_ref, sems.at[1]).start()

    @pl.when(place == 3)
    def _():
        pltpu.make_async_copy(init_hbm, extra_ref, sems.at[1]).start()

    @pl.when(place > 3)
    def _():
        pltpu.make_async_copy(guess_hbm, extra_ref, sems.at[1]).start()

    def each():
        for zl in range(4):
            for y in range(4):
                for zhi in range(2):
                    tile = SIDE * zhi + chip_order(zl, y)
                    for core in range(2):
                        yield block_index(zl, core, y, zhi), core, tile

    source_copy.wait()
    for at, core, tile in each():
        out_ref[at, 0] = src_ref[core, tile * ROWS : (tile + 1) * ROWS]
    pltpu.make_async_copy(guess_hbm, extra_ref, sems.at[1]).wait()

    def fill(shift):
        for at, core, tile in each():
            tile = tile + shift
            if 0 <= tile < TILES:
                out_ref[at, 1] = extra_ref[core, tile * ROWS : (tile + 1) * ROWS]
            else:
                out_ref[at, 1] = zero

    pl.when(place == 1)(functools.partial(fill, 1))
    pl.when(place == 2)(functools.partial(fill, -1))
    pl.when((place != 1) & (place != 2))(functools.partial(fill, 0))


def pack_body(core_ref, own_ref, other_ref, f_ref, g_ref, k_ref, first_ref, up_ref, down_ref):
    def order(halves):
        for z in range(NZ):
            s, p = z // 2, z % 2
            half = halves[p]
            for n in range(8):
                f_ref[n, z] = half[n, s, 0]
            g_ref[z] = half[7, s, 1]
            k_ref[z, 0:8] = half[2, s, 1]
            k_ref[z, 8:16] = half[0, s, 1]
            k_ref[z, 16:24] = half[1, s, 1]
            first_ref[z] = half[3, s, 1]

    pl.when(core_ref[0] == 0)(functools.partial(order, (own_ref, other_ref)))
    pl.when(core_ref[0] == 1)(functools.partial(order, (other_ref, own_ref)))
    row = lax.broadcasted_iota(jnp.int32, (ROWS, LANES), 0)
    for z in range(NZ):
        for phase in range(2):
            f = [f_ref[4 * phase + n, z] for n in range(4)]
            down_ref[2 * phase, z] = jnp.where(row < 7, f[0], pltpu.roll(f[3], 7, 0))
            down_ref[2 * phase + 1, z] = jnp.where(row < 5, f[1], pltpu.roll(f[2], 5, 0))
            up_ref[2 * phase, z] = jnp.where(row >= 1, f[0], pltpu.roll(f[3], 1, 0))
            up_ref[2 * phase + 1, z] = jnp.where(row >= 3, f[1], pltpu.roll(f[2], 3, 0))


def coefficients(rate, k_ref, k_s, co_s):
    zero = jnp.zeros((WIN, LANES), F32)
    for z in range(NZ):
        k_s[z + 1] = k_ref[z]
    k_s[0] = zero
    k_s[NZ + 1] = zero
    lane = lax.broadcasted_iota(jnp.int32, (WIN, LANES), 1)
    first = lane == 0
    last = lane == LANES - 1

    def layer(z, carry):
        k = k_s[z + 1]
        side = 0.5 * rate
        tall = 0.5 * rate * z_weight
        c = [
            tall * (k + k_s[z]),
            tall * (k + k_s[z + 2]),
            side * (k + pltpu.roll(k, 1, 0)),
            side * (k + pltpu.roll(k, WIN - 1, 0)),
            side * (k + jnp.where(first, 0.0, pltpu.roll(k, 1, 1))),
            side * (k + jnp.where(last, 0.0, pltpu.roll(k, LANES - 1, 1))),
        ]
        total = ((c[0] + c[1]) + (c[2] + c[3])) + (c[4] + c[5])
        d = jnp.where(k > 0.0, damping / (1.0 + total), 0.0)
        co_s[0, z] = c[0] * d
        co_s[1, z] = c[1] * d
        co_s[2, z] = c[2] * d
        co_s[3, z] = c[3] * d
        co_s[4, z] = jnp.where(first, 0.0, c[4] * d)
        co_s[5, z] = jnp.where(last, 0.0, c[5] * d)
        co_s[6, z] = d
        return carry

    lax.fori_loop(0, NZ, layer, 0)


def one_sweep(src, dst, co_s, db_s):
    for z in range(NZ):
        w = src[z + 1]
        acc = (db_s[z] + (1.0 - damping) * w) + (co_s[0, z] * src[z] + co_s[1, z] * src[z + 2])
        acc = acc + (co_s[2, z] * pltpu.roll(w, 1, 0) + co_s[3, z] * pltpu.roll(w, WIN - 1, 0))
        acc = acc + (co_s[4, z] * pltpu.roll(w, 1, 1) + co_s[5, z] * pltpu.roll(w, LANES - 1, 1))
        dst[z + 1] = acc


def load_window(a_s, own_ref, below_ref, above_ref, b_s):
    zero = jnp.zeros((WIN, LANES), F32)
    for ref in (a_s, b_s):
        ref[0] = zero
        ref[NZ + 1] = zero
    for z in range(NZ):
        a_s[z + 1, 0:8] = below_ref[z]
        a_s[z + 1, 8:16] = own_ref[z]
        a_s[z + 1, 16:24] = above_ref[z]


def fine_steps(phase, f_ref, fb_ref, fa_ref, co_s, a_s, b_s, db_s, keep):
    for n in range(4):
        tile, turn = ((0, 0), (1, 0), (1, 5), (0, 7))[n]
        for z in range(NZ):
            below = fb_ref[2 * phase + tile, z]
            above = fa_ref[2 * phase + tile, z]
            if turn:
                below = pltpu.roll(below, turn, 0)
                above = pltpu.roll(above, ROWS - turn, 0)
            forcing = jnp.concatenate([below, f_ref[4 * phase + n, z], above], axis=0)
            db_s[z] = co_s[6, z] * (a_s[z + 1] + step_size * forcing)
        one_sweep(a_s, b_s, co_s, db_s)
        one_sweep(b_s, a_s, co_s, db_s)
        for z in range(NZ):
            keep(n, z, a_s[z + 1, 8:16])


def early_body(k_ref, f_ref, fb_ref, fa_ref, own_ref, below_ref, above_ref, out_ref, end_ref, k_s, co_s, a_s, b_s, db_s):
    coefficients(step_size, k_ref, k_s, co_s)
    load_window(a_s, own_ref, below_ref, above_ref, b_s)

    def keep(n, z, mine):
        out_ref[n, z] = mine
        if n == 3:
            end_ref[z] = mine

    fine_steps(0, f_ref, fb_ref, fa_ref, co_s, a_s, b_s, db_s, keep)


def late_body(
    core_ref, k_ref, f_ref, fb_ref, fa_ref, own_ref, below_ref, above_ref, g_ref, early_ref,
    out_ref, res_ref, k_s, co_s, a_s, b_s, db_s, late_s,
):
    coefficients(step_size, k_ref, k_s, co_s)
    load_window(a_s, own_ref, below_ref, above_ref, b_s)

    def keep(n, z, mine):
        if n < 3:
            late_s[n, z] = mine
        else:
            res_ref[z] = mine - g_ref[z]

    fine_steps(1, f_ref, fb_ref, fa_ref, co_s, a_s, b_s, db_s, keep)
    core = core_ref[0]
    for y in range(4):
        for zhi in range(2):
            z = 2 * (2 * y + zhi) + core
            for n in range(4):
                out_ref[zhi, n, y] = early_ref[n, z]
            for n in range(3):
                out_ref[zhi, 4 + n, y] = late_s[n, z]


def coarse_steps(steps, co_s, a_s, b_s, db_s, keep):
    for n in range(steps):
        for z in range(NZ):
            db_s[z] = co_s[6, z] * a_s[z + 1]
        one_sweep(a_s, b_s, co_s, db_s)
        one_sweep(b_s, a_s, co_s, db_s)
        for z in range(NZ):
            keep(n, z, a_s[z + 1, 8:16])


def powers_early_body(k_ref, own_ref, below_ref, above_ref, out_ref, end_ref, k_s, co_s, a_s, b_s, db_s):
    coefficients(coarse_size, k_ref, k_s, co_s)
    load_window(a_s, own_ref, below_ref, above_ref, b_s)

    def keep(n, z, mine):
        out_ref[n, z] = mine
        if n == 3:
            end_ref[z] = mine

    coarse_steps(4, co_s, a_s, b_s, db_s, keep)


def powers_late_body(
    place_ref, k_ref, own_ref, below_ref, above_ref, res_ref, early_ref, out_ref, k_s, co_s, a_s, b_s, db_s, pow_s
):
    coefficients(coarse_size, k_ref, k_s, co_s)
    load_window(a_s, own_ref, below_ref, above_ref, b_s)
    for z in range(NZ):
        pow_s[0, z] = res_ref[z]
        for n in range(4):
            pow_s[1 + n, z] = early_ref[n, z]

    def keep(n, z, mine):
        pow_s[5 + n, z] = mine

    coarse_steps(3, co_s, a_s, b_s, db_s, keep)
    c, core = place_ref[0], place_ref[1]
    for b in range(NB):
        power = jnp.clip(b - c, 0, NB - 1)
        live = b >= c
        for y in range(4):
            for zhi in range(2):
                value = pow_s[power, 2 * (2 * y + zhi) + core]
                out_ref[2 * b + zhi, y] = jnp.where(live, value, 0.0)


SWEEP_SCRATCH = (
    pltpu.VMEM((NZ + 2, WIN, LANES), F32),
    pltpu.VMEM((7, NZ, WIN, LANES), F32),
    pltpu.VMEM((NZ + 2, WIN, LANES), F32),
    pltpu.VMEM((NZ + 2, WIN, LANES), F32),
    pltpu.VMEM((NZ, WIN, LANES), F32),
)


def collect_body(got_ref, v_ref, out_ref):
    for side in range(2):
        for y in range(4):
            total = got_ref[side, y]
            for b in range(1, NB):
                total = total + got_ref[2 * b + side, y]
            out_ref[7 * 4 + y, side] = total
            for n in range(7):
                out_ref[n * 4 + y, side] = v_ref[side, n, y]


def home_body(j_ref, got_ref, guess_ref, out_ref):
    last = j_ref[0] == 7

    def write(add):
        for tile in range(TILES):
            zhi = 0 if tile < TILES // 2 else 1
            m = tile - SIDE * zhi
            zl, y = m // 4, m % 4
            if zl % 2 == 1:
                y = 3 - y
            rows = slice(tile * ROWS, (tile + 1) * ROWS)
            for core in range(2):
                value = got_ref[(zl * 2 + core) * 4 + y, zhi]
                if add:
                    value = guess_ref[core, rows] + value
                out_ref[core, rows] = value

    pl.when(last)(functools.partial(write, True))
    pl.when(jnp.logical_not(last))(functools.partial(write, False))


def on_device(guess, source, diffusivity, initial):
    guess = guess[0]
    source = source[0]
    core = lax.axis_index("core")
    place = lax.axis_index(("zl", "core"))[None]
    block = lax.axis_index(BLOCKS)
    block_core = jnp.stack([block, core])

    sent = pl.pallas_call(
        scatter_body,
        out_shape=sds(64, 2, ROWS, LANES),
        in_specs=[pl.BlockSpec(memory_space=pltpu.SMEM)] + [pl.BlockSpec(memory_space=pltpu.HBM)] * 4,
        out_specs=pl.BlockSpec(memory_space=pltpu.VMEM),
        scratch_shapes=[
            pltpu.VMEM((2, TILES * ROWS, LANES), F32),
            pltpu.VMEM((2, TILES * ROWS, LANES), F32),
            pltpu.SemaphoreType.DMA((2,)),
        ],
        compiler_params=pltpu.CompilerParams(vmem_limit_bytes=32 * 1024 * 1024),
    )(place, source, guess, diffusivity, initial)
    strips = lax.all_to_all(sent, BLOCK, 0, 0, tiled=True).reshape(8, 8, 2, ROWS, LANES)
    other = lax.ppermute(strips, "core", [(0, 1), (1, 0)])

    f, g, k, first, f_up, f_down = call(
        pack_body,
        [sds(8, NZ, ROWS, LANES), sds(NZ, ROWS, LANES), sds(NZ, WIN, LANES), sds(NZ, ROWS, LANES)]
        + [sds(4, NZ, ROWS, LANES)] * 2,
        core[None], strips, other, smem=1,
    )

    def exchange(up, down):
        below = lax.ppermute(up, ("zl", "y"), neighbours(1))
        above = lax.ppermute(down, ("zl", "y"), neighbours(-1))
        return below, above

    f_below, f_above = exchange(f_up, f_down)
    shifted = lax.ppermute(g, BLOCKS, [(b, b + 1) for b in range(NB - 1)])
    v0 = jnp.where(block == 0, first, shifted)
    below, above = exchange(v0, v0)
    flops = 8 * NZ * WIN * LANES * 15
    v_early, v4 = call(
        early_body, [sds(4, NZ, ROWS, LANES), sds(NZ, ROWS, LANES)],
        k, f, f_below, f_above, v0, below, above, scratch=SWEEP_SCRATCH, flops=flops,
    )
    below, above = exchange(v4, v4)
    v, residual = call(
        late_body, [sds(2, 7, 4, ROWS, LANES), sds(NZ, ROWS, LANES)],
        core[None], k, f, f_below, f_above, v4, below, above, g, v_early, smem=1,
        scratch=SWEEP_SCRATCH + (pltpu.VMEM((3, NZ, ROWS, LANES), F32),), flops=flops,
    )
    below, above = exchange(residual, residual)
    v = lax.all_to_all(v, "zhi", 0, 0, tiled=True)
    z_early, z4 = call(
        powers_early_body, [sds(4, NZ, ROWS, LANES), sds(NZ, ROWS, LANES)],
        k, residual, below, above, scratch=SWEEP_SCRATCH, flops=flops,
    )
    below, above = exchange(z4, z4)
    (powers,) = call(
        powers_late_body, [sds(2 * NB, 4, ROWS, LANES)],
        block_core, k, z4, below, above, residual, z_early, smem=1,
        scratch=SWEEP_SCRATCH + (pltpu.VMEM((NB, NZ, ROWS, LANES), F32),), flops=flops,
    )
    arrived = lax.all_to_all(powers, BLOCKS + ("zhi",), 0, 0, tiled=True)
    (back,) = call(collect_body, [sds(32, 2, ROWS, LANES)], arrived, v)
    returned = lax.all_to_all(back, ("zl", "core", "y"), 0, 0, tiled=True)
    (result,) = call(home_body, [sds(2, TILES * ROWS, LANES)], place, returned, guess, smem=1)
    return result[None]


def solution(mesh):
    fine = Mesh(mesh.devices.reshape(SIZES), AXES)
    tm = ("x", "zh", "zl", "core")
    space = ("y", "zhi")
    in_specs = (P(tm, space, None, None), P(tm, space, None, None), P(space, None, None), P(space, None, None))
    out_specs = P(tm, space, None, None)
    return jax.shard_map(on_device, mesh=fine, in_specs=in_specs, out_specs=out_specs, check_vma=False)
```

```python
import functools

import jax
import jax.numpy as jnp
from jax import lax
from jax.experimental import pallas as pl
from jax.experimental.pallas import tpu as pltpu
from jax.sharding import Mesh, PartitionSpec as P

SWEEPS = 2
F32 = jnp.float32

damping = 0.8
step_size = 0.5
coarse_size = 4.0
z_weight = 8.0

AXES = ("x", "zh", "zl", "core", "y", "zhi")
SIZES = (4, 2, 4, 2, 4, 2)
BLOCK = ("zl", "core", "y", "zhi")
BLOCKS = ("x", "zh")
NB = 8
NZ = 16
ROWS = 8
TILES = 24
CHIPS = 16
SIDE = 8
HALO = 2 * ROWS
WIN = ROWS + 2 * HALO
LANES = 128


def chip_order(zl, y):
    return zl * 4 + (y if zl % 2 == 0 else 3 - y)


def block_index(zl, core, y, zhi):
    return ((zl * 2 + core) * 4 + y) * 2 + zhi


def neighbours(step):
    place = {chip_order(zl, y): zl * 4 + y for zl in range(4) for y in range(4)}
    return [(place[m], place[m + step]) for m in range(CHIPS) if 0 <= m + step < CHIPS]


def call(body, outs, *args, scratch=(), smem=0, flops=0):
    specs = [pl.BlockSpec(memory_space=pltpu.SMEM)] * smem
    specs += [pl.BlockSpec(memory_space=pltpu.VMEM)] * (len(args) - smem)
    out_specs = [pl.BlockSpec(memory_space=pltpu.VMEM)] * len(outs)
    size = sum(4 * a.size for a in args) + sum(4 * o.size for o in outs)
    return pl.pallas_call(
        body,
        out_shape=list(outs),
        in_specs=specs,
        out_specs=out_specs,
        scratch_shapes=list(scratch),
        compiler_params=pltpu.CompilerParams(vmem_limit_bytes=32 * 1024 * 1024),
        cost_estimate=pl.CostEstimate(flops=flops, bytes_accessed=size, transcendentals=0),
    )(*args)


def sds(*shape):
    return jax.ShapeDtypeStruct(shape, F32)


def scatter_body(j_ref, src_hbm, guess_hbm, cond_hbm, init_hbm, out_ref, src_ref, extra_ref, sems):
    place = j_ref[0]
    zero = jnp.zeros((ROWS, LANES), F32)
    source_copy = pltpu.make_async_copy(src_hbm, src_ref, sems.at[0])
    source_copy.start()

    @pl.when((place != 3) & (place < 6))
    def _():
        pltpu.make_async_copy(cond_hbm, extra_ref, sems.at[1]).start()

    @pl.when(place == 3)
    def _():
        pltpu.make_async_copy(init_hbm, extra_ref, sems.at[1]).start()

    @pl.when(place > 5)
    def _():
        pltpu.make_async_copy(guess_hbm, extra_ref, sems.at[1]).start()

    def each():
        for zl in range(4):
            for y in range(4):
                for zhi in range(2):
                    tile = SIDE * zhi + chip_order(zl, y)
                    for core in range(2):
                        yield block_index(zl, core, y, zhi), core, tile

    source_copy.wait()
    for at, core, tile in each():
        out_ref[at, 0] = src_ref[core, tile * ROWS : (tile + 1) * ROWS]
    pltpu.make_async_copy(guess_hbm, extra_ref, sems.at[1]).wait()

    def fill(shift):
        for at, core, tile in each():
            tile = tile + shift
            if 0 <= tile < TILES:
                out_ref[at, 1] = extra_ref[core, tile * ROWS : (tile + 1) * ROWS]
            else:
                out_ref[at, 1] = zero

    pl.when(place == 1)(functools.partial(fill, 1))
    pl.when(place == 2)(functools.partial(fill, -1))
    pl.when(place == 4)(functools.partial(fill, 2))
    pl.when(place == 5)(functools.partial(fill, -2))
    pl.when((place == 0) | (place == 3) | (place > 5))(functools.partial(fill, 0))


def pack_body(strip_ref, start_ref, up1_ref, up2_ref, down1_ref, down2_ref):
    row = lax.broadcasted_iota(jnp.int32, (ROWS, LANES), 0)
    for s in range(8):
        start_ref[s] = strip_ref[7, s, 1]
        for n in range(4):
            up1_ref[n, s] = strip_ref[n, s, 0]
            down1_ref[n, s] = strip_ref[n, s, 0]
        for phase, up_ref, down_ref, at in ((0, up2_ref, down2_ref, 0), (1, up1_ref, down1_ref, 4)):
            f = [strip_ref[4 * phase + n, s, 0] for n in range(4)]
            down_ref[at, s] = jnp.where(row < 7, f[0], pltpu.roll(f[3], 7, 0))
            down_ref[at + 1, s] = jnp.where(row < 5, f[1], pltpu.roll(f[2], 5, 0))
            up_ref[at, s] = jnp.where(row >= 1, f[0], pltpu.roll(f[3], 1, 0))
            up_ref[at + 1, s] = jnp.where(row >= 3, f[1], pltpu.roll(f[2], 3, 0))


def in_order(core_ref, body, mine, other):
    pl.when(core_ref[0] == 0)(functools.partial(body, (mine, other)))
    pl.when(core_ref[0] == 1)(functools.partial(body, (other, mine)))


def merge_body(core_ref, block_ref, half_ref, half2_ref, strip_ref, strip2_ref, out_ref):
    first = block_ref[0] == 0

    def body(halves):
        for z in range(NZ):
            half, strip = halves[z % 2]
            out_ref[z] = jnp.where(first, strip[3, z // 2, 1], half[z // 2])

    in_order(core_ref, body, (half_ref, strip_ref), (half2_ref, strip2_ref))


def load_diffusivity(core_ref, mine_ref, other_ref, k_s):
    def body(halves):
        for z in range(NZ):
            half, s = halves[z % 2], z // 2
            for place, at in ((5, 0), (2, 8), (0, 16), (1, 24), (4, 32)):
                k_s[z + 1, at : at + 8] = half[place, s, 1]

    in_order(core_ref, body, mine_ref, other_ref)
    zero = jnp.zeros((WIN, LANES), F32)
    k_s[0] = zero
    k_s[NZ + 1] = zero


def load_sources(core_ref, mine, other, f_s):
    zero = jnp.zeros((ROWS, LANES), F32)

    def body(halves):
        for z in range(NZ):
            (strip, halo), s = halves[z % 2], z // 2
            for n in range(8):
                f_s[n, z, 16:24] = strip[n, s, 0]
            for n in range(4):
                f_s[n, z, 8:16] = halo[n, s]
                f_s[n, z, 24:32] = halo[8 + n, s]
                f_s[4 + n, z, 0:8] = zero
                f_s[4 + n, z, 32:40] = zero
            for first, at, below, above in ((0, 0, 6, 14), (4, 8, 4, 12)):
                low, high = slice(at, at + 8), slice(32 - at, 40 - at)
                f_s[first, z, low] = halo[below, s]
                f_s[first + 1, z, low] = halo[below + 1, s]
                f_s[first + 2, z, low] = pltpu.roll(halo[below + 1, s], 5, 0)
                f_s[first + 3, z, low] = pltpu.roll(halo[below, s], 7, 0)
                f_s[first, z, high] = halo[above, s]
                f_s[first + 1, z, high] = halo[above + 1, s]
                f_s[first + 2, z, high] = pltpu.roll(halo[above + 1, s], 3, 0)
                f_s[first + 3, z, high] = pltpu.roll(halo[above, s], 1, 0)

    in_order(core_ref, body, mine, other)


def load_window(a_s, b_s, own_ref, below2_ref, below1_ref, above1_ref, above2_ref):
    zero = jnp.zeros((WIN, LANES), F32)
    for ref in (a_s, b_s):
        ref[0] = zero
        ref[NZ + 1] = zero
    for z in range(NZ):
        for n, ref in enumerate((below2_ref, below1_ref, own_ref, above1_ref, above2_ref)):
            a_s[z + 1, 8 * n : 8 * n + 8] = ref[z]


def coefficients(rate, k_s, co_s):
    lane = lax.broadcasted_iota(jnp.int32, (WIN, LANES), 1)
    first = lane == 0
    last = lane == LANES - 1

    def layer(z, carry):
        k = k_s[z + 1]
        side = 0.5 * rate
        tall = 0.5 * rate * z_weight
        c = [
            tall * (k + k_s[z]),
            tall * (k + k_s[z + 2]),
            side * (k + pltpu.roll(k, 1, 0)),
            side * (k + pltpu.roll(k, WIN - 1, 0)),
            side * (k + jnp.where(first, 0.0, pltpu.roll(k, 1, 1))),
            side * (k + jnp.where(last, 0.0, pltpu.roll(k, LANES - 1, 1))),
        ]
        total = ((c[0] + c[1]) + (c[2] + c[3])) + (c[4] + c[5])
        d = jnp.where(k > 0.0, damping / (1.0 + total), 0.0)
        co_s[0, z] = c[0] * d
        co_s[1, z] = c[1] * d
        co_s[2, z] = c[2] * d
        co_s[3, z] = c[3] * d
        co_s[4, z] = jnp.where(first, 0.0, c[4] * d)
        co_s[5, z] = jnp.where(last, 0.0, c[5] * d)
        co_s[6, z] = d
        return carry

    lax.fori_loop(0, NZ, layer, 0)


def one_sweep(src, dst, co_s, db_s, rows):
    tall = rows.stop - rows.start
    for z in range(NZ):
        w = src[z + 1, rows]
        acc = (db_s[z, rows] + (1.0 - damping) * w) + (
            co_s[0, z, rows] * src[z, rows] + co_s[1, z, rows] * src[z + 2, rows]
        )
        acc = acc + (
            co_s[2, z, rows] * pltpu.roll(w, 1, 0) + co_s[3, z, rows] * pltpu.roll(w, tall - 1, 0)
        )
        acc = acc + (
            co_s[4, z, rows] * pltpu.roll(w, 1, 1) + co_s[5, z, rows] * pltpu.roll(w, LANES - 1, 1)
        )
        dst[z + 1, rows] = acc


def rows_at(step):
    return slice(0, WIN) if step < 4 else slice(ROWS, WIN - ROWS)


def fine_body(
    core_ref, strip_ref, strip2_ref, halo_ref, halo2_ref, own_ref, below2_ref, below1_ref, above1_ref,
    above2_ref, out_ref, res_ref, k_s, co_s, a_s, b_s, db_s, f_s, v_s,
):
    load_diffusivity(core_ref, strip_ref, strip2_ref, k_s)
    load_sources(core_ref, (strip_ref, halo_ref), (strip2_ref, halo2_ref), f_s)
    load_window(a_s, b_s, own_ref, below2_ref, below1_ref, above1_ref, above2_ref)
    coefficients(step_size, k_s, co_s)
    for n in range(8):
        rows = rows_at(n)
        for z in range(NZ):
            db_s[z, rows] = co_s[6, z, rows] * (a_s[z + 1, rows] + step_size * f_s[n, z, rows])
        one_sweep(a_s, b_s, co_s, db_s, rows)
        one_sweep(b_s, a_s, co_s, db_s, rows)
        for z in range(NZ):
            v_s[n, z] = a_s[z + 1, 16:24]

    def subtract(halves):
        for z in range(NZ):
            res_ref[z] = v_s[7, z] - halves[z % 2][7, z // 2, 1]

    in_order(core_ref, subtract, strip_ref, strip2_ref)
    core = core_ref[0]
    for y in range(4):
        for zhi in range(2):
            for n in range(7):
                out_ref[zhi, n, y] = v_s[n, 2 * (2 * y + zhi) + core]


def powers_body(
    core_ref, place_ref, strip_ref, strip2_ref, own_ref, below2_ref, below1_ref, above1_ref, above2_ref,
    out_ref, k_s, co_s, a_s, b_s, db_s, pow_s,
):
    load_diffusivity(core_ref, strip_ref, strip2_ref, k_s)
    load_window(a_s, b_s, own_ref, below2_ref, below1_ref, above1_ref, above2_ref)
    coefficients(coarse_size, k_s, co_s)
    for z in range(NZ):
        pow_s[0, z] = own_ref[z]
    for n in range(NB - 1):
        rows = rows_at(n)
        for z in range(NZ):
            db_s[z, rows] = co_s[6, z, rows] * a_s[z + 1, rows]
        one_sweep(a_s, b_s, co_s, db_s, rows)
        one_sweep(b_s, a_s, co_s, db_s, rows)
        for z in range(NZ):
            pow_s[1 + n, z] = a_s[z + 1, 16:24]
    core, c = core_ref[0], place_ref[0]
    for b in range(NB):
        power = jnp.clip(b - c, 0, NB - 1)
        live = b >= c
        for y in range(4):
            for zhi in range(2):
                value = pow_s[power, 2 * (2 * y + zhi) + core]
                out_ref[2 * b + zhi, y] = jnp.where(live, value, 0.0)


SWEEP_SCRATCH = (
    pltpu.VMEM((NZ + 2, WIN, LANES), F32),
    pltpu.VMEM((7, NZ, WIN, LANES), F32),
    pltpu.VMEM((NZ + 2, WIN, LANES), F32),
    pltpu.VMEM((NZ + 2, WIN, LANES), F32),
    pltpu.VMEM((NZ, WIN, LANES), F32),
)


def collect_body(got_ref, v_ref, out_ref):
    for side in range(2):
        for y in range(4):
            total = got_ref[side, y]
            for b in range(1, NB):
                total = total + got_ref[2 * b + side, y]
            out_ref[7 * 4 + y, side] = total
            for n in range(7):
                out_ref[n * 4 + y, side] = v_ref[side, n, y]


def home_body(j_ref, got_ref, guess_ref, out_ref):
    last = j_ref[0] == 7

    def write(add):
        for tile in range(TILES):
            zhi = 0 if tile < TILES // 2 else 1
            m = tile - SIDE * zhi
            zl, y = m // 4, m % 4
            if zl % 2 == 1:
                y = 3 - y
            rows = slice(tile * ROWS, (tile + 1) * ROWS)
            for core in range(2):
                value = got_ref[(zl * 2 + core) * 4 + y, zhi]
                if add:
                    value = guess_ref[core, rows] + value
                out_ref[core, rows] = value

    pl.when(last)(functools.partial(write, True))
    pl.when(jnp.logical_not(last))(functools.partial(write, False))


def on_device(guess, source, diffusivity, initial):
    guess = guess[0]
    source = source[0]
    core = lax.axis_index("core")
    place = lax.axis_index(("zl", "core"))[None]
    block = lax.axis_index(BLOCKS)

    sent = pl.pallas_call(
        scatter_body,
        out_shape=sds(64, 2, ROWS, LANES),
        in_specs=[pl.BlockSpec(memory_space=pltpu.SMEM)] + [pl.BlockSpec(memory_space=pltpu.HBM)] * 4,
        out_specs=pl.BlockSpec(memory_space=pltpu.VMEM),
        scratch_shapes=[
            pltpu.VMEM((2, TILES * ROWS, LANES), F32),
            pltpu.VMEM((2, TILES * ROWS, LANES), F32),
            pltpu.SemaphoreType.DMA((2,)),
        ],
        compiler_params=pltpu.CompilerParams(vmem_limit_bytes=60 * 1024 * 1024),
    )(place, source, guess, diffusivity, initial)
    strips = lax.all_to_all(sent, BLOCK, 0, 0, tiled=True).reshape(8, 8, 2, ROWS, LANES)

    def swap(mine):
        return lax.ppermute(mine, "core", [(0, 1), (1, 0)])

    def along(mine, step):
        return lax.ppermute(mine, ("zl", "y"), neighbours(step))

    def exchange(mine):
        return [along(mine, step) for step in (2, 1, -1, -2)]

    half = [sds(8, ROWS, LANES)]
    messages = [sds(6, 8, ROWS, LANES), sds(2, 8, ROWS, LANES)] * 2
    start, up1, up2, down1, down2 = call(pack_body, half + messages, strips)
    shifted = lax.ppermute(start, BLOCKS, [(b, b + 1) for b in range(NB - 1)])
    halos = jnp.concatenate([along(up1, 1), along(up2, 2), along(down1, -1), along(down2, -2)])
    strips2 = swap(strips)
    halos2 = swap(halos)
    (v0,) = call(
        merge_body, [sds(NZ, ROWS, LANES)],
        core[None], block[None], shifted, swap(shifted), strips, strips2, smem=2,
    )
    flops = 16 * NZ * WIN * LANES * 15
    v, residual = call(
        fine_body, [sds(2, 7, 4, ROWS, LANES), sds(NZ, ROWS, LANES)],
        core[None], strips, strips2, halos, halos2, v0, *exchange(v0), smem=1,
        scratch=SWEEP_SCRATCH + (pltpu.VMEM((8, NZ, WIN, LANES), F32), pltpu.VMEM((8, NZ, ROWS, LANES), F32)),
        flops=flops,
    )
    v = lax.all_to_all(v, "zhi", 0, 0, tiled=True)
    (powers,) = call(
        powers_body, [sds(2 * NB, 4, ROWS, LANES)],
        core[None], block[None], strips, strips2, residual, *exchange(residual), smem=2,
        scratch=SWEEP_SCRATCH + (pltpu.VMEM((NB, NZ, ROWS, LANES), F32),), flops=flops,
    )
    arrived = lax.all_to_all(powers, BLOCKS + ("zhi",), 0, 0, tiled=True)
    (back,) = call(collect_body, [sds(32, 2, ROWS, LANES)], arrived, v)
    returned = lax.all_to_all(back, ("zl", "core", "y"), 0, 0, tiled=True)
    (result,) = call(home_body, [sds(2, TILES * ROWS, LANES)], place, returned, guess, smem=1)
    return result[None]


def solution(mesh):
    fine = Mesh(mesh.devices.reshape(SIZES), AXES)
    tm = ("x", "zh", "zl", "core")
    space = ("y", "zhi")
    in_specs = (P(tm, space, None, None), P(tm, space, None, None), P(space, None, None), P(space, None, None))
    out_specs = P(tm, space, None, None)
    return jax.shard_map(on_device, mesh=fine, in_specs=in_specs, out_specs=out_specs, check_vma=False)
```

```python
import functools

import jax
import jax.numpy as jnp
from jax import lax
from jax.experimental import pallas as pl
from jax.experimental.pallas import tpu as pltpu
from jax.sharding import Mesh, PartitionSpec as P

SWEEPS = 2
F32 = jnp.float32

damping = 0.8
step_size = 0.5
coarse_size = 4.0
z_weight = 8.0

AXES = ("x", "zh", "zl", "core", "y", "zhi")
SIZES = (4, 2, 4, 2, 4, 2)
BLOCK = ("zl", "core", "y", "zhi")
BLOCKS = ("x", "zh")
NB = 8
NZ = 16
ROWS = 8
TILES = 24
CHIPS = 16
SIDE = 8
FINE = 3 * ROWS
WIDE = 5 * ROWS
LANES = 128


def chip_order(zl, y):
    return zl * 4 + (y if zl % 2 == 0 else 3 - y)


def block_index(zl, core, y, zhi):
    return ((zl * 2 + core) * 4 + y) * 2 + zhi


def neighbours(step):
    place = {chip_order(zl, y): zl * 4 + y for zl in range(4) for y in range(4)}
    return [(place[m], place[m + step]) for m in range(CHIPS) if 0 <= m + step < CHIPS]


def call(body, outs, *args, scratch=(), smem=0, flops=0):
    specs = [pl.BlockSpec(memory_space=pltpu.SMEM)] * smem
    specs += [pl.BlockSpec(memory_space=pltpu.VMEM)] * (len(args) - smem)
    out_specs = [pl.BlockSpec(memory_space=pltpu.VMEM)] * len(outs)
    size = sum(4 * a.size for a in args) + sum(4 * o.size for o in outs)
    return pl.pallas_call(
        body,
        out_shape=list(outs),
        in_specs=specs,
        out_specs=out_specs,
        scratch_shapes=list(scratch),
        compiler_params=pltpu.CompilerParams(vmem_limit_bytes=32 * 1024 * 1024),
        cost_estimate=pl.CostEstimate(flops=flops, bytes_accessed=size, transcendentals=0),
    )(*args)


def sds(*shape):
    return jax.ShapeDtypeStruct(shape, F32)


def scatter_body(j_ref, src_hbm, guess_hbm, cond_hbm, init_hbm, out_ref, src_ref, extra_ref, sems):
    place = j_ref[0]
    zero = jnp.zeros((ROWS, LANES), F32)
    source_copy = pltpu.make_async_copy(src_hbm, src_ref, sems.at[0])
    source_copy.start()

    @pl.when(place < 3)
    def _():
        pltpu.make_async_copy(cond_hbm, extra_ref, sems.at[1]).start()

    @pl.when((place > 2) & (place < 6))
    def _():
        pltpu.make_async_copy(init_hbm, extra_ref, sems.at[1]).start()

    @pl.when(place > 5)
    def _():
        pltpu.make_async_copy(guess_hbm, extra_ref, sems.at[1]).start()

    def each():
        for zl in range(4):
            for y in range(4):
                for zhi in range(2):
                    tile = SIDE * zhi + chip_order(zl, y)
                    for core in range(2):
                        yield block_index(zl, core, y, zhi), core, tile

    source_copy.wait()
    for at, core, tile in each():
        out_ref[at, 0] = src_ref[core, tile * ROWS : (tile + 1) * ROWS]
    pltpu.make_async_copy(guess_hbm, extra_ref, sems.at[1]).wait()

    def fill(shift):
        for at, core, tile in each():
            tile = tile + shift
            if 0 <= tile < TILES:
                out_ref[at, 1] = extra_ref[core, tile * ROWS : (tile + 1) * ROWS]
            else:
                out_ref[at, 1] = zero

    pl.when((place == 1) | (place == 4))(functools.partial(fill, 1))
    pl.when((place == 2) | (place == 5))(functools.partial(fill, -1))
    pl.when((place == 0) | (place == 3) | (place > 5))(functools.partial(fill, 0))


def pack_body(core_ref, own_ref, other_ref, f_ref, g_ref, k_ref, first_ref, up_ref, down_ref):
    def order(halves):
        for z in range(NZ):
            half, s = halves[z % 2], z // 2
            for n in range(8):
                f_ref[n, z] = half[n, s, 0]
            g_ref[z] = half[7, s, 1]
            for n, place in enumerate((2, 0, 1)):
                k_ref[z, 8 * n : 8 * n + 8] = half[place, s, 1]
                first_ref[z, 8 * n : 8 * n + 8] = half[3 + place, s, 1]
            up_ref[4, z] = half[2, s, 1]
            down_ref[4, z] = half[1, s, 1]

    pl.when(core_ref[0] == 0)(functools.partial(order, (own_ref, other_ref)))
    pl.when(core_ref[0] == 1)(functools.partial(order, (other_ref, own_ref)))
    row = lax.broadcasted_iota(jnp.int32, (ROWS, LANES), 0)
    for z in range(NZ):
        for phase in range(2):
            f = [f_ref[4 * phase + n, z] for n in range(4)]
            down_ref[2 * phase, z] = jnp.where(row < 7, f[0], pltpu.roll(f[3], 7, 0))
            down_ref[2 * phase + 1, z] = jnp.where(row < 5, f[1], pltpu.roll(f[2], 5, 0))
            up_ref[2 * phase, z] = jnp.where(row >= 1, f[0], pltpu.roll(f[3], 1, 0))
            up_ref[2 * phase + 1, z] = jnp.where(row >= 3, f[1], pltpu.roll(f[2], 3, 0))


def load_window(a_s, b_s, tiles):
    zero = jnp.zeros((a_s.shape[1], LANES), F32)
    for ref in (a_s, b_s):
        ref[0] = zero
        ref[NZ + 1] = zero
    for z in range(NZ):
        for n, tile in enumerate(tiles):
            a_s[z + 1, 8 * n : 8 * n + 8] = tile[z]


def load_diffusivity(k_s, parts):
    zero = jnp.zeros((k_s.shape[1], LANES), F32)
    k_s[0] = zero
    k_s[NZ + 1] = zero
    for z in range(NZ):
        at = 0
        for part in parts:
            tile = part(z)
            k_s[z + 1, at : at + tile.shape[0]] = tile
            at += tile.shape[0]


def coefficients(rate, k_s, co_s):
    tall_win = k_s.shape[1]
    lane = lax.broadcasted_iota(jnp.int32, (tall_win, LANES), 1)
    first = lane == 0
    last = lane == LANES - 1

    def layer(z, carry):
        k = k_s[z + 1]
        side = 0.5 * rate
        tall = 0.5 * rate * z_weight
        c = [
            tall * (k + k_s[z]),
            tall * (k + k_s[z + 2]),
            side * (k + pltpu.roll(k, 1, 0)),
            side * (k + pltpu.roll(k, tall_win - 1, 0)),
            side * (k + jnp.where(first, 0.0, pltpu.roll(k, 1, 1))),
            side * (k + jnp.where(last, 0.0, pltpu.roll(k, LANES - 1, 1))),
        ]
        total = ((c[0] + c[1]) + (c[2] + c[3])) + (c[4] + c[5])
        d = jnp.where(k > 0.0, damping / (1.0 + total), 0.0)
        co_s[0, z] = c[0] * d
        co_s[1, z] = c[1] * d
        co_s[2, z] = c[2] * d
        co_s[3, z] = c[3] * d
        co_s[4, z] = jnp.where(first, 0.0, c[4] * d)
        co_s[5, z] = jnp.where(last, 0.0, c[5] * d)
        co_s[6, z] = d
        return carry

    lax.fori_loop(0, NZ, layer, 0)


def one_sweep(src, dst, co_s, db_s, rows):
    tall = rows.stop - rows.start
    for z in range(NZ):
        w = src[z + 1, rows]
        acc = (db_s[z, rows] + (1.0 - damping) * w) + (
            co_s[0, z, rows] * src[z, rows] + co_s[1, z, rows] * src[z + 2, rows]
        )
        acc = acc + (
            co_s[2, z, rows] * pltpu.roll(w, 1, 0) + co_s[3, z, rows] * pltpu.roll(w, tall - 1, 0)
        )
        acc = acc + (
            co_s[4, z, rows] * pltpu.roll(w, 1, 1) + co_s[5, z, rows] * pltpu.roll(w, LANES - 1, 1)
        )
        dst[z + 1, rows] = acc


def fine_steps(phase, f_ref, fb_ref, fa_ref, co_s, a_s, b_s, db_s, keep):
    rows = slice(0, FINE)
    for n in range(4):
        tile, turn = ((0, 0), (1, 0), (1, 5), (0, 7))[n]
        for z in range(NZ):
            below = fb_ref[2 * phase + tile, z]
            above = fa_ref[2 * phase + tile, z]
            if turn:
                below = pltpu.roll(below, turn, 0)
                above = pltpu.roll(above, ROWS - turn, 0)
            forcing = jnp.concatenate([below, f_ref[4 * phase + n, z], above], axis=0)
            db_s[z] = co_s[6, z] * (a_s[z + 1] + step_size * forcing)
        one_sweep(a_s, b_s, co_s, db_s, rows)
        one_sweep(b_s, a_s, co_s, db_s, rows)
        for z in range(NZ):
            keep(n, z, a_s[z + 1, 8:16])


def early_body(
    block_ref, k_ref, f_ref, fb_ref, fa_ref, first_ref, below_ref, own_ref, above_ref,
    out_ref, end_ref, k_s, co_s, a_s, b_s, db_s,
):
    load_diffusivity(k_s, [lambda z: k_ref[z]])
    coefficients(step_size, k_s, co_s)
    load_window(a_s, b_s, (below_ref, own_ref, above_ref))

    @pl.when(block_ref[0] == 0)
    def _():
        for z in range(NZ):
            a_s[z + 1] = first_ref[z]

    def keep(n, z, mine):
        out_ref[n, z] = mine
        if n == 3:
            end_ref[z] = mine

    fine_steps(0, f_ref, fb_ref, fa_ref, co_s, a_s, b_s, db_s, keep)


def late_body(
    k_ref, f_ref, fb_ref, fa_ref, below_ref, own_ref, above_ref, g_ref,
    out_ref, res_ref, k_s, co_s, a_s, b_s, db_s,
):
    load_diffusivity(k_s, [lambda z: k_ref[z]])
    coefficients(step_size, k_s, co_s)
    load_window(a_s, b_s, (below_ref, own_ref, above_ref))

    def keep(n, z, mine):
        if n < 3:
            out_ref[n, z] = mine
        else:
            res_ref[z] = mine - g_ref[z]

    fine_steps(1, f_ref, fb_ref, fa_ref, co_s, a_s, b_s, db_s, keep)


def powers_body(
    core_ref, block_ref, k_ref, fb_ref, fa_ref, below2_ref, below1_ref, own_ref, above1_ref, above2_ref,
    out_ref, k_s, co_s, a_s, b_s, db_s, pow_s,
):
    load_diffusivity(k_s, [lambda z: fb_ref[4, z], lambda z: k_ref[z], lambda z: fa_ref[4, z]])
    coefficients(coarse_size, k_s, co_s)
    load_window(a_s, b_s, (below2_ref, below1_ref, own_ref, above1_ref, above2_ref))
    for z in range(NZ):
        pow_s[0, z] = own_ref[z]
    for n in range(NB - 1):
        rows = slice(0, WIDE) if n < 4 else slice(ROWS, WIDE - ROWS)
        for z in range(NZ):
            db_s[z, rows] = co_s[6, z, rows] * a_s[z + 1, rows]
        one_sweep(a_s, b_s, co_s, db_s, rows)
        one_sweep(b_s, a_s, co_s, db_s, rows)
        for z in range(NZ):
            pow_s[1 + n, z] = a_s[z + 1, 16:24]
    core, c = core_ref[0], block_ref[0]
    for b in range(NB):
        power = jnp.clip(b - c, 0, NB - 1)
        live = b >= c
        for s in range(8):
            out_ref[b, s] = jnp.where(live, pow_s[power, 2 * s + core], 0.0)


def sweep_scratch(window):
    return (
        pltpu.VMEM((NZ + 2, window, LANES), F32),
        pltpu.VMEM((7, NZ, window, LANES), F32),
        pltpu.VMEM((NZ + 2, window, LANES), F32),
        pltpu.VMEM((NZ + 2, window, LANES), F32),
        pltpu.VMEM((NZ, window, LANES), F32),
    )


def collect_body(core_ref, got_ref, early_ref, late_ref, out_ref):
    core = core_ref[0]
    for s in range(8):
        total = got_ref[0, s]
        for b in range(1, NB):
            total = total + got_ref[b, s]
        out_ref[7 * 8 + s] = total
        for n in range(4):
            out_ref[n * 8 + s] = early_ref[n, 2 * s + core]
        for n in range(3):
            out_ref[(4 + n) * 8 + s] = late_ref[n, 2 * s + core]


def home_body(j_ref, got_ref, guess_ref, out_ref):
    last = j_ref[0] == 7

    def write(add):
        for tile in range(TILES):
            zhi = 0 if tile < TILES // 2 else 1
            m = tile - SIDE * zhi
            zl, y = m // 4, m % 4
            if zl % 2 == 1:
                y = 3 - y
            rows = slice(tile * ROWS, (tile + 1) * ROWS)
            for core in range(2):
                value = got_ref[block_index(zl, core, y, zhi)]
                if add:
                    value = guess_ref[core, rows] + value
                out_ref[core, rows] = value

    pl.when(last)(functools.partial(write, True))
    pl.when(jnp.logical_not(last))(functools.partial(write, False))


def on_device(guess, source, diffusivity, initial):
    guess = guess[0]
    source = source[0]
    core = lax.axis_index("core")
    place = lax.axis_index(("zl", "core"))[None]
    block = lax.axis_index(BLOCKS)

    sent = pl.pallas_call(
        scatter_body,
        out_shape=sds(64, 2, ROWS, LANES),
        in_specs=[pl.BlockSpec(memory_space=pltpu.SMEM)] + [pl.BlockSpec(memory_space=pltpu.HBM)] * 4,
        out_specs=pl.BlockSpec(memory_space=pltpu.VMEM),
        scratch_shapes=[
            pltpu.VMEM((2, TILES * ROWS, LANES), F32),
            pltpu.VMEM((2, TILES * ROWS, LANES), F32),
            pltpu.SemaphoreType.DMA((2,)),
        ],
        compiler_params=pltpu.CompilerParams(vmem_limit_bytes=60 * 1024 * 1024),
    )(place, source, guess, diffusivity, initial)
    strips = lax.all_to_all(sent, BLOCK, 0, 0, tiled=True).reshape(8, 8, 2, ROWS, LANES)

    strips2 = lax.ppermute(strips, "core", [(0, 1), (1, 0)])
    full = sds(NZ, ROWS, LANES)
    f, g, k, first, f_up, f_down = call(
        pack_body,
        [sds(8, NZ, ROWS, LANES), full] + [sds(NZ, FINE, LANES)] * 2 + [sds(5, NZ, ROWS, LANES)] * 2,
        core[None], strips, strips2, smem=1,
    )

    def along(mine, step):
        return lax.ppermute(mine, ("zl", "y"), neighbours(step))

    def onward(mine, step):
        route = [(16 * b + i, 16 * (b + 1) + j) for b in range(NB - 1) for i, j in neighbours(step)]
        return lax.ppermute(mine, BLOCKS + ("zl", "y"), route)

    v0 = [onward(g, step) for step in (1, 0, -1)]
    f_below, f_above = along(f_up, 1), along(f_down, -1)
    flops = 8 * NZ * FINE * LANES * 15
    v_early, v4 = call(
        early_body, [sds(4, NZ, ROWS, LANES), full],
        block[None], k, f, f_below, f_above, first, *v0, smem=1, scratch=sweep_scratch(FINE), flops=flops,
    )
    v_late, residual = call(
        late_body, [sds(3, NZ, ROWS, LANES), full],
        k, f, f_below, f_above, along(v4, 1), v4, along(v4, -1), g, scratch=sweep_scratch(FINE), flops=flops,
    )
    (powers,) = call(
        powers_body, [sds(NB, 8, ROWS, LANES)],
        core[None], block[None], k, f_below, f_above,
        along(residual, 2), along(residual, 1), residual, along(residual, -1), along(residual, -2), smem=2,
        scratch=sweep_scratch(WIDE) + (pltpu.VMEM((NB, NZ, ROWS, LANES), F32),), flops=3 * flops,
    )
    arrived = lax.all_to_all(powers, BLOCKS, 0, 0, tiled=True)
    (back,) = call(collect_body, [sds(64, ROWS, LANES)], core[None], arrived, v_early, v_late, smem=1)
    returned = lax.all_to_all(back, BLOCK, 0, 0, tiled=True)
    (result,) = call(home_body, [sds(2, TILES * ROWS, LANES)], place, returned, guess, smem=1)
    return result[None]


def solution(mesh):
    fine = Mesh(mesh.devices.reshape(SIZES), AXES)
    tm = ("x", "zh", "zl", "core")
    space = ("y", "zhi")
    in_specs = (P(tm, space, None, None), P(tm, space, None, None), P(space, None, None), P(space, None, None))
    out_specs = P(tm, space, None, None)
    return jax.shard_map(on_device, mesh=fine, in_specs=in_specs, out_specs=out_specs, check_vma=False)
```

```python
import functools

import jax
import jax.numpy as jnp
from jax import lax
from jax.experimental import pallas as pl
from jax.experimental.pallas import tpu as pltpu
from jax.sharding import Mesh, PartitionSpec as P

SWEEPS = 2
F32 = jnp.float32

damping = 0.8
step_size = 0.5
coarse_size = 4.0
z_weight = 8.0

AXES = ("x", "zh", "zl", "core", "y", "zhi")
SIZES = (4, 2, 4, 2, 4, 2)
BLOCK = ("zl", "core", "y", "zhi")
BLOCKS = ("x", "zh")
NB = 8
NZ = 16
ROWS = 8
TILES = 24
CHIPS = 16
SIDE = 8
FINE = 3 * ROWS
WIDE = 5 * ROWS
LANES = 128


def chip_order(zl, y):
    return zl * 4 + (y if zl % 2 == 0 else 3 - y)


def block_index(zl, core, y, zhi):
    return ((zl * 2 + core) * 4 + y) * 2 + zhi


def neighbours(step):
    place = {chip_order(zl, y): zl * 4 + y for zl in range(4) for y in range(4)}
    return [(place[m], place[m + step]) for m in range(CHIPS) if 0 <= m + step < CHIPS]


def call(body, outs, *args, scratch=(), smem=0, flops=0):
    specs = [pl.BlockSpec(memory_space=pltpu.SMEM)] * smem
    specs += [pl.BlockSpec(memory_space=pltpu.VMEM)] * (len(args) - smem)
    out_specs = [pl.BlockSpec(memory_space=pltpu.VMEM)] * len(outs)
    size = sum(4 * a.size for a in args) + sum(4 * o.size for o in outs)
    return pl.pallas_call(
        body,
        out_shape=list(outs),
        in_specs=specs,
        out_specs=out_specs,
        scratch_shapes=list(scratch),
        compiler_params=pltpu.CompilerParams(vmem_limit_bytes=32 * 1024 * 1024),
        cost_estimate=pl.CostEstimate(flops=flops, bytes_accessed=size, transcendentals=0),
    )(*args)


def sds(*shape):
    return jax.ShapeDtypeStruct(shape, F32)


def scatter_body(j_ref, src_hbm, guess_hbm, cond_hbm, init_hbm, out_ref, src_ref, extra_ref, sems):
    place = j_ref[0]
    zero = jnp.zeros((ROWS, LANES), F32)
    source_copy = pltpu.make_async_copy(src_hbm, src_ref, sems.at[0])
    source_copy.start()

    @pl.when(place < 3)
    def _():
        pltpu.make_async_copy(cond_hbm, extra_ref, sems.at[1]).start()

    @pl.when((place > 2) & (place < 6))
    def _():
        pltpu.make_async_copy(init_hbm, extra_ref, sems.at[1]).start()

    @pl.when(place > 5)
    def _():
        pltpu.make_async_copy(guess_hbm, extra_ref, sems.at[1]).start()

    def each():
        for zl in range(4):
            for y in range(4):
                for zhi in range(2):
                    tile = SIDE * zhi + chip_order(zl, y)
                    for core in range(2):
                        yield block_index(zl, core, y, zhi), core, tile

    source_copy.wait()
    for at, core, tile in each():
        out_ref[at, 0] = src_ref[core, tile * ROWS : (tile + 1) * ROWS]
    pltpu.make_async_copy(guess_hbm, extra_ref, sems.at[1]).wait()

    def fill(shift):
        for at, core, tile in each():
            tile = tile + shift
            if 0 <= tile < TILES:
                out_ref[at, 1] = extra_ref[core, tile * ROWS : (tile + 1) * ROWS]
            else:
                out_ref[at, 1] = zero

    pl.when((place == 1) | (place == 4))(functools.partial(fill, 1))
    pl.when((place == 2) | (place == 5))(functools.partial(fill, -1))
    pl.when((place == 0) | (place == 3) | (place > 5))(functools.partial(fill, 0))


def pack_body(core_ref, own_ref, other_ref, f_ref, g_ref, k_ref, first_ref, up_ref, down_ref):
    def order(halves):
        for z in range(NZ):
            half, s = halves[z % 2], z // 2
            for n in range(8):
                f_ref[n, z] = half[n, s, 0]
            g_ref[z] = half[7, s, 1]
            for n, place in enumerate((2, 0, 1)):
                k_ref[z, 8 * n : 8 * n + 8] = half[place, s, 1]
                first_ref[z, 8 * n : 8 * n + 8] = half[3 + place, s, 1]
            up_ref[4, z] = half[2, s, 1]
            down_ref[4, z] = half[1, s, 1]

    pl.when(core_ref[0] == 0)(functools.partial(order, (own_ref, other_ref)))
    pl.when(core_ref[0] == 1)(functools.partial(order, (other_ref, own_ref)))
    row = lax.broadcasted_iota(jnp.int32, (ROWS, LANES), 0)
    for z in range(NZ):
        for phase in range(2):
            f = [f_ref[4 * phase + n, z] for n in range(4)]
            down_ref[2 * phase, z] = jnp.where(row < 7, f[0], pltpu.roll(f[3], 7, 0))
            down_ref[2 * phase + 1, z] = jnp.where(row < 5, f[1], pltpu.roll(f[2], 5, 0))
            up_ref[2 * phase, z] = jnp.where(row >= 1, f[0], pltpu.roll(f[3], 1, 0))
            up_ref[2 * phase + 1, z] = jnp.where(row >= 3, f[1], pltpu.roll(f[2], 3, 0))


def load_window(a_s, b_s, tiles):
    zero = jnp.zeros((a_s.shape[1], LANES), F32)
    for ref in (a_s, b_s):
        ref[0] = zero
        ref[NZ + 1] = zero
    for z in range(NZ):
        for n, tile in enumerate(tiles):
            a_s[z + 1, 8 * n : 8 * n + 8] = tile[z]


def load_diffusivity(k_s, parts):
    zero = jnp.zeros((k_s.shape[1], LANES), F32)
    k_s[0] = zero
    k_s[NZ + 1] = zero
    for z in range(NZ):
        at = 0
        for part in parts:
            tile = part(z)
            k_s[z + 1, at : at + tile.shape[0]] = tile
            at += tile.shape[0]


def coefficients(rate, k_s, co_s):
    tall_win = k_s.shape[1]
    lane = lax.broadcasted_iota(jnp.int32, (tall_win, LANES), 1)
    first = lane == 0
    last = lane == LANES - 1

    def layer(z, carry):
        k = k_s[z + 1]
        side = 0.5 * rate
        tall = 0.5 * rate * z_weight
        c = [
            tall * (k + k_s[z]),
            tall * (k + k_s[z + 2]),
            side * (k + pltpu.roll(k, 1, 0)),
            side * (k + pltpu.roll(k, tall_win - 1, 0)),
            side * (k + jnp.where(first, 0.0, pltpu.roll(k, 1, 1))),
            side * (k + jnp.where(last, 0.0, pltpu.roll(k, LANES - 1, 1))),
        ]
        total = ((c[0] + c[1]) + (c[2] + c[3])) + (c[4] + c[5])
        d = jnp.where(k > 0.0, damping / (1.0 + total), 0.0)
        co_s[0, z] = c[0] * d
        co_s[1, z] = c[1] * d
        co_s[2, z] = c[2] * d
        co_s[3, z] = c[3] * d
        co_s[4, z] = jnp.where(first, 0.0, c[4] * d)
        co_s[5, z] = jnp.where(last, 0.0, c[5] * d)
        co_s[6, z] = d
        return carry

    lax.fori_loop(0, NZ, layer, 0)


def one_sweep(src, dst, co_s, db_s, rows):
    tall = rows.stop - rows.start
    for z in range(NZ):
        w = src[z + 1, rows]
        acc = (db_s[z, rows] + (1.0 - damping) * w) + (
            co_s[0, z, rows] * src[z, rows] + co_s[1, z, rows] * src[z + 2, rows]
        )
        acc = acc + (
            co_s[2, z, rows] * pltpu.roll(w, 1, 0) + co_s[3, z, rows] * pltpu.roll(w, tall - 1, 0)
        )
        acc = acc + (
            co_s[4, z, rows] * pltpu.roll(w, 1, 1) + co_s[5, z, rows] * pltpu.roll(w, LANES - 1, 1)
        )
        dst[z + 1, rows] = acc


def fine_steps(phase, f_ref, fb_ref, fa_ref, co_s, a_s, b_s, db_s, keep):
    rows = slice(0, FINE)
    for n in range(4):
        tile, turn = ((0, 0), (1, 0), (1, 5), (0, 7))[n]
        for z in range(NZ):
            below = fb_ref[2 * phase + tile, z]
            above = fa_ref[2 * phase + tile, z]
            if turn:
                below = pltpu.roll(below, turn, 0)
                above = pltpu.roll(above, ROWS - turn, 0)
            forcing = jnp.concatenate([below, f_ref[4 * phase + n, z], above], axis=0)
            db_s[z] = co_s[6, z] * (a_s[z + 1] + step_size * forcing)
        one_sweep(a_s, b_s, co_s, db_s, rows)
        one_sweep(b_s, a_s, co_s, db_s, rows)
        for z in range(NZ):
            keep(n, z, a_s[z + 1, 8:16])


def early_body(
    block_ref, k_ref, f_ref, fb_ref, fa_ref, first_ref, below_ref, own_ref, above_ref,
    out_ref, end_ref, k_s, co_s, a_s, b_s, db_s,
):
    load_diffusivity(k_s, [lambda z: k_ref[z]])
    coefficients(step_size, k_s, co_s)
    load_window(a_s, b_s, (below_ref, own_ref, above_ref))

    @pl.when(block_ref[0] == 0)
    def _():
        for z in range(NZ):
            a_s[z + 1] = first_ref[z]

    def keep(n, z, mine):
        out_ref[n, z] = mine
        if n == 3:
            end_ref[z] = mine

    fine_steps(0, f_ref, fb_ref, fa_ref, co_s, a_s, b_s, db_s, keep)


def late_body(
    k_ref, f_ref, fb_ref, fa_ref, below_ref, own_ref, above_ref, g_ref,
    out_ref, res_ref, k_s, co_s, a_s, b_s, db_s,
):
    load_diffusivity(k_s, [lambda z: k_ref[z]])
    coefficients(step_size, k_s, co_s)
    load_window(a_s, b_s, (below_ref, own_ref, above_ref))

    def keep(n, z, mine):
        if n < 3:
            out_ref[n, z] = mine
        else:
            res_ref[z] = mine - g_ref[z]

    fine_steps(1, f_ref, fb_ref, fa_ref, co_s, a_s, b_s, db_s, keep)


def powers_body(
    core_ref, block_ref, k_ref, fb_ref, fa_ref, below2_ref, below1_ref, own_ref, above1_ref, above2_ref,
    out_ref, k_s, co_s, a_s, b_s, db_s, pow_s,
):
    load_diffusivity(k_s, [lambda z: fb_ref[4, z], lambda z: k_ref[z], lambda z: fa_ref[4, z]])
    coefficients(coarse_size, k_s, co_s)
    load_window(a_s, b_s, (below2_ref, below1_ref, own_ref, above1_ref, above2_ref))
    for z in range(NZ):
        pow_s[0, z] = own_ref[z]
    for n in range(NB - 1):
        rows = slice(0, WIDE) if n < 4 else slice(ROWS, WIDE - ROWS)
        for z in range(NZ):
            db_s[z, rows] = co_s[6, z, rows] * a_s[z + 1, rows]
        one_sweep(a_s, b_s, co_s, db_s, rows)
        one_sweep(b_s, a_s, co_s, db_s, rows)
        for z in range(NZ):
            pow_s[1 + n, z] = a_s[z + 1, 16:24]
    core, c = core_ref[0], block_ref[0]
    for b in range(NB):
        power = jnp.clip(b - c, 0, NB - 1)
        live = b >= c
        for s in range(8):
            out_ref[b, s] = jnp.where(live, pow_s[power, 2 * s + core], 0.0)


def sweep_scratch(window):
    return (
        pltpu.VMEM((NZ + 2, window, LANES), F32),
        pltpu.VMEM((7, NZ, window, LANES), F32),
        pltpu.VMEM((NZ + 2, window, LANES), F32),
        pltpu.VMEM((NZ + 2, window, LANES), F32),
        pltpu.VMEM((NZ, window, LANES), F32),
    )


def collect_body(core_ref, got_ref, early_ref, late_ref, out_ref):
    core = core_ref[0]
    for s in range(8):
        total = got_ref[0, s]
        for b in range(1, NB):
            total = total + got_ref[b, s]
        out_ref[7 * 8 + s] = total
        for n in range(4):
            out_ref[n * 8 + s] = early_ref[n, 2 * s + core]
        for n in range(3):
            out_ref[(4 + n) * 8 + s] = late_ref[n, 2 * s + core]


def home_body(j_ref, got_ref, guess_ref, out_ref):
    last = j_ref[0] == 7

    def write(add):
        for tile in range(TILES):
            zhi = 0 if tile < TILES // 2 else 1
            m = tile - SIDE * zhi
            zl, y = m // 4, m % 4
            if zl % 2 == 1:
                y = 3 - y
            rows = slice(tile * ROWS, (tile + 1) * ROWS)
            for core in range(2):
                value = got_ref[block_index(zl, core, y, zhi)]
                if add:
                    value = guess_ref[core, rows] + value
                out_ref[core, rows] = value

    pl.when(last)(functools.partial(write, True))
    pl.when(jnp.logical_not(last))(functools.partial(write, False))


def on_device(guess, source, diffusivity, initial):
    guess = guess[0]
    source = source[0]
    core = lax.axis_index("core")
    place = lax.axis_index(("zl", "core"))[None]
    block = lax.axis_index(BLOCKS)

    sent = pl.pallas_call(
        scatter_body,
        out_shape=sds(64, 2, ROWS, LANES),
        in_specs=[pl.BlockSpec(memory_space=pltpu.SMEM)] + [pl.BlockSpec(memory_space=pltpu.HBM)] * 4,
        out_specs=pl.BlockSpec(memory_space=pltpu.VMEM),
        scratch_shapes=[
            pltpu.VMEM((2, TILES * ROWS, LANES), F32),
            pltpu.VMEM((2, TILES * ROWS, LANES), F32),
            pltpu.SemaphoreType.DMA((2,)),
        ],
        compiler_params=pltpu.CompilerParams(vmem_limit_bytes=60 * 1024 * 1024),
    )(place, source, guess, diffusivity, initial)
    strips = lax.all_to_all(sent, BLOCK, 0, 0, tiled=True).reshape(8, 8, 2, ROWS, LANES)

    strips2 = lax.ppermute(strips, "core", [(0, 1), (1, 0)])
    full = sds(NZ, ROWS, LANES)
    f, g, k, first, f_up, f_down = call(
        pack_body,
        [sds(8, NZ, ROWS, LANES), full] + [sds(NZ, FINE, LANES)] * 2 + [sds(5, NZ, ROWS, LANES)] * 2,
        core[None], strips, strips2, smem=1,
    )

    def along(mine, step):
        return lax.ppermute(mine, ("zl", "y"), neighbours(step))

    v0 = lax.ppermute(g, BLOCKS, [(b, b + 1) for b in range(NB - 1)])
    f_below, f_above = along(f_up, 1), along(f_down, -1)
    flops = 8 * NZ * FINE * LANES * 15
    v_early, v4 = call(
        early_body, [sds(4, NZ, ROWS, LANES), full],
        block[None], k, f, f_below, f_above, first, along(v0, 1), v0, along(v0, -1), smem=1, scratch=sweep_scratch(FINE), flops=flops,
    )
    v_late, residual = call(
        late_body, [sds(3, NZ, ROWS, LANES), full],
        k, f, f_below, f_above, along(v4, 1), v4, along(v4, -1), g, scratch=sweep_scratch(FINE), flops=flops,
    )
    (powers,) = call(
        powers_body, [sds(NB, 8, ROWS, LANES)],
        core[None], block[None], k, f_below, f_above,
        along(residual, 2), along(residual, 1), residual, along(residual, -1), along(residual, -2), smem=2,
        scratch=sweep_scratch(WIDE) + (pltpu.VMEM((NB, NZ, ROWS, LANES), F32),), flops=3 * flops,
    )
    arrived = lax.all_to_all(powers, BLOCKS, 0, 0, tiled=True)
    (back,) = call(collect_body, [sds(64, ROWS, LANES)], core[None], arrived, v_early, v_late, smem=1)
    returned = lax.all_to_all(back, BLOCK, 0, 0, tiled=True)
    (result,) = call(home_body, [sds(2, TILES * ROWS, LANES)], place, returned, guess, smem=1)
    return result[None]


def solution(mesh):
    fine = Mesh(mesh.devices.reshape(SIZES), AXES)
    tm = ("x", "zh", "zl", "core")
    space = ("y", "zhi")
    in_specs = (P(tm, space, None, None), P(tm, space, None, None), P(space, None, None), P(space, None, None))
    out_specs = P(tm, space, None, None)
    return jax.shard_map(on_device, mesh=fine, in_specs=in_specs, out_specs=out_specs, check_vma=False)
```

```python
import functools

import jax
import jax.numpy as jnp
from jax import lax
from jax.experimental import pallas as pl
from jax.experimental.pallas import tpu as pltpu
from jax.sharding import Mesh, PartitionSpec as P

F32 = jnp.float32

damping = 0.8
step_size = 0.5
coarse_size = 4.0
z_weight = 8.0

AXES = ("x", "zh", "zl", "core", "y", "zhi")
SIZES = (4, 2, 4, 2, 4, 2)
BLOCK = ("zl", "core", "y", "zhi")
BLOCKS = ("x", "zh")
NB = 8
NZ = 16
NY = 192
CHIPS = 16
STRIP = NY // CHIPS
PAIR = 2 * STRIP
LANES = 128
LOW, OWN, HIGH, WIN = 4, 16, 28, 40


def chip_order(zl, y):
    return zl * 4 + (y if zl % 2 == 0 else 3 - y)


def neighbours(step):
    place = {chip_order(zl, y): zl * 4 + y for zl in range(4) for y in range(4)}
    return [(place[m], place[m + step]) for m in range(CHIPS) if 0 <= m + step < CHIPS]


def at(z, first, last):
    return slice((z % 2) * STRIP + first, (z % 2) * STRIP + last)


def call(body, outs, *args, scratch=(), smem=0, flops=0):
    specs = [pl.BlockSpec(memory_space=pltpu.SMEM)] * smem
    specs += [pl.BlockSpec(memory_space=pltpu.VMEM)] * (len(args) - smem)
    out_specs = [pl.BlockSpec(memory_space=pltpu.VMEM)] * len(outs)
    size = sum(4 * a.size for a in args) + sum(4 * o.size for o in outs)
    return pl.pallas_call(
        body,
        out_shape=list(outs),
        in_specs=specs,
        out_specs=out_specs,
        scratch_shapes=list(scratch),
        compiler_params=pltpu.CompilerParams(vmem_limit_bytes=32 * 1024 * 1024),
        cost_estimate=pl.CostEstimate(flops=flops, bytes_accessed=size, transcendentals=0),
    )(*args)


def sds(*shape):
    return jax.ShapeDtypeStruct(shape, F32)


def scatter_body(j_ref, block_ref, src_hbm, prev_hbm, cond_hbm, init_hbm, out_ref, src_ref, extra_ref, sems):
    place = j_ref[0]
    zero = jnp.zeros((STRIP, LANES), F32)
    source_copy = pltpu.make_async_copy(src_hbm, src_ref, sems.at[0])
    source_copy.start()

    @pl.when(place < 7)
    def _():
        pltpu.make_async_copy(cond_hbm, extra_ref, sems.at[1]).start()

    @pl.when((place == 7) & (block_ref[0] == 0))
    def _():
        pltpu.make_async_copy(init_hbm, extra_ref, sems.at[1]).start()

    @pl.when((place == 7) & (block_ref[0] > 0))
    def _():
        pltpu.make_async_copy(prev_hbm, extra_ref, sems.at[1]).start()

    def each():
        for zl in range(4):
            for y in range(4):
                for zhi in range(2):
                    for core in range(2):
                        yield ((zl * 2 + core) * 4 + y) * 2 + zhi, core, chip_order(zl, y)

    source_copy.wait()
    for to, core, m in each():
        out_ref[to, 0:STRIP] = src_ref[core, m * STRIP : (m + 1) * STRIP]
    pltpu.make_async_copy(cond_hbm, extra_ref, sems.at[1]).wait()

    def fill(shift):
        for to, core, m in each():
            m = m + shift
            if 0 <= m < CHIPS:
                out_ref[to, STRIP:PAIR] = extra_ref[core, m * STRIP : (m + 1) * STRIP]
            else:
                out_ref[to, STRIP:PAIR] = zero

    pl.when(place == 1)(functools.partial(fill, 1))
    pl.when(place == 2)(functools.partial(fill, -1))
    pl.when((place != 1) & (place != 2))(functools.partial(fill, 0))


def pack_body(core_ref, own_ref, other_ref, f_ref, k_ref, up_ref, down_ref):
    def order(halves):
        for z in range(NZ):
            half, s = halves[z % 2], z // 2
            for n in range(8):
                f_ref[n, z] = half[n, s, 0:STRIP]
            start = half[7, s, STRIP:PAIR]
            up_ref[0, s, at(z, 0, STRIP)] = start
            down_ref[0, s, at(z, 0, STRIP)] = start
            k_ref[z, 0:LOW] = jnp.zeros((LOW, LANES), F32)
            k_ref[z, LOW:OWN] = half[2, s, STRIP:PAIR]
            k_ref[z, OWN:HIGH] = half[0, s, STRIP:PAIR]
            k_ref[z, HIGH:WIN] = half[1, s, STRIP:PAIR]

    pl.when(core_ref[0] == 0)(functools.partial(order, (own_ref, other_ref)))
    pl.when(core_ref[0] == 1)(functools.partial(order, (other_ref, own_ref)))
    for z in range(NZ):
        s = z // 2
        for n in range(3):
            rows = 11 - 2 * n
            early, late = f_ref[n, z], f_ref[5 - n, z]
            down_ref[1 + n, s, at(z, 0, rows)] = early[0:rows]
            down_ref[1 + n, s, at(z, rows, STRIP)] = late[0 : STRIP - rows]
            up_ref[1 + n, s, at(z, STRIP - rows, STRIP)] = early[STRIP - rows : STRIP]
            up_ref[1 + n, s, at(z, 0, STRIP - rows)] = late[rows:STRIP]


def clear_ends(*refs):
    zero = jnp.zeros((WIN, LANES), F32)
    for ref in refs:
        ref[0] = zero
        ref[NZ + 1] = zero


def load_window(a_s, below, own, above):
    zero = jnp.zeros((LOW, LANES), F32)
    for z in range(NZ):
        a_s[z + 1, 0:LOW] = zero
        a_s[z + 1, LOW:OWN] = below(z)
        a_s[z + 1, OWN:HIGH] = own(z)
        a_s[z + 1, HIGH:WIN] = above(z)


def strips_of(ref, field):
    return lambda z: ref[field, z // 2, at(z, 0, STRIP)]


def coefficients(rate, k_ref, k_s, co_s):
    clear_ends(k_s)
    for z in range(NZ):
        k_s[z + 1] = k_ref[z]
    lane = lax.broadcasted_iota(jnp.int32, (WIN, LANES), 1)
    first = lane == 0
    last = lane == LANES - 1

    def layer(z, carry):
        k = k_s[z + 1]
        side = 0.5 * rate
        tall = 0.5 * rate * z_weight
        c = [
            tall * (k + k_s[z]),
            tall * (k + k_s[z + 2]),
            side * (k + pltpu.roll(k, 1, 0)),
            side * (k + pltpu.roll(k, WIN - 1, 0)),
            side * (k + jnp.where(first, 0.0, pltpu.roll(k, 1, 1))),
            side * (k + jnp.where(last, 0.0, pltpu.roll(k, LANES - 1, 1))),
        ]
        total = ((c[0] + c[1]) + (c[2] + c[3])) + (c[4] + c[5])
        d = jnp.where(k > 0.0, damping / (1.0 + total), 0.0)
        co_s[0, z] = c[0] * d
        co_s[1, z] = c[1] * d
        co_s[2, z] = c[2] * d
        co_s[3, z] = c[3] * d
        co_s[4, z] = jnp.where(first, 0.0, c[4] * d)
        co_s[5, z] = jnp.where(last, 0.0, c[5] * d)
        co_s[6, z] = d
        return carry

    lax.fori_loop(0, NZ, layer, 0)


def one_sweep(src, dst, co_s, db_s):
    for z in range(NZ):
        w = src[z + 1]
        acc = (db_s[z] + (1.0 - damping) * w) + (co_s[0, z] * src[z] + co_s[1, z] * src[z + 2])
        acc = acc + (co_s[2, z] * pltpu.roll(w, 1, 0) + co_s[3, z] * pltpu.roll(w, WIN - 1, 0))
        acc = acc + (co_s[4, z] * pltpu.roll(w, 1, 1) + co_s[5, z] * pltpu.roll(w, LANES - 1, 1))
        dst[z + 1] = acc


def step(a_s, b_s, co_s, db_s, forcing=None):
    for z in range(NZ):
        target = a_s[z + 1]
        if forcing is not None:
            target = target + step_size * forcing[z]
        db_s[z] = co_s[6, z] * target
    one_sweep(a_s, b_s, co_s, db_s)
    one_sweep(b_s, a_s, co_s, db_s)


def early_body(k_ref, f_ref, own_ref, below_ref, above_ref, out_ref, next_ref, k_s, co_s, a_s, b_s, db_s, f_s):
    coefficients(step_size, k_ref, k_s, co_s)
    clear_ends(a_s, b_s)
    load_window(a_s, strips_of(below_ref, 0), strips_of(own_ref, 0), strips_of(above_ref, 0))
    for n in range(3):
        rows = 11 - 2 * n
        for z in range(NZ):
            s = z // 2
            for m in (n, 5 - n):
                f_s[m, z] = jnp.zeros((WIN, LANES), F32)
                f_s[m, z, OWN:HIGH] = f_ref[m, z]
            f_s[n, z, OWN - rows : OWN] = below_ref[1 + n, s, at(z, STRIP - rows, STRIP)]
            f_s[n, z, HIGH : HIGH + rows] = above_ref[1 + n, s, at(z, 0, rows)]
            f_s[5 - n, z, OWN - STRIP + rows : OWN] = below_ref[1 + n, s, at(z, 0, STRIP - rows)]
            f_s[5 - n, z, HIGH : HIGH + STRIP - rows] = above_ref[1 + n, s, at(z, rows, STRIP)]
    for n in range(6):
        step(a_s, b_s, co_s, db_s, f_s.at[n])
        for z in range(NZ):
            out_ref[n, z] = a_s[z + 1, OWN:HIGH]
    for z in range(NZ):
        next_ref[0, z // 2, at(z, 0, STRIP)] = a_s[z + 1, OWN:HIGH]
        for n in range(2):
            next_ref[1 + n, z // 2, at(z, 0, STRIP)] = f_ref[6 + n, z]


def late_body(
    block_ref, k_ref, own_ref, below_ref, above_ref, start_ref, start_below_ref, start_above_ref,
    out_ref, pow_ref, next_ref, k_s, co_s, a_s, b_s, db_s, f_s, y_s,
):
    coefficients(step_size, k_ref, k_s, co_s)
    clear_ends(a_s, b_s)
    load_window(a_s, strips_of(below_ref, 0), strips_of(own_ref, 0), strips_of(above_ref, 0))
    for n in range(2):
        load_window(f_s, strips_of(below_ref, 1 + n), strips_of(own_ref, 1 + n), strips_of(above_ref, 1 + n))
        step(a_s, b_s, co_s, db_s, f_s.at[pl.ds(1, NZ)])
        if n == 0:
            for z in range(NZ):
                out_ref[z] = a_s[z + 1, OWN:HIGH]
    for z in range(NZ):
        y_s[z] = a_s[z + 1]
    coefficients(coarse_size, k_ref, k_s, co_s)
    load_window(a_s, strips_of(start_below_ref, 0), strips_of(start_ref, 0), strips_of(start_above_ref, 0))
    step(a_s, b_s, co_s, db_s)
    later = block_ref[0] > 0
    for z in range(NZ):
        a_s[z + 1] = y_s[z] - jnp.where(later, a_s[z + 1], 0.0)
    for n in range(5):
        if n > 0:
            step(a_s, b_s, co_s, db_s)
        for z in range(NZ):
            pow_ref[n, z] = a_s[z + 1, OWN:HIGH]
    for z in range(NZ):
        next_ref[0, z // 2, at(z, 0, STRIP)] = a_s[z + 1, OWN:HIGH]


def powers_body(
    core_ref, side_ref, block_ref, k_ref, own_ref, below_ref, above_ref, early_ref,
    out_ref, k_s, co_s, a_s, b_s, db_s, pow_s,
):
    coefficients(coarse_size, k_ref, k_s, co_s)
    clear_ends(a_s, b_s)
    load_window(a_s, strips_of(below_ref, 0), strips_of(own_ref, 0), strips_of(above_ref, 0))
    for n in range(5):
        for z in range(NZ):
            pow_s[n, z] = early_ref[n, z]
    for n in range(3):
        step(a_s, b_s, co_s, db_s)
        for z in range(NZ):
            pow_s[5 + n, z] = a_s[z + 1, OWN:HIGH]
    c = block_ref[0]
    for b in range(NB):
        power = jnp.clip(b - c, 0, NB - 1)
        live = b >= c
        for y in range(4):
            value = pow_s[power, 2 * (2 * y + side_ref[0]) + core_ref[0]]
            out_ref[b, y * STRIP : (y + 1) * STRIP] = jnp.where(live, value, 0.0)


SWEEP_SCRATCH = (
    pltpu.VMEM((NZ + 2, WIN, LANES), F32),
    pltpu.VMEM((7, NZ, WIN, LANES), F32),
    pltpu.VMEM((NZ + 2, WIN, LANES), F32),
    pltpu.VMEM((NZ + 2, WIN, LANES), F32),
    pltpu.VMEM((NZ, WIN, LANES), F32),
)


def collect_body(core_ref, side_ref, got_ref, early_ref, late_ref, out_ref):
    for y in range(4):
        z = 2 * (2 * y + side_ref[0]) + core_ref[0]
        rows = slice(y * STRIP, (y + 1) * STRIP)
        total = got_ref[0, rows]
        for b in range(1, NB):
            total = total + got_ref[b, rows]
        out_ref[7 * 4 + y, 0:STRIP] = total
        for n in range(6):
            out_ref[n * 4 + y, 0:STRIP] = early_ref[n, z]
        out_ref[6 * 4 + y, 0:STRIP] = late_ref[z]
        for n in range(8):
            out_ref[n * 4 + y, STRIP:16] = jnp.zeros((16 - STRIP, LANES), F32)


def home_body(got_ref, out_ref):
    for zl in range(4):
        for y in range(4):
            m = chip_order(zl, y)
            for core in range(2):
                out_ref[core, m * STRIP : (m + 1) * STRIP] = got_ref[(zl * 2 + core) * 4 + y, 0:STRIP]


def on_device(guess, source, diffusivity, initial):
    guess = guess[0]
    source = source[0]
    core = lax.axis_index("core")[None]
    side = lax.axis_index("zhi")[None]
    place = lax.axis_index(("zl", "core"))[None]
    block = lax.axis_index(BLOCKS)[None]

    previous = lax.ppermute(guess, BLOCKS + ("zl", "core"), [(8 * b + 7, 8 * b + 15) for b in range(NB - 1)])
    sent = pl.pallas_call(
        scatter_body,
        out_shape=sds(64, PAIR, LANES),
        in_specs=[pl.BlockSpec(memory_space=pltpu.SMEM)] * 2 + [pl.BlockSpec(memory_space=pltpu.HBM)] * 4,
        out_specs=pl.BlockSpec(memory_space=pltpu.VMEM),
        scratch_shapes=[
            pltpu.VMEM((2, NY, LANES), F32),
            pltpu.VMEM((2, NY, LANES), F32),
            pltpu.SemaphoreType.DMA((2,)),
        ],
        compiler_params=pltpu.CompilerParams(vmem_limit_bytes=60 * 1024 * 1024),
    )(place, block, source, previous, diffusivity, initial)
    strips = lax.all_to_all(sent, BLOCK, 0, 0, tiled=True).reshape(8, 8, PAIR, LANES)
    strips2 = lax.ppermute(strips, "core", [(0, 1), (1, 0)])

    f, k, f_up, f_down = call(
        pack_body,
        [sds(8, NZ, STRIP, LANES), sds(NZ, WIN, LANES)] + [sds(4, 8, PAIR, LANES)] * 2,
        core, strips, strips2, smem=1,
    )

    def exchange(up, down):
        below = lax.ppermute(up, ("zl", "y"), neighbours(1))
        above = lax.ppermute(down, ("zl", "y"), neighbours(-1))
        return below, above

    flops = NZ * WIN * LANES * 15
    window = pltpu.VMEM((NZ, WIN, LANES), F32)
    f_below, f_above = exchange(f_up, f_down)
    v_early, state = call(
        early_body, [sds(6, NZ, STRIP, LANES), sds(3, 8, PAIR, LANES)],
        k, f, f_up, f_below, f_above, flops=12 * flops,
        scratch=SWEEP_SCRATCH + (pltpu.VMEM((6, NZ, WIN, LANES), F32),),
    )
    below, above = exchange(state, state)
    v_late, first_powers, last = call(
        late_body, [sds(NZ, STRIP, LANES), sds(5, NZ, STRIP, LANES), sds(1, 8, PAIR, LANES)],
        block, k, state, below, above, f_up, f_below, f_above, smem=1, flops=14 * flops,
        scratch=SWEEP_SCRATCH + (pltpu.VMEM((NZ + 2, WIN, LANES), F32), window),
    )
    below, above = exchange(last, last)
    (powers,) = call(
        powers_body, [sds(NB, 4 * STRIP, LANES)],
        core, side, block, k, last, below, above, first_powers, smem=3, flops=6 * flops,
        scratch=SWEEP_SCRATCH + (pltpu.VMEM((NB, NZ, STRIP, LANES), F32),),
    )
    arrived = lax.all_to_all(powers, BLOCKS, 0, 0, tiled=True)
    (back,) = call(collect_body, [sds(32, 16, LANES)], core, side, arrived, v_early, v_late, smem=2)
    returned = lax.all_to_all(back, ("zl", "core", "y"), 0, 0, tiled=True)
    (result,) = call(home_body, [sds(2, NY, LANES)], returned)
    return result[None]


def solution(mesh):
    fine = Mesh(mesh.devices.reshape(SIZES), AXES)
    tm = ("x", "zh", "zl", "core")
    space = ("y", "zhi")
    in_specs = (P(tm, space, None, None), P(tm, space, None, None), P(space, None, None), P(space, None, None))
    out_specs = P(tm, space, None, None)
    return jax.shard_map(on_device, mesh=fine, in_specs=in_specs, out_specs=out_specs, check_vma=False)
```

```python
import functools

import jax
import jax.numpy as jnp
from jax import lax
from jax.experimental import pallas as pl
from jax.experimental.pallas import tpu as pltpu
from jax.sharding import Mesh, PartitionSpec as P

F32 = jnp.float32

damping = 0.8
step_size = 0.5
coarse_size = 4.0
z_weight = 8.0

AXES = ("x", "zh", "zl", "core", "y", "zhi")
SIZES = (4, 2, 4, 2, 4, 2)
BLOCK = ("zl", "core", "y", "zhi")
BLOCKS = ("x", "zh")
NB = 8
NZ = 16
NY = 192
CHIPS = 16
STRIP = NY // CHIPS
PAIR = 2 * STRIP
LANES = 128
LOW, OWN, HIGH, WIN = 4, 16, 28, 40


def chip_order(zl, y):
    return zl * 4 + (y if zl % 2 == 0 else 3 - y)


def neighbours(step):
    place = {chip_order(zl, y): zl * 4 + y for zl in range(4) for y in range(4)}
    return [(place[m], place[m + step]) for m in range(CHIPS) if 0 <= m + step < CHIPS]


def at(z, first, last):
    return slice((z % 2) * STRIP + first, (z % 2) * STRIP + last)


def call(body, outs, *args, scratch=(), smem=0, flops=0):
    specs = [pl.BlockSpec(memory_space=pltpu.SMEM)] * smem
    specs += [pl.BlockSpec(memory_space=pltpu.VMEM)] * (len(args) - smem)
    out_specs = [pl.BlockSpec(memory_space=pltpu.VMEM)] * len(outs)
    size = sum(4 * a.size for a in args) + sum(4 * o.size for o in outs)
    return pl.pallas_call(
        body,
        out_shape=list(outs),
        in_specs=specs,
        out_specs=out_specs,
        scratch_shapes=list(scratch),
        compiler_params=pltpu.CompilerParams(vmem_limit_bytes=32 * 1024 * 1024),
        cost_estimate=pl.CostEstimate(flops=flops, bytes_accessed=size, transcendentals=0),
    )(*args)


def sds(*shape):
    return jax.ShapeDtypeStruct(shape, F32)


def scatter_body(
    j_ref, block_ref, src_hbm, prev6_hbm, prev7_hbm, cond_hbm, init_hbm, out_ref, src_ref, extra_ref, sems
):
    place = j_ref[0]
    source_copy = pltpu.make_async_copy(src_hbm, src_ref, sems.at[0])
    source_copy.start()
    first = block_ref[0] == 0
    for live, field in (
        (place < 6, cond_hbm),
        ((place > 5) & first, init_hbm),
        ((place == 6) & jnp.logical_not(first), prev6_hbm),
        ((place == 7) & jnp.logical_not(first), prev7_hbm),
    ):

        @pl.when(live)
        def _(field=field):
            pltpu.make_async_copy(field, extra_ref, sems.at[1]).start()

    def each():
        for zl in range(4):
            for y in range(4):
                for zhi in range(2):
                    for core in range(2):
                        yield ((zl * 2 + core) * 4 + y) * 2 + zhi, core, chip_order(zl, y)

    source_copy.wait()
    for to, core, m in each():
        for r in range(6):
            row = m * STRIP + 2 * r
            out_ref[to, r] = src_ref[core, row : row + 2]
    pltpu.make_async_copy(cond_hbm, extra_ref, sems.at[1]).wait()

    def fill(shift, half):
        for to, core, m in each():
            m = m + shift
            for r in range(3):
                row = m * STRIP + 6 * half + 2 * r
                if 0 <= m < CHIPS:
                    out_ref[to, 6 + r] = extra_ref[core, row : row + 2]
                else:
                    out_ref[to, 6 + r] = jnp.zeros((2, LANES), F32)

    for half in range(2):
        pl.when((place == half) | (place == 6 + half))(functools.partial(fill, 0, half))
        pl.when(place == 2 + half)(functools.partial(fill, 1, half))
        pl.when(place == 4 + half)(functools.partial(fill, -1, half))


def pack_body(core_ref, own_ref, other_ref, f_ref, k_ref, up_ref, down_ref):
    def order(halves):
        for z in range(NZ):
            half, s = halves[z % 2], z // 2
            k_ref[z, 0:LOW] = jnp.zeros((LOW, LANES), F32)
            for r in range(6):
                for n in range(8):
                    f_ref[n, z, 2 * r : 2 * r + 2] = half[n, s, r]
                part, extra = r // 3, 6 + r % 3
                start = half[6 + part, s, extra]
                up_ref[0, s, at(z, 2 * r, 2 * r + 2)] = start
                down_ref[0, s, at(z, 2 * r, 2 * r + 2)] = start
                for place, base in ((4, LOW), (0, OWN), (2, HIGH)):
                    k_ref[z, base + 2 * r : base + 2 * r + 2] = half[place + part, s, extra]

    pl.when(core_ref[0] == 0)(functools.partial(order, (own_ref, other_ref)))
    pl.when(core_ref[0] == 1)(functools.partial(order, (other_ref, own_ref)))
    for z in range(NZ):
        s = z // 2
        for n in range(3):
            rows = 11 - 2 * n
            early, late = f_ref[n, z], f_ref[5 - n, z]
            down_ref[1 + n, s, at(z, 0, rows)] = early[0:rows]
            down_ref[1 + n, s, at(z, rows, STRIP)] = late[0 : STRIP - rows]
            up_ref[1 + n, s, at(z, STRIP - rows, STRIP)] = early[STRIP - rows : STRIP]
            up_ref[1 + n, s, at(z, 0, STRIP - rows)] = late[rows:STRIP]


def clear_ends(*refs):
    zero = jnp.zeros((WIN, LANES), F32)
    for ref in refs:
        ref[0] = zero
        ref[NZ + 1] = zero


def load_window(a_s, below, own, above):
    zero = jnp.zeros((LOW, LANES), F32)
    for z in range(NZ):
        a_s[z + 1, 0:LOW] = zero
        a_s[z + 1, LOW:OWN] = below(z)
        a_s[z + 1, OWN:HIGH] = own(z)
        a_s[z + 1, HIGH:WIN] = above(z)


def strips_of(ref, field):
    return lambda z: ref[field, z // 2, at(z, 0, STRIP)]


def coefficients(rate, k_ref, k_s, co_s):
    clear_ends(k_s)
    for z in range(NZ):
        k_s[z + 1] = k_ref[z]
    lane = lax.broadcasted_iota(jnp.int32, (WIN, LANES), 1)
    first = lane == 0
    last = lane == LANES - 1

    def layer(z, carry):
        k = k_s[z + 1]
        side = 0.5 * rate
        tall = 0.5 * rate * z_weight
        c = [
            tall * (k + k_s[z]),
            tall * (k + k_s[z + 2]),
            side * (k + pltpu.roll(k, 1, 0)),
            side * (k + pltpu.roll(k, WIN - 1, 0)),
            side * (k + jnp.where(first, 0.0, pltpu.roll(k, 1, 1))),
            side * (k + jnp.where(last, 0.0, pltpu.roll(k, LANES - 1, 1))),
        ]
        total = ((c[0] + c[1]) + (c[2] + c[3])) + (c[4] + c[5])
        d = jnp.where(k > 0.0, damping / (1.0 + total), 0.0)
        co_s[0, z] = c[0] * d
        co_s[1, z] = c[1] * d
        co_s[2, z] = c[2] * d
        co_s[3, z] = c[3] * d
        co_s[4, z] = jnp.where(first, 0.0, c[4] * d)
        co_s[5, z] = jnp.where(last, 0.0, c[5] * d)
        co_s[6, z] = d
        return carry

    lax.fori_loop(0, NZ, layer, 0)


def one_sweep(src, dst, co_s, db_s, rows):
    tall = rows.stop - rows.start
    for z in range(NZ):
        w = src[z + 1, rows]
        acc = (db_s[z, rows] + (1.0 - damping) * w) + (
            co_s[0, z, rows] * src[z, rows] + co_s[1, z, rows] * src[z + 2, rows]
        )
        acc = acc + (
            co_s[2, z, rows] * pltpu.roll(w, 1, 0) + co_s[3, z, rows] * pltpu.roll(w, tall - 1, 0)
        )
        acc = acc + (
            co_s[4, z, rows] * pltpu.roll(w, 1, 1) + co_s[5, z, rows] * pltpu.roll(w, LANES - 1, 1)
        )
        dst[z + 1, rows] = acc


def step(halo, a_s, b_s, co_s, db_s, forcing=None):
    rows = slice(8, 32) if halo <= 4 else slice(8, WIN) if halo <= 8 else slice(0, WIN)
    for z in range(NZ):
        target = a_s[z + 1, rows]
        if forcing is not None:
            target = target + step_size * forcing[z, rows]
        db_s[z, rows] = co_s[6, z, rows] * target
    one_sweep(a_s, b_s, co_s, db_s, rows)
    one_sweep(b_s, a_s, co_s, db_s, rows)


def early_body(k_ref, f_ref, own_ref, below_ref, above_ref, out_ref, next_ref, k_s, co_s, a_s, b_s, db_s, f_s):
    coefficients(step_size, k_ref, k_s, co_s)
    clear_ends(a_s, b_s)
    load_window(a_s, strips_of(below_ref, 0), strips_of(own_ref, 0), strips_of(above_ref, 0))
    for n in range(3):
        rows = 11 - 2 * n
        for z in range(NZ):
            s = z // 2
            for m in (n, 5 - n):
                f_s[m, z] = jnp.zeros((WIN, LANES), F32)
                f_s[m, z, OWN:HIGH] = f_ref[m, z]
            f_s[n, z, OWN - rows : OWN] = below_ref[1 + n, s, at(z, STRIP - rows, STRIP)]
            f_s[n, z, HIGH : HIGH + rows] = above_ref[1 + n, s, at(z, 0, rows)]
            f_s[5 - n, z, OWN - STRIP + rows : OWN] = below_ref[1 + n, s, at(z, 0, STRIP - rows)]
            f_s[5 - n, z, HIGH : HIGH + STRIP - rows] = above_ref[1 + n, s, at(z, rows, STRIP)]
    for n in range(6):
        step(12 - 2 * n, a_s, b_s, co_s, db_s, f_s.at[n])
        for z in range(NZ):
            out_ref[n, z] = a_s[z + 1, OWN:HIGH]
    for z in range(NZ):
        next_ref[0, z // 2, at(z, 0, STRIP)] = a_s[z + 1, OWN:HIGH]
        for n in range(2):
            next_ref[1 + n, z // 2, at(z, 0, STRIP)] = f_ref[6 + n, z]


def late_body(
    block_ref, k_ref, own_ref, below_ref, above_ref, start_ref, start_below_ref, start_above_ref,
    out_ref, pow_ref, next_ref, k_s, co_s, a_s, b_s, db_s, f_s, y_s,
):
    coefficients(step_size, k_ref, k_s, co_s)
    clear_ends(a_s, b_s)
    load_window(a_s, strips_of(below_ref, 0), strips_of(own_ref, 0), strips_of(above_ref, 0))
    for n in range(2):
        load_window(f_s, strips_of(below_ref, 1 + n), strips_of(own_ref, 1 + n), strips_of(above_ref, 1 + n))
        step(12 - 2 * n, a_s, b_s, co_s, db_s, f_s.at[pl.ds(1, NZ)])
        if n == 0:
            for z in range(NZ):
                out_ref[z] = a_s[z + 1, OWN:HIGH]
    for z in range(NZ):
        y_s[z] = a_s[z + 1]
    coefficients(coarse_size, k_ref, k_s, co_s)
    load_window(a_s, strips_of(start_below_ref, 0), strips_of(start_ref, 0), strips_of(start_above_ref, 0))
    step(10, a_s, b_s, co_s, db_s)
    later = block_ref[0] > 0
    for z in range(NZ):
        a_s[z + 1] = y_s[z] - jnp.where(later, a_s[z + 1], 0.0)
    for n in range(5):
        if n > 0:
            step(10 - 2 * n, a_s, b_s, co_s, db_s)
        for z in range(NZ):
            pow_ref[n, z] = a_s[z + 1, OWN:HIGH]
    for z in range(NZ):
        next_ref[0, z // 2, at(z, 0, STRIP)] = a_s[z + 1, OWN:HIGH]


def powers_body(
    core_ref, side_ref, block_ref, k_ref, own_ref, below_ref, above_ref, early_ref,
    out_ref, k_s, co_s, a_s, b_s, db_s, pow_s,
):
    coefficients(coarse_size, k_ref, k_s, co_s)
    clear_ends(a_s, b_s)
    load_window(a_s, strips_of(below_ref, 0), strips_of(own_ref, 0), strips_of(above_ref, 0))
    for n in range(5):
        for z in range(NZ):
            pow_s[n, z] = early_ref[n, z]
    for n in range(3):
        step(6 - 2 * n, a_s, b_s, co_s, db_s)
        for z in range(NZ):
            pow_s[5 + n, z] = a_s[z + 1, OWN:HIGH]
    c = block_ref[0]
    for b in range(NB):
        power = jnp.clip(b - c, 0, NB - 1)
        live = b >= c
        for y in range(4):
            value = pow_s[power, 2 * (2 * y + side_ref[0]) + core_ref[0]]
            out_ref[b, y * STRIP : (y + 1) * STRIP] = jnp.where(live, value, 0.0)


SWEEP_SCRATCH = (
    pltpu.VMEM((NZ + 2, WIN, LANES), F32),
    pltpu.VMEM((7, NZ, WIN, LANES), F32),
    pltpu.VMEM((NZ + 2, WIN, LANES), F32),
    pltpu.VMEM((NZ + 2, WIN, LANES), F32),
    pltpu.VMEM((NZ, WIN, LANES), F32),
)


def collect_body(core_ref, side_ref, got_ref, early_ref, late_ref, out_ref):
    for y in range(4):
        z = 2 * (2 * y + side_ref[0]) + core_ref[0]
        rows = slice(y * STRIP, (y + 1) * STRIP)
        total = got_ref[0, rows]
        for b in range(1, NB):
            total = total + got_ref[b, rows]
        out_ref[7 * 4 + y, 0:STRIP] = total
        for n in range(6):
            out_ref[n * 4 + y, 0:STRIP] = early_ref[n, z]
        out_ref[6 * 4 + y, 0:STRIP] = late_ref[z]
        for n in range(8):
            out_ref[n * 4 + y, STRIP:16] = jnp.zeros((16 - STRIP, LANES), F32)


def home_body(got_ref, out_ref):
    for zl in range(4):
        for y in range(4):
            m = chip_order(zl, y)
            for core in range(2):
                out_ref[core, m * STRIP : (m + 1) * STRIP] = got_ref[(zl * 2 + core) * 4 + y, 0:STRIP]


def on_device(guess, source, diffusivity, initial):
    guess = guess[0]
    source = source[0]
    core = lax.axis_index("core")[None]
    side = lax.axis_index("zhi")[None]
    place = lax.axis_index(("zl", "core"))[None]
    block = lax.axis_index(BLOCKS)[None]

    def onward(place):
        return lax.ppermute(guess, BLOCKS + ("zl", "core"), [(8 * b + 7, 8 * b + 8 + place) for b in range(NB - 1)])

    sent = pl.pallas_call(
        scatter_body,
        out_shape=sds(64, 9, 2, LANES),
        in_specs=[pl.BlockSpec(memory_space=pltpu.SMEM)] * 2 + [pl.BlockSpec(memory_space=pl.ANY)] * 5,
        out_specs=pl.BlockSpec(memory_space=pltpu.VMEM),
        scratch_shapes=[
            pltpu.VMEM((2, NY, LANES), F32),
            pltpu.VMEM((2, NY, LANES), F32),
            pltpu.SemaphoreType.DMA((2,)),
        ],
        compiler_params=pltpu.CompilerParams(vmem_limit_bytes=60 * 1024 * 1024),
    )(place, block, source, onward(6), onward(7), diffusivity, initial)
    strips = lax.all_to_all(sent, BLOCK, 0, 0, tiled=True).reshape(8, 8, 9, 2, LANES)
    strips2 = lax.ppermute(strips, "core", [(0, 1), (1, 0)])

    f, k, f_up, f_down = call(
        pack_body,
        [sds(8, NZ, STRIP, LANES), sds(NZ, WIN, LANES)] + [sds(4, 8, PAIR, LANES)] * 2,
        core, strips, strips2, smem=1,
    )

    def exchange(up, down):
        below = lax.ppermute(up, ("zl", "y"), neighbours(1))
        above = lax.ppermute(down, ("zl", "y"), neighbours(-1))
        return below, above

    flops = NZ * WIN * LANES * 15
    window = pltpu.VMEM((NZ, WIN, LANES), F32)
    f_below, f_above = exchange(f_up, f_down)
    v_early, state = call(
        early_body, [sds(6, NZ, STRIP, LANES), sds(3, 8, PAIR, LANES)],
        k, f, f_up, f_below, f_above, flops=12 * flops,
        scratch=SWEEP_SCRATCH + (pltpu.VMEM((6, NZ, WIN, LANES), F32),),
    )
    below, above = exchange(state, state)
    v_late, first_powers, last = call(
        late_body, [sds(NZ, STRIP, LANES), sds(5, NZ, STRIP, LANES), sds(1, 8, PAIR, LANES)],
        block, k, state, below, above, f_up, f_below, f_above, smem=1, flops=14 * flops,
        scratch=SWEEP_SCRATCH + (pltpu.VMEM((NZ + 2, WIN, LANES), F32), window),
    )
    below, above = exchange(last, last)
    (powers,) = call(
        powers_body, [sds(NB, 4 * STRIP, LANES)],
        core, side, block, k, last, below, above, first_powers, smem=3, flops=6 * flops,
        scratch=SWEEP_SCRATCH + (pltpu.VMEM((NB, NZ, STRIP, LANES), F32),),
    )
    arrived = lax.all_to_all(powers, BLOCKS, 0, 0, tiled=True)
    (back,) = call(collect_body, [sds(32, 16, LANES)], core, side, arrived, v_early, v_late, smem=2)
    returned = lax.all_to_all(back, ("zl", "core", "y"), 0, 0, tiled=True)
    (result,) = call(home_body, [sds(2, NY, LANES)], returned)
    return result[None]


def solution(mesh):
    fine = Mesh(mesh.devices.reshape(SIZES), AXES)
    tm = ("x", "zh", "zl", "core")
    space = ("y", "zhi")
    in_specs = (P(tm, space, None, None), P(tm, space, None, None), P(space, None, None), P(space, None, None))
    out_specs = P(tm, space, None, None)
    return jax.shard_map(on_device, mesh=fine, in_specs=in_specs, out_specs=out_specs, check_vma=False)
```

```python
import functools

import jax
import jax.numpy as jnp
from jax import lax
from jax.experimental import pallas as pl
from jax.experimental.pallas import tpu as pltpu
from jax.sharding import Mesh, PartitionSpec as P

F32 = jnp.float32

damping = 0.8
step_size = 0.5
coarse_size = 4.0
z_weight = 8.0

AXES = ("x", "zh", "zl", "core", "y", "zhi")
SIZES = (4, 2, 4, 2, 4, 2)
BLOCK = ("zl", "core", "y", "zhi")
BLOCKS = ("x", "zh")
NB = 8
NZ = 16
NY = 192
CHIPS = 16
STRIP = NY // CHIPS
PAIR = 2 * STRIP
LANES = 128
LOW, OWN, HIGH, WIN = 4, 16, 28, 40


def chip_order(zl, y):
    return zl * 4 + (y if zl % 2 == 0 else 3 - y)


def neighbour_route():
    place = {chip_order(zl, y): (zl, y) for zl in range(4) for y in range(4)}
    route = []
    for core, step in ((0, 1), (1, -1)):
        for m in range(CHIPS):
            if 0 <= m + step < CHIPS:
                (zl, y), (to_zl, to_y) = place[m], place[m + step]
                route.append(((zl * 2 + core) * 4 + y, (to_zl * 2 + core) * 4 + to_y))
    return route


def at(z, first, last):
    return slice((z % 2) * STRIP + first, (z % 2) * STRIP + last)


def call(body, outs, *args, scratch=(), smem=0, flops=0):
    specs = [pl.BlockSpec(memory_space=pltpu.SMEM)] * smem
    specs += [pl.BlockSpec(memory_space=pltpu.VMEM)] * (len(args) - smem)
    out_specs = [pl.BlockSpec(memory_space=pltpu.VMEM)] * len(outs)
    size = sum(4 * a.size for a in args) + sum(4 * o.size for o in outs)
    return pl.pallas_call(
        body,
        out_shape=list(outs),
        in_specs=specs,
        out_specs=out_specs,
        scratch_shapes=list(scratch),
        compiler_params=pltpu.CompilerParams(vmem_limit_bytes=32 * 1024 * 1024),
        cost_estimate=pl.CostEstimate(flops=flops, bytes_accessed=size, transcendentals=0),
    )(*args)


def sds(*shape):
    return jax.ShapeDtypeStruct(shape, F32)


def targets():
    for zl in range(4):
        for y in range(4):
            for zhi in range(2):
                for core in range(2):
                    yield ((zl * 2 + core) * 4 + y) * 2 + zhi, core, chip_order(zl, y)


def source_body(src_ref, out_ref):
    for to, core, m in targets():
        for r in range(6):
            row = m * STRIP + 2 * r
            out_ref[to, r] = src_ref[core, row : row + 2]


def extra_body(j_ref, block_ref, prev6_ref, prev7_ref, cond_ref, init_ref, base_ref, out_ref):
    place = j_ref[0]
    first = block_ref[0] == 0
    later = jnp.logical_not(first)

    def fill(ref, shift, half):
        for to, core, m in targets():
            m = m + shift
            for r in range(3):
                row = m * STRIP + 6 * half + 2 * r
                if 0 <= m < CHIPS:
                    out_ref[to, 6 + r] = ref[core, row : row + 2]
                else:
                    out_ref[to, 6 + r] = jnp.zeros((2, LANES), F32)

    for half, prev_ref in ((0, prev6_ref), (1, prev7_ref)):
        for n, shift in enumerate((0, 1, -1)):
            pl.when(place == 2 * n + half)(functools.partial(fill, cond_ref, shift, half))
        pl.when((place == 6 + half) & first)(functools.partial(fill, init_ref, 0, half))
        pl.when((place == 6 + half) & later)(functools.partial(fill, prev_ref, 0, half))


def by_core(core_ref, body, mine, other):
    pl.when(core_ref[0] == 0)(functools.partial(body, mine, other))
    pl.when(core_ref[0] == 1)(functools.partial(body, other, mine))


def pack_body(core_ref, own_ref, other_ref, f_ref, k_ref, start_ref, out_ref):
    def order(*halves):
        for z in range(NZ):
            half, s = halves[z % 2], z // 2
            k_ref[z, 0:LOW] = jnp.zeros((LOW, LANES), F32)
            for r in range(6):
                for n in range(8):
                    f_ref[n, z, 2 * r : 2 * r + 2] = half[n, s, r]
                part, extra = r // 3, 6 + r % 3
                start = half[6 + part, s, extra]
                start_ref[0, s, at(z, 2 * r, 2 * r + 2)] = start
                out_ref[0, s, at(z, 2 * r, 2 * r + 2)] = start
                for place, base in ((4, LOW), (0, OWN), (2, HIGH)):
                    k_ref[z, base + 2 * r : base + 2 * r + 2] = half[place + part, s, extra]

    by_core(core_ref, order, own_ref, other_ref)

    @pl.when(core_ref[0] == 0)
    def _():
        for z in range(NZ):
            for n in range(3):
                rows = 11 - 2 * n
                out_ref[1 + n, z // 2, at(z, STRIP - rows, STRIP)] = f_ref[n, z, STRIP - rows : STRIP]
                out_ref[1 + n, z // 2, at(z, 0, STRIP - rows)] = f_ref[5 - n, z, rows:STRIP]

    @pl.when(core_ref[0] == 1)
    def _():
        for z in range(NZ):
            for n in range(3):
                rows = 11 - 2 * n
                out_ref[1 + n, z // 2, at(z, 0, rows)] = f_ref[n, z, 0:rows]
                out_ref[1 + n, z // 2, at(z, rows, STRIP)] = f_ref[5 - n, z, 0 : STRIP - rows]


def clear_ends(*refs):
    zero = jnp.zeros((WIN, LANES), F32)
    for ref in refs:
        ref[0] = zero
        ref[NZ + 1] = zero


def load_window(core_ref, a_s, field, own_ref, got_ref, got2_ref):
    def load(below_ref, above_ref):
        zero = jnp.zeros((LOW, LANES), F32)
        for z in range(NZ):
            a_s[z + 1, 0:LOW] = zero
            a_s[z + 1, LOW:OWN] = below_ref[field, z // 2, at(z, 0, STRIP)]
            a_s[z + 1, OWN:HIGH] = own_ref[field, z // 2, at(z, 0, STRIP)]
            a_s[z + 1, HIGH:WIN] = above_ref[field, z // 2, at(z, 0, STRIP)]

    by_core(core_ref, load, got_ref, got2_ref)


def coefficients(rate, k_ref, k_s, co_s):
    clear_ends(k_s)
    for z in range(NZ):
        k_s[z + 1] = k_ref[z]
    lane = lax.broadcasted_iota(jnp.int32, (WIN, LANES), 1)
    first = lane == 0
    last = lane == LANES - 1

    def layer(z, carry):
        k = k_s[z + 1]
        side = 0.5 * rate
        tall = 0.5 * rate * z_weight
        c = [
            tall * (k + k_s[z]),
            tall * (k + k_s[z + 2]),
            side * (k + pltpu.roll(k, 1, 0)),
            side * (k + pltpu.roll(k, WIN - 1, 0)),
            side * (k + jnp.where(first, 0.0, pltpu.roll(k, 1, 1))),
            side * (k + jnp.where(last, 0.0, pltpu.roll(k, LANES - 1, 1))),
        ]
        total = ((c[0] + c[1]) + (c[2] + c[3])) + (c[4] + c[5])
        d = jnp.where(k > 0.0, damping / (1.0 + total), 0.0)
        co_s[0, z] = c[0] * d
        co_s[1, z] = c[1] * d
        co_s[2, z] = c[2] * d
        co_s[3, z] = c[3] * d
        co_s[4, z] = jnp.where(first, 0.0, c[4] * d)
        co_s[5, z] = jnp.where(last, 0.0, c[5] * d)
        co_s[6, z] = d
        return carry

    lax.fori_loop(0, NZ, layer, 0)


def one_sweep(src, dst, co_s, db_s, rows):
    tall = rows.stop - rows.start
    for z in range(NZ):
        w = src[z + 1, rows]
        acc = (db_s[z, rows] + (1.0 - damping) * w) + (
            co_s[0, z, rows] * src[z, rows] + co_s[1, z, rows] * src[z + 2, rows]
        )
        acc = acc + (
            co_s[2, z, rows] * pltpu.roll(w, 1, 0) + co_s[3, z, rows] * pltpu.roll(w, tall - 1, 0)
        )
        acc = acc + (
            co_s[4, z, rows] * pltpu.roll(w, 1, 1) + co_s[5, z, rows] * pltpu.roll(w, LANES - 1, 1)
        )
        dst[z + 1, rows] = acc


def step(halo, a_s, b_s, co_s, db_s, forcing=None):
    rows = slice(8, 32) if halo <= 4 else slice(8, WIN) if halo <= 8 else slice(0, WIN)
    for z in range(NZ):
        target = a_s[z + 1, rows]
        if forcing is not None:
            target = target + step_size * forcing[z, rows]
        db_s[z, rows] = co_s[6, z, rows] * target
    one_sweep(a_s, b_s, co_s, db_s, rows)
    one_sweep(b_s, a_s, co_s, db_s, rows)


def early_body(
    core_ref, k_ref, f_ref, own_ref, got_ref, got2_ref, out_ref, next_ref, k_s, co_s, a_s, b_s, db_s, f_s
):
    coefficients(step_size, k_ref, k_s, co_s)
    clear_ends(a_s, b_s)
    load_window(core_ref, a_s, 0, own_ref, got_ref, got2_ref)
    for n in range(6):
        for z in range(NZ):
            f_s[n, z] = jnp.zeros((WIN, LANES), F32)
            f_s[n, z, OWN:HIGH] = f_ref[n, z]

    def halos(below_ref, above_ref):
        for n in range(3):
            rows = 11 - 2 * n
            for z in range(NZ):
                s = z // 2
                f_s[n, z, OWN - rows : OWN] = below_ref[1 + n, s, at(z, STRIP - rows, STRIP)]
                f_s[n, z, HIGH : HIGH + rows] = above_ref[1 + n, s, at(z, 0, rows)]
                f_s[5 - n, z, OWN - STRIP + rows : OWN] = below_ref[1 + n, s, at(z, 0, STRIP - rows)]
                f_s[5 - n, z, HIGH : HIGH + STRIP - rows] = above_ref[1 + n, s, at(z, rows, STRIP)]

    by_core(core_ref, halos, got_ref, got2_ref)
    for n in range(6):
        step(12 - 2 * n, a_s, b_s, co_s, db_s, f_s.at[n])
        for z in range(NZ):
            out_ref[n, z] = a_s[z + 1, OWN:HIGH]
    for z in range(NZ):
        next_ref[0, z // 2, at(z, 0, STRIP)] = a_s[z + 1, OWN:HIGH]
        for n in range(2):
            next_ref[1 + n, z // 2, at(z, 0, STRIP)] = f_ref[6 + n, z]


def late_body(
    core_ref, block_ref, k_ref, own_ref, got_ref, got2_ref, start_ref, start_got_ref, start_got2_ref,
    out_ref, pow_ref, next_ref, k_s, co_s, a_s, b_s, db_s, f_s, y_s,
):
    coefficients(step_size, k_ref, k_s, co_s)
    clear_ends(a_s, b_s)
    load_window(core_ref, a_s, 0, own_ref, got_ref, got2_ref)
    for n in range(2):
        load_window(core_ref, f_s, 1 + n, own_ref, got_ref, got2_ref)
        step(12 - 2 * n, a_s, b_s, co_s, db_s, f_s.at[pl.ds(1, NZ)])
        if n == 0:
            for z in range(NZ):
                out_ref[z] = a_s[z + 1, OWN:HIGH]
    for z in range(NZ):
        y_s[z] = a_s[z + 1]
    coefficients(coarse_size, k_ref, k_s, co_s)
    load_window(core_ref, a_s, 0, start_ref, start_got_ref, start_got2_ref)
    step(10, a_s, b_s, co_s, db_s)
    later = block_ref[0] > 0
    for z in range(NZ):
        a_s[z + 1] = y_s[z] - jnp.where(later, a_s[z + 1], 0.0)
    for n in range(5):
        if n > 0:
            step(10 - 2 * n, a_s, b_s, co_s, db_s)
        for z in range(NZ):
            pow_ref[n, z] = a_s[z + 1, OWN:HIGH]
    for z in range(NZ):
        next_ref[0, z // 2, at(z, 0, STRIP)] = a_s[z + 1, OWN:HIGH]


def powers_body(
    core_ref, side_ref, block_ref, k_ref, own_ref, got_ref, got2_ref, early_ref,
    out_ref, k_s, co_s, a_s, b_s, db_s, pow_s,
):
    coefficients(coarse_size, k_ref, k_s, co_s)
    clear_ends(a_s, b_s)
    load_window(core_ref, a_s, 0, own_ref, got_ref, got2_ref)
    for n in range(5):
        for z in range(NZ):
            pow_s[n, z] = early_ref[n, z]
    for n in range(3):
        step(6 - 2 * n, a_s, b_s, co_s, db_s)
        for z in range(NZ):
            pow_s[5 + n, z] = a_s[z + 1, OWN:HIGH]
    c = block_ref[0]
    for b in range(NB):
        power = jnp.clip(b - c, 0, NB - 1)
        live = b >= c
        for y in range(4):
            value = pow_s[power, 2 * (2 * y + side_ref[0]) + core_ref[0]]
            out_ref[b, y * STRIP : (y + 1) * STRIP] = jnp.where(live, value, 0.0)


SWEEP_SCRATCH = (
    pltpu.VMEM((NZ + 2, WIN, LANES), F32),
    pltpu.VMEM((7, NZ, WIN, LANES), F32),
    pltpu.VMEM((NZ + 2, WIN, LANES), F32),
    pltpu.VMEM((NZ + 2, WIN, LANES), F32),
    pltpu.VMEM((NZ, WIN, LANES), F32),
)


def collect_body(core_ref, side_ref, got_ref, early_ref, late_ref, out_ref):
    for y in range(4):
        z = 2 * (2 * y + side_ref[0]) + core_ref[0]
        rows = slice(y * STRIP, (y + 1) * STRIP)
        total = got_ref[0, rows]
        for b in range(1, NB):
            total = total + got_ref[b, rows]
        out_ref[7 * 4 + y, 0:STRIP] = total
        for n in range(6):
            out_ref[n * 4 + y, 0:STRIP] = early_ref[n, z]
        out_ref[6 * 4 + y, 0:STRIP] = late_ref[z]
        for n in range(8):
            out_ref[n * 4 + y, STRIP:16] = jnp.zeros((16 - STRIP, LANES), F32)


def home_body(got_ref, out_ref):
    for zl in range(4):
        for y in range(4):
            m = chip_order(zl, y)
            for core in range(2):
                out_ref[core, m * STRIP : (m + 1) * STRIP] = got_ref[(zl * 2 + core) * 4 + y, 0:STRIP]


def on_device(guess, source, diffusivity, initial):
    guess = guess[0]
    source = source[0]
    core = lax.axis_index("core")[None]
    side = lax.axis_index("zhi")[None]
    place = lax.axis_index(("zl", "core"))[None]
    block = lax.axis_index(BLOCKS)[None]

    def onward(place):
        return lax.ppermute(guess, BLOCKS + ("zl", "core"), [(8 * b + 7, 8 * b + 8 + place) for b in range(NB - 1)])

    prev6, prev7 = onward(6), onward(7)
    (base,) = call(source_body, [sds(64, 9, 2, LANES)], source)
    vmem = pl.BlockSpec(memory_space=pltpu.VMEM)
    sent = pl.pallas_call(
        extra_body,
        out_shape=sds(64, 9, 2, LANES),
        in_specs=[pl.BlockSpec(memory_space=pltpu.SMEM)] * 2 + [vmem] * 5,
        out_specs=vmem,
        input_output_aliases={6: 0},
        compiler_params=pltpu.CompilerParams(vmem_limit_bytes=32 * 1024 * 1024),
    )(place, block, prev6, prev7, diffusivity, initial, base)
    strips = lax.all_to_all(sent, BLOCK, 0, 0, tiled=True).reshape(8, 8, 9, 2, LANES)

    def swap(mine):
        return lax.ppermute(mine, "core", [(0, 1), (1, 0)])

    def exchange(mine):
        got = lax.ppermute(mine, ("zl", "core", "y"), neighbour_route())
        return got, swap(got)

    f, k, start, message = call(
        pack_body,
        [sds(8, NZ, STRIP, LANES), sds(NZ, WIN, LANES), sds(1, 8, PAIR, LANES), sds(4, 8, PAIR, LANES)],
        core, strips, swap(strips), smem=1,
    )
    flops = NZ * WIN * LANES * 15
    window = pltpu.VMEM((NZ, WIN, LANES), F32)
    got, got2 = exchange(message)
    v_early, state = call(
        early_body, [sds(6, NZ, STRIP, LANES), sds(3, 8, PAIR, LANES)],
        core, k, f, start, got, got2, smem=1, flops=12 * flops,
        scratch=SWEEP_SCRATCH + (pltpu.VMEM((6, NZ, WIN, LANES), F32),),
    )
    v_late, first_powers, last = call(
        late_body, [sds(NZ, STRIP, LANES), sds(5, NZ, STRIP, LANES), sds(1, 8, PAIR, LANES)],
        core, block, k, state, *exchange(state), start, got, got2, smem=2, flops=14 * flops,
        scratch=SWEEP_SCRATCH + (pltpu.VMEM((NZ + 2, WIN, LANES), F32), window),
    )
    (powers,) = call(
        powers_body, [sds(NB, 4 * STRIP, LANES)],
        core, side, block, k, last, *exchange(last), first_powers, smem=3, flops=6 * flops,
        scratch=SWEEP_SCRATCH + (pltpu.VMEM((NB, NZ, STRIP, LANES), F32),),
    )
    arrived = lax.all_to_all(powers, BLOCKS, 0, 0, tiled=True)
    (back,) = call(collect_body, [sds(32, 16, LANES)], core, side, arrived, v_early, v_late, smem=2)
    returned = lax.all_to_all(back, ("zl", "core", "y"), 0, 0, tiled=True)
    (result,) = call(home_body, [sds(2, NY, LANES)], returned)
    return result[None]


def solution(mesh):
    fine = Mesh(mesh.devices.reshape(SIZES), AXES)
    tm = ("x", "zh", "zl", "core")
    space = ("y", "zhi")
    in_specs = (P(tm, space, None, None), P(tm, space, None, None), P(space, None, None), P(space, None, None))
    out_specs = P(tm, space, None, None)
    return jax.shard_map(on_device, mesh=fine, in_specs=in_specs, out_specs=out_specs, check_vma=False)
```

```python
import functools

import jax
import jax.numpy as jnp
from jax import lax
from jax.experimental import pallas as pl
from jax.experimental.pallas import tpu as pltpu
from jax.sharding import Mesh, PartitionSpec as P

F32 = jnp.float32

damping = 0.8
step_size = 0.5
coarse_size = 4.0
z_weight = 8.0

AXES = ("x", "zh", "zl", "core", "y", "zhi")
SIZES = (4, 2, 4, 2, 4, 2)
BLOCK = ("zl", "core", "y", "zhi")
BLOCKS = ("x", "zh")
NB = 8
NZ = 16
NY = 192
CHIPS = 16
STRIP = NY // CHIPS
PAIR = 2 * STRIP
LANES = 128
LOW, OWN, HIGH, WIN = 4, 16, 28, 40


def chip_order(zl, y):
    return zl * 4 + (y if zl % 2 == 0 else 3 - y)


def neighbour_route():
    place = {chip_order(zl, y): (zl, y) for zl in range(4) for y in range(4)}
    route = []
    for core, step in ((0, 1), (1, -1)):
        for m in range(CHIPS):
            if 0 <= m + step < CHIPS:
                (zl, y), (to_zl, to_y) = place[m], place[m + step]
                route.append(((zl * 2 + core) * 4 + y, (to_zl * 2 + core) * 4 + to_y))
    return route


def at(z, first, last):
    return slice((z % 2) * STRIP + first, (z % 2) * STRIP + last)


def call(body, outs, *args, scratch=(), smem=0, flops=0):
    specs = [pl.BlockSpec(memory_space=pltpu.SMEM)] * smem
    specs += [pl.BlockSpec(memory_space=pltpu.VMEM)] * (len(args) - smem)
    out_specs = [pl.BlockSpec(memory_space=pltpu.VMEM)] * len(outs)
    size = sum(4 * a.size for a in args) + sum(4 * o.size for o in outs)
    return pl.pallas_call(
        body,
        out_shape=list(outs),
        in_specs=specs,
        out_specs=out_specs,
        scratch_shapes=list(scratch),
        compiler_params=pltpu.CompilerParams(vmem_limit_bytes=32 * 1024 * 1024),
        cost_estimate=pl.CostEstimate(flops=flops, bytes_accessed=size, transcendentals=0),
    )(*args)


def sds(*shape):
    return jax.ShapeDtypeStruct(shape, F32)


def targets():
    for zl in range(4):
        for y in range(4):
            for zhi in range(2):
                for core in range(2):
                    yield ((zl * 2 + core) * 4 + y) * 2 + zhi, core, chip_order(zl, y)


def source_body(src_ref, out_ref):
    for to, core, m in targets():
        for r in range(6):
            row = m * STRIP + 2 * r
            out_ref[to, r] = src_ref[core, row : row + 2]


def extra_body(j_ref, block_ref, prev0_ref, prev1_ref, cond_ref, init_ref, base_ref, out_ref):
    place = j_ref[0]
    first = block_ref[0] == 0
    later = jnp.logical_not(first)

    def fill(ref, shift, half):
        for to, core, m in targets():
            m = m + shift
            for r in range(3):
                row = m * STRIP + 6 * half + 2 * r
                if 0 <= m < CHIPS:
                    out_ref[to, 6 + r] = ref[core, row : row + 2]
                else:
                    out_ref[to, 6 + r] = jnp.zeros((2, LANES), F32)

    for half, prev_ref in ((0, prev0_ref), (1, prev1_ref)):
        for n, shift in enumerate((0, 1, -1)):
            pl.when(place == 2 + 2 * n + half)(functools.partial(fill, cond_ref, shift, half))
        pl.when((place == half) & first)(functools.partial(fill, init_ref, 0, half))
        pl.when((place == half) & later)(functools.partial(fill, prev_ref, 0, half))


def by_core(core_ref, body, mine, other):
    pl.when(core_ref[0] == 0)(functools.partial(body, mine, other))
    pl.when(core_ref[0] == 1)(functools.partial(body, other, mine))


def pack_body(core_ref, flip_ref, own_ref, other_ref, f_ref, k_ref, start_ref, out_ref):
    flip = flip_ref[0]

    def order(*halves):
        for z in range(NZ):
            half, s = halves[z % 2], z // 2
            k_ref[z, 0:LOW] = jnp.zeros((LOW, LANES), F32)
            for r in range(6):
                for n in range(8):
                    f_ref[n, z, 2 * r : 2 * r + 2] = half[n, s, r]
                part, extra = r // 3, 6 + r % 3
                start = half[part, s + (1 - 2 * (s % 2)) * flip, extra]
                start_ref[0, s, at(z, 2 * r, 2 * r + 2)] = start
                out_ref[0, s, at(z, 2 * r, 2 * r + 2)] = start
                for place, base in ((6, LOW), (2, OWN), (4, HIGH)):
                    k_ref[z, base + 2 * r : base + 2 * r + 2] = half[place + part, s, extra]

    by_core(core_ref, order, own_ref, other_ref)

    @pl.when(core_ref[0] == 0)
    def _():
        for z in range(NZ):
            for n in range(3):
                rows = 11 - 2 * n
                out_ref[1 + n, z // 2, at(z, STRIP - rows, STRIP)] = f_ref[n, z, STRIP - rows : STRIP]
                out_ref[1 + n, z // 2, at(z, 0, STRIP - rows)] = f_ref[5 - n, z, rows:STRIP]

    @pl.when(core_ref[0] == 1)
    def _():
        for z in range(NZ):
            for n in range(3):
                rows = 11 - 2 * n
                out_ref[1 + n, z // 2, at(z, 0, rows)] = f_ref[n, z, 0:rows]
                out_ref[1 + n, z // 2, at(z, rows, STRIP)] = f_ref[5 - n, z, 0 : STRIP - rows]


def clear_ends(*refs):
    zero = jnp.zeros((WIN, LANES), F32)
    for ref in refs:
        ref[0] = zero
        ref[NZ + 1] = zero


def load_window(core_ref, a_s, field, own_ref, got_ref, got2_ref):
    def load(below_ref, above_ref):
        zero = jnp.zeros((LOW, LANES), F32)
        for z in range(NZ):
            a_s[z + 1, 0:LOW] = zero
            a_s[z + 1, LOW:OWN] = below_ref[field, z // 2, at(z, 0, STRIP)]
            a_s[z + 1, OWN:HIGH] = own_ref[field, z // 2, at(z, 0, STRIP)]
            a_s[z + 1, HIGH:WIN] = above_ref[field, z // 2, at(z, 0, STRIP)]

    by_core(core_ref, load, got_ref, got2_ref)


def coefficients(rate, k_s, co_s):
    lane = lax.broadcasted_iota(jnp.int32, (WIN, LANES), 1)
    first = lane == 0
    last = lane == LANES - 1

    def layer(z, carry):
        k = k_s[z + 1]
        side = 0.5 * rate
        tall = 0.5 * rate * z_weight
        c = [
            tall * (k + k_s[z]),
            tall * (k + k_s[z + 2]),
            side * (k + pltpu.roll(k, 1, 0)),
            side * (k + pltpu.roll(k, WIN - 1, 0)),
            side * (k + jnp.where(first, 0.0, pltpu.roll(k, 1, 1))),
            side * (k + jnp.where(last, 0.0, pltpu.roll(k, LANES - 1, 1))),
        ]
        total = ((c[0] + c[1]) + (c[2] + c[3])) + (c[4] + c[5])
        d = jnp.where(k > 0.0, damping / (1.0 + total), 0.0)
        co_s[0, z] = c[0] * d
        co_s[1, z] = c[1] * d
        co_s[2, z] = c[2] * d
        co_s[3, z] = c[3] * d
        co_s[4, z] = jnp.where(first, 0.0, c[4] * d)
        co_s[5, z] = jnp.where(last, 0.0, c[5] * d)
        co_s[6, z] = d
        return carry

    lax.fori_loop(0, NZ, layer, 0)


def coefficients_body(k_ref, fine_ref, coarse_ref, k_s):
    clear_ends(k_s)
    for z in range(NZ):
        k_s[z + 1] = k_ref[z]
    coefficients(step_size, k_s, fine_ref)
    coefficients(coarse_size, k_s, coarse_ref)


def one_sweep(src, dst, co_s, db_s, rows):
    tall = rows.stop - rows.start
    under, w = src[0, rows], src[1, rows]
    for z in range(NZ):
        over = src[z + 2, rows]
        acc = (db_s[z, rows] + (1.0 - damping) * w) + (co_s[0, z, rows] * under + co_s[1, z, rows] * over)
        acc = acc + (
            co_s[2, z, rows] * pltpu.roll(w, 1, 0) + co_s[3, z, rows] * pltpu.roll(w, tall - 1, 0)
        )
        acc = acc + (
            co_s[4, z, rows] * pltpu.roll(w, 1, 1) + co_s[5, z, rows] * pltpu.roll(w, LANES - 1, 1)
        )
        dst[z + 1, rows] = acc
        under, w = w, over


def step(halo, a_s, b_s, co_s, db_s, forcing=None):
    rows = slice(8, 32) if halo <= 4 else slice(8, WIN) if halo <= 8 else slice(0, WIN)
    for z in range(NZ):
        target = a_s[z + 1, rows]
        if forcing is not None:
            target = target + step_size * forcing[z, rows]
        db_s[z, rows] = co_s[6, z, rows] * target
    one_sweep(a_s, b_s, co_s, db_s, rows)
    one_sweep(b_s, a_s, co_s, db_s, rows)


def early_body(
    core_ref, co_s, f_ref, own_ref, got_ref, got2_ref, out_ref, next_ref, a_s, b_s, db_s, f_s
):
    clear_ends(a_s, b_s)
    load_window(core_ref, a_s, 0, own_ref, got_ref, got2_ref)
    for n in range(6):
        for z in range(NZ):
            f_s[n, z] = jnp.zeros((WIN, LANES), F32)
            f_s[n, z, OWN:HIGH] = f_ref[n, z]

    def halos(below_ref, above_ref):
        for n in range(3):
            rows = 11 - 2 * n
            for z in range(NZ):
                s = z // 2
                f_s[n, z, OWN - rows : OWN] = below_ref[1 + n, s, at(z, STRIP - rows, STRIP)]
                f_s[n, z, HIGH : HIGH + rows] = above_ref[1 + n, s, at(z, 0, rows)]
                f_s[5 - n, z, OWN - STRIP + rows : OWN] = below_ref[1 + n, s, at(z, 0, STRIP - rows)]
                f_s[5 - n, z, HIGH : HIGH + STRIP - rows] = above_ref[1 + n, s, at(z, rows, STRIP)]

    by_core(core_ref, halos, got_ref, got2_ref)
    for n in range(6):
        step(12 - 2 * n, a_s, b_s, co_s, db_s, f_s.at[n])
        for z in range(NZ):
            out_ref[n, z] = a_s[z + 1, OWN:HIGH]
    for z in range(NZ):
        next_ref[0, z // 2, at(z, 0, STRIP)] = a_s[z + 1, OWN:HIGH]
        for n in range(2):
            next_ref[1 + n, z // 2, at(z, 0, STRIP)] = f_ref[6 + n, z]


def start_body(core_ref, block_ref, co_s, own_ref, got_ref, got2_ref, out_ref, a_s, b_s, db_s):
    clear_ends(a_s, b_s)
    load_window(core_ref, a_s, 0, own_ref, got_ref, got2_ref)
    step(10, a_s, b_s, co_s, db_s)
    later = block_ref[0] > 0
    for z in range(NZ):
        out_ref[z] = jnp.where(later, a_s[z + 1], 0.0)


def late_body(
    core_ref, fine_s, co_s, own_ref, got_ref, got2_ref, start_ref,
    out_ref, pow_ref, next_ref, a_s, b_s, db_s, f_s,
):
    clear_ends(a_s, b_s)
    load_window(core_ref, a_s, 0, own_ref, got_ref, got2_ref)
    for n in range(2):
        load_window(core_ref, f_s, 1 + n, own_ref, got_ref, got2_ref)
        step(12 - 2 * n, a_s, b_s, fine_s, db_s, f_s.at[pl.ds(1, NZ)])
        if n == 0:
            for z in range(NZ):
                out_ref[z] = a_s[z + 1, OWN:HIGH]
    for z in range(NZ):
        a_s[z + 1] = a_s[z + 1] - start_ref[z]
    for n in range(5):
        if n > 0:
            step(10 - 2 * n, a_s, b_s, co_s, db_s)
        for z in range(NZ):
            pow_ref[n, z] = a_s[z + 1, OWN:HIGH]
    for z in range(NZ):
        next_ref[0, z // 2, at(z, 0, STRIP)] = a_s[z + 1, OWN:HIGH]


def powers_body(
    core_ref, side_ref, block_ref, co_s, own_ref, got_ref, got2_ref, early_ref,
    out_ref, a_s, b_s, db_s, pow_s,
):
    clear_ends(a_s, b_s)
    load_window(core_ref, a_s, 0, own_ref, got_ref, got2_ref)
    for n in range(5):
        for z in range(NZ):
            pow_s[n, z] = early_ref[n, z]
    for n in range(3):
        step(6 - 2 * n, a_s, b_s, co_s, db_s)
        for z in range(NZ):
            pow_s[5 + n, z] = a_s[z + 1, OWN:HIGH]
    c = block_ref[0]
    for b in range(NB):
        power = jnp.clip(b - c, 0, NB - 1)
        live = b >= c
        for y in range(4):
            value = pow_s[power, 2 * (2 * y + side_ref[0]) + core_ref[0]]
            out_ref[b, y * STRIP : (y + 1) * STRIP] = jnp.where(live, value, 0.0)


SWEEP_SCRATCH = (
    pltpu.VMEM((NZ + 2, WIN, LANES), F32),
    pltpu.VMEM((NZ + 2, WIN, LANES), F32),
    pltpu.VMEM((NZ, WIN, LANES), F32),
)


def collect_body(core_ref, side_ref, got_ref, early_ref, late_ref, out_ref):
    for y in range(4):
        z = 2 * (2 * y + side_ref[0]) + core_ref[0]
        rows = slice(y * STRIP, (y + 1) * STRIP)
        total = got_ref[0, rows]
        for b in range(1, NB):
            total = total + got_ref[b, rows]
        out_ref[7 * 4 + y, 0:STRIP] = total
        for n in range(6):
            out_ref[n * 4 + y, 0:STRIP] = early_ref[n, z]
        out_ref[6 * 4 + y, 0:STRIP] = late_ref[z]
        for n in range(8):
            out_ref[n * 4 + y, STRIP:16] = jnp.zeros((16 - STRIP, LANES), F32)


def home_body(got_ref, out_ref):
    for zl in range(4):
        for y in range(4):
            m = chip_order(zl, y)
            for core in range(2):
                out_ref[core, m * STRIP : (m + 1) * STRIP] = got_ref[(zl * 2 + core) * 4 + y, 0:STRIP]


def on_device(guess, source, diffusivity, initial):
    guess = guess[0]
    source = source[0]
    core = lax.axis_index("core")[None]
    side = lax.axis_index("zhi")[None]
    place = lax.axis_index(("zl", "core"))[None]
    block = lax.axis_index(BLOCKS)[None]

    def onward(place):
        route = []
        for b in range(NB - 1):
            for y in range(4):
                for zhi in range(2):
                    to = zhi if b % 2 == 0 else 1 - zhi
                    route.append((((b * 8 + 7) * 4 + y) * 2 + zhi, (((b + 1) * 8 + place) * 4 + y) * 2 + to))
        return lax.ppermute(guess, AXES, route)

    prev0, prev1 = onward(0), onward(1)
    flip = ((block > 0) & (block % 2 == 0)).astype(jnp.int32)
    (base,) = call(source_body, [sds(64, 9, 2, LANES)], source)
    vmem = pl.BlockSpec(memory_space=pltpu.VMEM)
    sent = pl.pallas_call(
        extra_body,
        out_shape=sds(64, 9, 2, LANES),
        in_specs=[pl.BlockSpec(memory_space=pltpu.SMEM)] * 2 + [vmem] * 5,
        out_specs=vmem,
        input_output_aliases={6: 0},
        compiler_params=pltpu.CompilerParams(vmem_limit_bytes=32 * 1024 * 1024),
    )(place, block, prev0, prev1, diffusivity, initial, base)
    strips = lax.all_to_all(sent, BLOCK, 0, 0, tiled=True).reshape(8, 8, 9, 2, LANES)

    def swap(mine):
        return lax.ppermute(mine, "core", [(0, 1), (1, 0)])

    def exchange(mine, beside):
        got = lax.ppermute(mine, ("zl", "core", "y"), neighbour_route())
        got, beside = lax.optimization_barrier((got, beside))
        return got, swap(got), beside

    f, k, start, message = call(
        pack_body,
        [sds(8, NZ, STRIP, LANES), sds(NZ, WIN, LANES), sds(1, 8, PAIR, LANES), sds(4, 8, PAIR, LANES)],
        core, flip, strips, swap(strips), smem=2,
    )
    flops = NZ * WIN * LANES * 15
    both_rates = call(
        coefficients_body, [sds(7, NZ, WIN, LANES)] * 2, k, flops=6 * flops,
        scratch=(pltpu.VMEM((NZ + 2, WIN, LANES), F32),),
    )
    got, got2, (fine, coarse) = exchange(message, both_rates)
    v_early, state = call(
        early_body, [sds(6, NZ, STRIP, LANES), sds(3, 8, PAIR, LANES)],
        core, fine, f, start, got, got2, smem=1, flops=12 * flops,
        scratch=SWEEP_SCRATCH + (pltpu.VMEM((6, NZ, WIN, LANES), F32),),
    )
    (start_g,) = call(
        start_body, [sds(NZ, WIN, LANES)],
        core, block, coarse, start, got, got2, smem=2, flops=2 * flops, scratch=SWEEP_SCRATCH,
    )
    state_got, state_got2, start_g = exchange(state, start_g)
    v_late, first_powers, last = call(
        late_body, [sds(NZ, STRIP, LANES), sds(5, NZ, STRIP, LANES), sds(1, 8, PAIR, LANES)],
        core, fine, coarse, state, state_got, state_got2, start_g, smem=1, flops=12 * flops,
        scratch=SWEEP_SCRATCH + (pltpu.VMEM((NZ + 2, WIN, LANES), F32),),
    )
    last_got, last_got2, _ = exchange(last, ())
    (powers,) = call(
        powers_body, [sds(NB, 4 * STRIP, LANES)],
        core, side, block, coarse, last, last_got, last_got2, first_powers, smem=3, flops=6 * flops,
        scratch=SWEEP_SCRATCH + (pltpu.VMEM((NB, NZ, STRIP, LANES), F32),),
    )
    arrived = lax.all_to_all(powers, BLOCKS, 0, 0, tiled=True)
    (back,) = call(collect_body, [sds(32, 16, LANES)], core, side, arrived, v_early, v_late, smem=2)
    returned = lax.all_to_all(back, ("zl", "core", "y"), 0, 0, tiled=True)
    (result,) = call(home_body, [sds(2, NY, LANES)], returned)
    return result[None]


def solution(mesh):
    fine = Mesh(mesh.devices.reshape(SIZES), AXES)
    tm = ("x", "zh", "zl", "core")
    space = ("y", "zhi")
    in_specs = (P(tm, space, None, None), P(tm, space, None, None), P(space, None, None), P(space, None, None))
    out_specs = P(tm, space, None, None)
    return jax.shard_map(on_device, mesh=fine, in_specs=in_specs, out_specs=out_specs, check_vma=False)
```

```python
import functools

import jax
import jax.numpy as jnp
from jax import lax
from jax.experimental import pallas as pl
from jax.experimental.pallas import tpu as pltpu
from jax.sharding import Mesh, PartitionSpec as P

F32 = jnp.float32

damping = 0.8
step_size = 0.5
coarse_size = 4.0
z_weight = 8.0

AXES = ("x", "zh", "zl", "core", "y", "zhi")
SIZES = (4, 2, 4, 2, 4, 2)
BLOCK = ("zl", "core", "y", "zhi")
BLOCKS = ("x", "zh")
NB = 8
NZ = 16
NY = 192
CHIPS = 16
STRIP = NY // CHIPS
PAIR = 2 * STRIP
LANES = 128
LOW, OWN, HIGH, WIN = 4, 16, 28, 40


def chip_order(zl, y):
    return zl * 4 + (y if zl % 2 == 0 else 3 - y)


def neighbour_route():
    place = {chip_order(zl, y): (zl, y) for zl in range(4) for y in range(4)}
    route = []
    for core, step in ((0, 1), (1, -1)):
        for m in range(CHIPS):
            if 0 <= m + step < CHIPS:
                (zl, y), (to_zl, to_y) = place[m], place[m + step]
                route.append(((zl * 2 + core) * 4 + y, (to_zl * 2 + core) * 4 + to_y))
    return route


def at(z, first, last):
    return slice((z % 2) * STRIP + first, (z % 2) * STRIP + last)


def call(body, outs, *args, scratch=(), smem=0, flops=0):
    specs = [pl.BlockSpec(memory_space=pltpu.SMEM)] * smem
    specs += [pl.BlockSpec(memory_space=pltpu.VMEM)] * (len(args) - smem)
    out_specs = [pl.BlockSpec(memory_space=pltpu.VMEM)] * len(outs)
    size = sum(4 * a.size for a in args) + sum(4 * o.size for o in outs)
    return pl.pallas_call(
        body,
        out_shape=list(outs),
        in_specs=specs,
        out_specs=out_specs,
        scratch_shapes=list(scratch),
        compiler_params=pltpu.CompilerParams(vmem_limit_bytes=12 * 1024 * 1024),
        cost_estimate=pl.CostEstimate(flops=flops, bytes_accessed=size, transcendentals=0),
    )(*args)


def sds(*shape):
    return jax.ShapeDtypeStruct(shape, F32)


def targets():
    for zl in range(4):
        for y in range(4):
            for zhi in range(2):
                for core in range(2):
                    yield ((zl * 2 + core) * 4 + y) * 2 + zhi, core, chip_order(zl, y)


def halves_body(guess_ref, half0_ref, half1_ref):
    for core in range(2):
        for m in range(CHIPS):
            for r in range(3):
                row = m * STRIP + 2 * r
                half0_ref[core, m, r] = guess_ref[core, row : row + 2]
                half1_ref[core, m, r] = guess_ref[core, row + 6 : row + 8]


def home_fields_body(j_ref, src_ref, cond_ref, init_ref, out_ref):
    place = j_ref[0]
    for to, core, m in targets():
        for r in range(6):
            row = m * STRIP + 2 * r
            out_ref[to, r] = src_ref[core, row : row + 2]

    def fill(ref, shift, half):
        for to, core, m in targets():
            m = m + shift
            for r in range(3):
                row = m * STRIP + 6 * half + 2 * r
                if 0 <= m < CHIPS:
                    out_ref[to, 6 + r] = ref[core, row : row + 2]
                else:
                    out_ref[to, 6 + r] = jnp.zeros((2, LANES), F32)

    for half in range(2):
        pl.when(place == half)(functools.partial(fill, init_ref, 0, half))
        for n, shift in enumerate((0, 1, -1)):
            pl.when(place == 2 + 2 * n + half)(functools.partial(fill, cond_ref, shift, half))


def previous_body(j_ref, block_ref, prev0_ref, prev1_ref, base_ref, out_ref):
    for half, prev_ref in ((0, prev0_ref), (1, prev1_ref)):

        @pl.when((j_ref[0] == half) & (block_ref[0] > 0))
        def _(prev_ref=prev_ref):
            for to, core, m in targets():
                for r in range(3):
                    out_ref[to, 6 + r] = prev_ref[core, m, r]


def by_core(core_ref, body, mine, other):
    pl.when(core_ref[0] == 0)(functools.partial(body, mine, other))
    pl.when(core_ref[0] == 1)(functools.partial(body, other, mine))


def pack_body(core_ref, flip_ref, own_ref, other_ref, f_ref, k_ref, start_ref, out_ref):
    flip = flip_ref[0]

    def order(*halves):
        for z in range(NZ):
            half, s = halves[z % 2], z // 2
            k_ref[z, 0:LOW] = jnp.zeros((LOW, LANES), F32)
            for r in range(6):
                for n in range(8):
                    f_ref[n, z, 2 * r : 2 * r + 2] = half[n, s, r]
                part, extra = r // 3, 6 + r % 3
                start = half[part, s + (1 - 2 * (s % 2)) * flip, extra]
                start_ref[0, s, at(z, 2 * r, 2 * r + 2)] = start
                out_ref[0, s, at(z, 2 * r, 2 * r + 2)] = start
                for place, base in ((6, LOW), (2, OWN), (4, HIGH)):
                    k_ref[z, base + 2 * r : base + 2 * r + 2] = half[place + part, s, extra]

    by_core(core_ref, order, own_ref, other_ref)

    @pl.when(core_ref[0] == 0)
    def _():
        for z in range(NZ):
            for n in range(3):
                rows = 11 - 2 * n
                out_ref[1 + n, z // 2, at(z, STRIP - rows, STRIP)] = f_ref[n, z, STRIP - rows : STRIP]
                out_ref[1 + n, z // 2, at(z, 0, STRIP - rows)] = f_ref[5 - n, z, rows:STRIP]

    @pl.when(core_ref[0] == 1)
    def _():
        for z in range(NZ):
            for n in range(3):
                rows = 11 - 2 * n
                out_ref[1 + n, z // 2, at(z, 0, rows)] = f_ref[n, z, 0:rows]
                out_ref[1 + n, z // 2, at(z, rows, STRIP)] = f_ref[5 - n, z, 0 : STRIP - rows]


def clear_ends(*refs):
    zero = jnp.zeros((WIN, LANES), F32)
    for ref in refs:
        ref[0] = zero
        ref[NZ + 1] = zero


def load_window(core_ref, a_s, field, own_ref, got_ref, got2_ref):
    def load(below_ref, above_ref):
        zero = jnp.zeros((LOW, LANES), F32)
        for z in range(NZ):
            a_s[z + 1, 0:LOW] = zero
            a_s[z + 1, LOW:OWN] = below_ref[field, z // 2, at(z, 0, STRIP)]
            a_s[z + 1, OWN:HIGH] = own_ref[field, z // 2, at(z, 0, STRIP)]
            a_s[z + 1, HIGH:WIN] = above_ref[field, z // 2, at(z, 0, STRIP)]

    by_core(core_ref, load, got_ref, got2_ref)


def coefficients(rate, k_s, co_s):
    lane = lax.broadcasted_iota(jnp.int32, (WIN, LANES), 1)
    first = lane == 0
    last = lane == LANES - 1

    def layer(z, carry):
        k = k_s[z + 1]
        side = 0.5 * rate
        tall = 0.5 * rate * z_weight
        c = [
            tall * (k + k_s[z]),
            tall * (k + k_s[z + 2]),
            side * (k + pltpu.roll(k, 1, 0)),
            side * (k + pltpu.roll(k, WIN - 1, 0)),
            side * (k + jnp.where(first, 0.0, pltpu.roll(k, 1, 1))),
            side * (k + jnp.where(last, 0.0, pltpu.roll(k, LANES - 1, 1))),
        ]
        total = ((c[0] + c[1]) + (c[2] + c[3])) + (c[4] + c[5])
        d = jnp.where(k > 0.0, damping / (1.0 + total), 0.0)
        co_s[0, z] = c[0] * d
        co_s[1, z] = c[1] * d
        co_s[2, z] = c[2] * d
        co_s[3, z] = c[3] * d
        co_s[4, z] = jnp.where(first, 0.0, c[4] * d)
        co_s[5, z] = jnp.where(last, 0.0, c[5] * d)
        co_s[6, z] = d
        return carry

    lax.fori_loop(0, NZ, layer, 0)


def coefficients_body(k_ref, fine_ref, coarse_ref, k_s):
    clear_ends(k_s)
    for z in range(NZ):
        k_s[z + 1] = k_ref[z]
    coefficients(step_size, k_s, fine_ref)
    coefficients(coarse_size, k_s, coarse_ref)


def one_sweep(src, dst, co_s, db_s, rows):
    tall = rows.stop - rows.start
    under, w = src[0, rows], src[1, rows]
    for z in range(NZ):
        over = src[z + 2, rows]
        acc = (db_s[z, rows] + (1.0 - damping) * w) + (co_s[0, z, rows] * under + co_s[1, z, rows] * over)
        acc = acc + (
            co_s[2, z, rows] * pltpu.roll(w, 1, 0) + co_s[3, z, rows] * pltpu.roll(w, tall - 1, 0)
        )
        acc = acc + (
            co_s[4, z, rows] * pltpu.roll(w, 1, 1) + co_s[5, z, rows] * pltpu.roll(w, LANES - 1, 1)
        )
        dst[z + 1, rows] = acc
        under, w = w, over


def step(halo, a_s, b_s, co_s, db_s, forcing=None):
    rows = slice(8, 32) if halo <= 4 else slice(8, WIN) if halo <= 8 else slice(0, WIN)
    for z in range(NZ):
        target = a_s[z + 1, rows]
        if forcing is not None:
            target = target + step_size * forcing[z, rows]
        db_s[z, rows] = co_s[6, z, rows] * target
    one_sweep(a_s, b_s, co_s, db_s, rows)
    one_sweep(b_s, a_s, co_s, db_s, rows)


def early_body(
    core_ref, co_s, f_ref, own_ref, got_ref, got2_ref, out_ref, next_ref, a_s, b_s, db_s, f_s
):
    clear_ends(a_s, b_s)
    load_window(core_ref, a_s, 0, own_ref, got_ref, got2_ref)
    for n in range(6):
        for z in range(NZ):
            f_s[n, z] = jnp.zeros((WIN, LANES), F32)
            f_s[n, z, OWN:HIGH] = f_ref[n, z]

    def halos(below_ref, above_ref):
        for n in range(3):
            rows = 11 - 2 * n
            for z in range(NZ):
                s = z // 2
                f_s[n, z, OWN - rows : OWN] = below_ref[1 + n, s, at(z, STRIP - rows, STRIP)]
                f_s[n, z, HIGH : HIGH + rows] = above_ref[1 + n, s, at(z, 0, rows)]
                f_s[5 - n, z, OWN - STRIP + rows : OWN] = below_ref[1 + n, s, at(z, 0, STRIP - rows)]
                f_s[5 - n, z, HIGH : HIGH + STRIP - rows] = above_ref[1 + n, s, at(z, rows, STRIP)]

    by_core(core_ref, halos, got_ref, got2_ref)
    for n in range(6):
        step(12 - 2 * n, a_s, b_s, co_s, db_s, f_s.at[n])
        for z in range(NZ):
            out_ref[n, z] = a_s[z + 1, OWN:HIGH]
    for z in range(NZ):
        next_ref[0, z // 2, at(z, 0, STRIP)] = a_s[z + 1, OWN:HIGH]
        for n in range(2):
            next_ref[1 + n, z // 2, at(z, 0, STRIP)] = f_ref[6 + n, z]


def start_body(core_ref, block_ref, co_s, own_ref, got_ref, got2_ref, out_ref, a_s, b_s, db_s):
    clear_ends(a_s, b_s)
    load_window(core_ref, a_s, 0, own_ref, got_ref, got2_ref)
    step(10, a_s, b_s, co_s, db_s)
    later = block_ref[0] > 0
    for z in range(NZ):
        out_ref[z] = jnp.where(later, a_s[z + 1], 0.0)


def late_body(
    core_ref, fine_s, co_s, own_ref, got_ref, got2_ref, start_ref,
    out_ref, pow_ref, next_ref, a_s, b_s, db_s, f_s,
):
    clear_ends(a_s, b_s)
    load_window(core_ref, a_s, 0, own_ref, got_ref, got2_ref)
    for n in range(2):
        load_window(core_ref, f_s, 1 + n, own_ref, got_ref, got2_ref)
        step(12 - 2 * n, a_s, b_s, fine_s, db_s, f_s.at[pl.ds(1, NZ)])
        if n == 0:
            for z in range(NZ):
                out_ref[z] = a_s[z + 1, OWN:HIGH]
    for z in range(NZ):
        a_s[z + 1] = a_s[z + 1] - start_ref[z]
    for n in range(5):
        if n > 0:
            step(10 - 2 * n, a_s, b_s, co_s, db_s)
        for z in range(NZ):
            pow_ref[n, z] = a_s[z + 1, OWN:HIGH]
    for z in range(NZ):
        next_ref[0, z // 2, at(z, 0, STRIP)] = a_s[z + 1, OWN:HIGH]


def powers_body(
    core_ref, side_ref, block_ref, co_s, own_ref, got_ref, got2_ref, early_ref,
    out_ref, a_s, b_s, db_s, pow_s,
):
    clear_ends(a_s, b_s)
    load_window(core_ref, a_s, 0, own_ref, got_ref, got2_ref)
    for n in range(5):
        for z in range(NZ):
            pow_s[n, z] = early_ref[n, z]
    for n in range(3):
        step(6 - 2 * n, a_s, b_s, co_s, db_s)
        for z in range(NZ):
            pow_s[5 + n, z] = a_s[z + 1, OWN:HIGH]
    c = block_ref[0]
    for b in range(NB):
        power = jnp.clip(b - c, 0, NB - 1)
        live = b >= c
        for y in range(4):
            value = pow_s[power, 2 * (2 * y + side_ref[0]) + core_ref[0]]
            out_ref[b, y * STRIP : (y + 1) * STRIP] = jnp.where(live, value, 0.0)


SWEEP_SCRATCH = (
    pltpu.VMEM((NZ + 2, WIN, LANES), F32),
    pltpu.VMEM((NZ + 2, WIN, LANES), F32),
    pltpu.VMEM((NZ, WIN, LANES), F32),
)


def collect_body(core_ref, side_ref, got_ref, early_ref, late_ref, out_ref):
    for y in range(4):
        z = 2 * (2 * y + side_ref[0]) + core_ref[0]
        rows = slice(y * STRIP, (y + 1) * STRIP)
        total = got_ref[0, rows]
        for b in range(1, NB):
            total = total + got_ref[b, rows]
        out_ref[7 * 4 + y, 0:STRIP] = total
        for n in range(6):
            out_ref[n * 4 + y, 0:STRIP] = early_ref[n, z]
        out_ref[6 * 4 + y, 0:STRIP] = late_ref[z]
        for n in range(8):
            out_ref[n * 4 + y, STRIP:16] = jnp.zeros((16 - STRIP, LANES), F32)


def home_body(got_ref, out_ref):
    for zl in range(4):
        for y in range(4):
            m = chip_order(zl, y)
            for core in range(2):
                out_ref[core, m * STRIP : (m + 1) * STRIP] = got_ref[(zl * 2 + core) * 4 + y, 0:STRIP]


def on_device(guess, source, diffusivity, initial):
    guess = guess[0]
    source = source[0]
    core = lax.axis_index("core")[None]
    side = lax.axis_index("zhi")[None]
    place = lax.axis_index(("zl", "core"))[None]
    block = lax.axis_index(BLOCKS)[None]

    def onward(mine, place):
        route = []
        for b in range(NB - 1):
            for y in range(4):
                for zhi in range(2):
                    to = zhi if b % 2 == 0 else 1 - zhi
                    route.append((((b * 8 + 7) * 4 + y) * 2 + zhi, (((b + 1) * 8 + place) * 4 + y) * 2 + to))
        return lax.ppermute(mine, AXES, route)

    half0, half1 = call(halves_body, [sds(2, CHIPS, 3, 2, LANES)] * 2, guess)
    prev0, prev1 = onward(half0, 0), onward(half1, 1)
    flip = ((block > 0) & (block % 2 == 0)).astype(jnp.int32)
    (base,) = call(home_fields_body, [sds(64, 9, 2, LANES)], place, source, diffusivity, initial, smem=1)
    vmem = pl.BlockSpec(memory_space=pltpu.VMEM)
    sent = pl.pallas_call(
        previous_body,
        out_shape=sds(64, 9, 2, LANES),
        in_specs=[pl.BlockSpec(memory_space=pltpu.SMEM)] * 2 + [vmem] * 3,
        out_specs=vmem,
        input_output_aliases={4: 0},
        compiler_params=pltpu.CompilerParams(vmem_limit_bytes=12 * 1024 * 1024),
    )(place, block, prev0, prev1, base)
    strips = lax.all_to_all(sent, BLOCK, 0, 0, tiled=True).reshape(8, 8, 9, 2, LANES)

    def swap(mine):
        return lax.ppermute(mine, "core", [(0, 1), (1, 0)])

    def exchange(mine, beside):
        got = lax.ppermute(mine, ("zl", "core", "y"), neighbour_route())
        got, beside = lax.optimization_barrier((got, beside))
        return got, swap(got), beside

    f, k, start, message = call(
        pack_body,
        [sds(8, NZ, STRIP, LANES), sds(NZ, WIN, LANES), sds(1, 8, PAIR, LANES), sds(4, 8, PAIR, LANES)],
        core, flip, strips, swap(strips), smem=2,
    )
    flops = NZ * WIN * LANES * 15
    both_rates = call(
        coefficients_body, [sds(7, NZ, WIN, LANES)] * 2, k, flops=6 * flops,
        scratch=(pltpu.VMEM((NZ + 2, WIN, LANES), F32),),
    )
    got, got2, (fine, coarse) = exchange(message, both_rates)
    v_early, state = call(
        early_body, [sds(6, NZ, STRIP, LANES), sds(3, 8, PAIR, LANES)],
        core, fine, f, start, got, got2, smem=1, flops=12 * flops,
        scratch=SWEEP_SCRATCH + (pltpu.VMEM((6, NZ, WIN, LANES), F32),),
    )
    (start_g,) = call(
        start_body, [sds(NZ, WIN, LANES)],
        core, block, coarse, start, got, got2, smem=2, flops=2 * flops, scratch=SWEEP_SCRATCH,
    )
    state_got, state_got2, start_g = exchange(state, start_g)
    v_late, first_powers, last = call(
        late_body, [sds(NZ, STRIP, LANES), sds(5, NZ, STRIP, LANES), sds(1, 8, PAIR, LANES)],
        core, fine, coarse, state, state_got, state_got2, start_g, smem=1, flops=12 * flops,
        scratch=SWEEP_SCRATCH + (pltpu.VMEM((NZ + 2, WIN, LANES), F32),),
    )
    last_got, last_got2, _ = exchange(last, ())
    (powers,) = call(
        powers_body, [sds(NB, 4 * STRIP, LANES)],
        core, side, block, coarse, last, last_got, last_got2, first_powers, smem=3, flops=6 * flops,
        scratch=SWEEP_SCRATCH + (pltpu.VMEM((NB, NZ, STRIP, LANES), F32),),
    )
    arrived = lax.all_to_all(powers, BLOCKS, 0, 0, tiled=True)
    (back,) = call(collect_body, [sds(32, 16, LANES)], core, side, arrived, v_early, v_late, smem=2)
    returned = lax.all_to_all(back, ("zl", "core", "y"), 0, 0, tiled=True)
    (result,) = call(home_body, [sds(2, NY, LANES)], returned)
    return result[None]


def solution(mesh):
    fine = Mesh(mesh.devices.reshape(SIZES), AXES)
    tm = ("x", "zh", "zl", "core")
    space = ("y", "zhi")
    in_specs = (P(tm, space, None, None), P(tm, space, None, None), P(space, None, None), P(space, None, None))
    out_specs = P(tm, space, None, None)
    return jax.shard_map(on_device, mesh=fine, in_specs=in_specs, out_specs=out_specs, check_vma=False)
```

```python
import functools

import jax
import jax.numpy as jnp
from jax import lax
from jax.experimental import pallas as pl
from jax.experimental.pallas import tpu as pltpu
from jax.sharding import Mesh, PartitionSpec as P

F32 = jnp.float32

damping = 0.8
step_size = 0.5
coarse_size = 4.0
z_weight = 8.0

AXES = ("x", "zh", "zl", "core", "y", "zhi")
SIZES = (4, 2, 4, 2, 4, 2)
BLOCK = ("zl", "core", "y", "zhi")
BLOCKS = ("x", "zh")
NB = 8
NZ = 16
NY = 192
CHIPS = 16
STRIP = NY // CHIPS
PAIR = 2 * STRIP
HALF = STRIP // 2
LANES = 128
LAYERS = [(y, p) for y in range(4) for p in range(2)]
LOW, OWN, HIGH, WIN = 4, 16, 28, 40


def chip_order(zl, y):
    return zl * 4 + (y if zl % 2 == 0 else 3 - y)


def neighbour_route():
    place = {chip_order(zl, y): (zl, y) for zl in range(4) for y in range(4)}
    route = []
    for core, step in ((0, 1), (1, -1)):
        for m in range(CHIPS):
            if 0 <= m + step < CHIPS:
                (zl, y), (to_zl, to_y) = place[m], place[m + step]
                route.append(((zl * 2 + core) * 4 + y, (to_zl * 2 + core) * 4 + to_y))
    return route


def at(z, first, last):
    return slice((z % 2) * STRIP + first, (z % 2) * STRIP + last)


def call(body, outs, *args, scratch=(), smem=0, flops=0):
    specs = [pl.BlockSpec(memory_space=pltpu.SMEM)] * smem
    specs += [pl.BlockSpec(memory_space=pltpu.VMEM)] * (len(args) - smem)
    out_specs = [pl.BlockSpec(memory_space=pltpu.VMEM)] * len(outs)
    size = sum(4 * a.size for a in args) + sum(4 * o.size for o in outs)
    return pl.pallas_call(
        body,
        out_shape=list(outs),
        in_specs=specs,
        out_specs=out_specs,
        scratch_shapes=list(scratch),
        compiler_params=pltpu.CompilerParams(vmem_limit_bytes=12 * 1024 * 1024),
        cost_estimate=pl.CostEstimate(flops=flops, bytes_accessed=size, transcendentals=0),
    )(*args)


def sds(*shape):
    return jax.ShapeDtypeStruct(shape, F32)


def targets():
    for zl in range(4):
        for y in range(4):
            for zhi in range(2):
                for core in range(2):
                    yield ((zl * 2 + core) * 4 + y) * 2 + zhi, core, chip_order(zl, y)


def halves_body(guess_ref, half0_ref, half1_ref):
    for core in range(2):
        for m in range(CHIPS):
            for r in range(3):
                row = m * STRIP + 2 * r
                half0_ref[core, m, r] = guess_ref[core, row : row + 2]
                half1_ref[core, m, r] = guess_ref[core, row + 6 : row + 8]


def home_fields_body(j_ref, src_ref, cond_ref, init_ref, out_ref):
    place = j_ref[0]
    for to, core, m in targets():
        for r in range(6):
            row = m * STRIP + 2 * r
            out_ref[to, r] = src_ref[core, row : row + 2]

    def fill(ref, shift, half):
        for to, core, m in targets():
            m = m + shift
            for r in range(3):
                row = m * STRIP + 6 * half + 2 * r
                if 0 <= m < CHIPS:
                    out_ref[to, 6 + r] = ref[core, row : row + 2]
                else:
                    out_ref[to, 6 + r] = jnp.zeros((2, LANES), F32)

    for half in range(2):
        pl.when(place == half)(functools.partial(fill, init_ref, 0, half))
        for n, shift in enumerate((0, 1, -1)):
            pl.when(place == 2 + 2 * n + half)(functools.partial(fill, cond_ref, shift, half))


def previous_body(j_ref, block_ref, prev0_ref, prev1_ref, base_ref, out_ref):
    for half, prev_ref in ((0, prev0_ref), (1, prev1_ref)):

        @pl.when((j_ref[0] == half) & (block_ref[0] > 0))
        def _(prev_ref=prev_ref):
            for to, core, m in targets():
                for r in range(3):
                    out_ref[to, 6 + r] = prev_ref[core, m, r]


def by_core(core_ref, body, mine, other):
    pl.when(core_ref[0] == 0)(functools.partial(body, mine, other))
    pl.when(core_ref[0] == 1)(functools.partial(body, other, mine))


def pack_body(core_ref, flip_ref, own_ref, other_ref, f_ref, k_ref, start_ref, out_ref):
    flip = flip_ref[0]

    def order(*halves):
        for z in range(NZ):
            half, s = halves[z % 2], z // 2
            k_ref[z, 0:LOW] = jnp.zeros((LOW, LANES), F32)
            for r in range(6):
                for n in range(8):
                    f_ref[n, z, 2 * r : 2 * r + 2] = half[n, s, r]
                part, extra = r // 3, 6 + r % 3
                start = half[part, s + (1 - 2 * (s % 2)) * flip, extra]
                start_ref[0, s, at(z, 2 * r, 2 * r + 2)] = start
                out_ref[0, s, at(z, 2 * r, 2 * r + 2)] = start
                for place, base in ((6, LOW), (2, OWN), (4, HIGH)):
                    k_ref[z, base + 2 * r : base + 2 * r + 2] = half[place + part, s, extra]

    by_core(core_ref, order, own_ref, other_ref)

    @pl.when(core_ref[0] == 0)
    def _():
        for z in range(NZ):
            for n in range(3):
                rows = 11 - 2 * n
                out_ref[1 + n, z // 2, at(z, STRIP - rows, STRIP)] = f_ref[n, z, STRIP - rows : STRIP]
                out_ref[1 + n, z // 2, at(z, 0, STRIP - rows)] = f_ref[5 - n, z, rows:STRIP]

    @pl.when(core_ref[0] == 1)
    def _():
        for z in range(NZ):
            for n in range(3):
                rows = 11 - 2 * n
                out_ref[1 + n, z // 2, at(z, 0, rows)] = f_ref[n, z, 0:rows]
                out_ref[1 + n, z // 2, at(z, rows, STRIP)] = f_ref[5 - n, z, 0 : STRIP - rows]


def clear_ends(*refs):
    zero = jnp.zeros((WIN, LANES), F32)
    for ref in refs:
        ref[0] = zero
        ref[NZ + 1] = zero


def load_window(core_ref, a_s, field, own_ref, got_ref, got2_ref):
    def load(below_ref, above_ref):
        zero = jnp.zeros((LOW, LANES), F32)
        for z in range(NZ):
            a_s[z + 1, 0:LOW] = zero
            a_s[z + 1, LOW:OWN] = below_ref[field, z // 2, at(z, 0, STRIP)]
            a_s[z + 1, OWN:HIGH] = own_ref[field, z // 2, at(z, 0, STRIP)]
            a_s[z + 1, HIGH:WIN] = above_ref[field, z // 2, at(z, 0, STRIP)]

    by_core(core_ref, load, got_ref, got2_ref)


def coefficients(rate, k_s, co_s):
    lane = lax.broadcasted_iota(jnp.int32, (WIN, LANES), 1)
    first = lane == 0
    last = lane == LANES - 1

    def layer(z, carry):
        k = k_s[z + 1]
        side = 0.5 * rate
        tall = 0.5 * rate * z_weight
        c = [
            tall * (k + k_s[z]),
            tall * (k + k_s[z + 2]),
            side * (k + pltpu.roll(k, 1, 0)),
            side * (k + pltpu.roll(k, WIN - 1, 0)),
            side * (k + jnp.where(first, 0.0, pltpu.roll(k, 1, 1))),
            side * (k + jnp.where(last, 0.0, pltpu.roll(k, LANES - 1, 1))),
        ]
        total = ((c[0] + c[1]) + (c[2] + c[3])) + (c[4] + c[5])
        d = jnp.where(k > 0.0, damping / (1.0 + total), 0.0)
        co_s[0, z] = c[0] * d
        co_s[1, z] = c[1] * d
        co_s[2, z] = c[2] * d
        co_s[3, z] = c[3] * d
        co_s[4, z] = jnp.where(first, 0.0, c[4] * d)
        co_s[5, z] = jnp.where(last, 0.0, c[5] * d)
        co_s[6, z] = d
        return carry

    lax.fori_loop(0, NZ, layer, 0)


def coefficients_body(k_ref, fine_ref, coarse_ref, k_s):
    clear_ends(k_s)
    for z in range(NZ):
        k_s[z + 1] = k_ref[z]
    coefficients(step_size, k_s, fine_ref)
    coefficients(coarse_size, k_s, coarse_ref)


def one_sweep(src, dst, co_s, db_s, rows):
    tall = rows.stop - rows.start
    under, w = src[0, rows], src[1, rows]
    for z in range(NZ):
        over = src[z + 2, rows]
        acc = (db_s[z, rows] + (1.0 - damping) * w) + (co_s[0, z, rows] * under + co_s[1, z, rows] * over)
        acc = acc + (
            co_s[2, z, rows] * pltpu.roll(w, 1, 0) + co_s[3, z, rows] * pltpu.roll(w, tall - 1, 0)
        )
        acc = acc + (
            co_s[4, z, rows] * pltpu.roll(w, 1, 1) + co_s[5, z, rows] * pltpu.roll(w, LANES - 1, 1)
        )
        dst[z + 1, rows] = acc
        under, w = w, over


def step(halo, a_s, b_s, co_s, db_s, forcing=None):
    rows = slice(8, 32) if halo <= 4 else slice(8, WIN) if halo <= 8 else slice(0, WIN)
    for z in range(NZ):
        target = a_s[z + 1, rows]
        if forcing is not None:
            target = target + step_size * forcing[z, rows]
        db_s[z, rows] = co_s[6, z, rows] * target
    one_sweep(a_s, b_s, co_s, db_s, rows)
    one_sweep(b_s, a_s, co_s, db_s, rows)


def early_body(
    core_ref, co_s, f_ref, own_ref, got_ref, got2_ref, out_ref, next_ref, a_s, b_s, db_s, f_s
):
    clear_ends(a_s, b_s)
    load_window(core_ref, a_s, 0, own_ref, got_ref, got2_ref)
    for n in range(6):
        for z in range(NZ):
            f_s[n, z] = jnp.zeros((WIN, LANES), F32)
            f_s[n, z, OWN:HIGH] = f_ref[n, z]

    def halos(below_ref, above_ref):
        for n in range(3):
            rows = 11 - 2 * n
            for z in range(NZ):
                s = z // 2
                f_s[n, z, OWN - rows : OWN] = below_ref[1 + n, s, at(z, STRIP - rows, STRIP)]
                f_s[n, z, HIGH : HIGH + rows] = above_ref[1 + n, s, at(z, 0, rows)]
                f_s[5 - n, z, OWN - STRIP + rows : OWN] = below_ref[1 + n, s, at(z, 0, STRIP - rows)]
                f_s[5 - n, z, HIGH : HIGH + STRIP - rows] = above_ref[1 + n, s, at(z, rows, STRIP)]

    by_core(core_ref, halos, got_ref, got2_ref)
    for n in range(6):
        step(12 - 2 * n, a_s, b_s, co_s, db_s, f_s.at[n])
        for z in range(NZ):
            out_ref[n, z] = a_s[z + 1, OWN:HIGH]
    for z in range(NZ):
        next_ref[0, z // 2, at(z, 0, STRIP)] = a_s[z + 1, OWN:HIGH]
        for n in range(2):
            next_ref[1 + n, z // 2, at(z, 0, STRIP)] = f_ref[6 + n, z]


def start_body(core_ref, block_ref, co_s, own_ref, got_ref, got2_ref, out_ref, a_s, b_s, db_s):
    clear_ends(a_s, b_s)
    load_window(core_ref, a_s, 0, own_ref, got_ref, got2_ref)
    step(10, a_s, b_s, co_s, db_s)
    later = block_ref[0] > 0
    for z in range(NZ):
        out_ref[z] = jnp.where(later, a_s[z + 1], 0.0)


def late_body(
    core_ref, fine_s, co_s, own_ref, got_ref, got2_ref, start_ref,
    out_ref, pow_ref, next_ref, a_s, b_s, db_s, f_s,
):
    clear_ends(a_s, b_s)
    load_window(core_ref, a_s, 0, own_ref, got_ref, got2_ref)
    for n in range(2):
        load_window(core_ref, f_s, 1 + n, own_ref, got_ref, got2_ref)
        step(12 - 2 * n, a_s, b_s, fine_s, db_s, f_s.at[pl.ds(1, NZ)])
        if n == 0:
            for z in range(NZ):
                out_ref[z] = a_s[z + 1, OWN:HIGH]
    for z in range(NZ):
        a_s[z + 1] = a_s[z + 1] - start_ref[z]
    for n in range(5):
        if n > 0:
            step(10 - 2 * n, a_s, b_s, co_s, db_s)
        for z in range(NZ):
            pow_ref[n, z] = a_s[z + 1, OWN:HIGH]
    for z in range(NZ):
        next_ref[0, z // 2, at(z, 0, STRIP)] = a_s[z + 1, OWN:HIGH]


def powers_body(
    core_ref, side_ref, block_ref, co_s, own_ref, got_ref, early_ref, out_ref, a_s, b_s, db_s, pow_s
):
    clear_ends(a_s, b_s)
    for z in range(NZ):
        a_s[z + 1] = jnp.zeros((WIN, LANES), F32)
        a_s[z + 1, OWN:HIGH] = own_ref[0, z // 2, at(z, 0, STRIP)]

    def halo(rows):
        for z in range(NZ):
            a_s[z + 1, rows] = got_ref[0, z // 2, at(z, 0, STRIP)]

    pl.when(core_ref[0] == 0)(functools.partial(halo, slice(LOW, OWN)))
    pl.when(core_ref[0] == 1)(functools.partial(halo, slice(HIGH, WIN)))
    for n in range(5):
        for z in range(NZ):
            pow_s[n, z] = early_ref[n, z]
    for n in range(3):
        step(6 - 2 * n, a_s, b_s, co_s, db_s)
        for z in range(NZ):
            pow_s[5 + n, z] = a_s[z + 1, OWN:HIGH]
    c = block_ref[0]

    def send(rows):
        for b in range(NB):
            power = jnp.clip(b - c, 0, NB - 1)
            live = b >= c
            for n, (y, p) in enumerate(LAYERS):
                value = pow_s[power, 2 * (2 * y + side_ref[0]) + p, rows]
                out_ref[b, n * HALF : (n + 1) * HALF] = jnp.where(live, value, 0.0)

    for core in range(2):
        pl.when(core_ref[0] == core)(functools.partial(send, slice(core * HALF, (core + 1) * HALF)))


SWEEP_SCRATCH = (
    pltpu.VMEM((NZ + 2, WIN, LANES), F32),
    pltpu.VMEM((NZ + 2, WIN, LANES), F32),
    pltpu.VMEM((NZ, WIN, LANES), F32),
)


def collect_body(core_ref, side_ref, got_ref, early_ref, late_ref, out_ref):
    def fill(rows):
        for n, (y, p) in enumerate(LAYERS):
            z = 2 * (2 * y + side_ref[0]) + p
            mine, to = slice(n * HALF, (n + 1) * HALF), slice(p * HALF, (p + 1) * HALF)
            total = got_ref[0, mine]
            for b in range(1, NB):
                total = total + got_ref[b, mine]
            out_ref[7 * 4 + y, to] = total
            for t in range(6):
                out_ref[t * 4 + y, to] = early_ref[t, z, rows]
            out_ref[6 * 4 + y, to] = late_ref[z, rows]

    for core in range(2):
        pl.when(core_ref[0] == core)(functools.partial(fill, slice(core * HALF, (core + 1) * HALF)))
    for n in range(32):
        out_ref[n, STRIP:16] = jnp.zeros((16 - STRIP, LANES), F32)


def home_body(got_ref, out_ref):
    for zl in range(4):
        for y in range(4):
            for core in range(2):
                row = chip_order(zl, y) * STRIP + core * HALF
                for p in range(2):
                    out_ref[p, row : row + HALF] = got_ref[(zl * 2 + core) * 4 + y, p * HALF : (p + 1) * HALF]


def on_device(guess, source, diffusivity, initial):
    guess = guess[0]
    source = source[0]
    core = lax.axis_index("core")[None]
    side = lax.axis_index("zhi")[None]
    place = lax.axis_index(("zl", "core"))[None]
    block = lax.axis_index(BLOCKS)[None]

    def onward(mine, place):
        route = []
        for b in range(NB - 1):
            for y in range(4):
                for zhi in range(2):
                    to = zhi if b % 2 == 0 else 1 - zhi
                    route.append((((b * 8 + 7) * 4 + y) * 2 + zhi, (((b + 1) * 8 + place) * 4 + y) * 2 + to))
        return lax.ppermute(mine, AXES, route)

    half0, half1 = call(halves_body, [sds(2, CHIPS, 3, 2, LANES)] * 2, guess)
    prev0, prev1 = onward(half0, 0), onward(half1, 1)
    flip = ((block > 0) & (block % 2 == 0)).astype(jnp.int32)
    (base,) = call(home_fields_body, [sds(64, 9, 2, LANES)], place, source, diffusivity, initial, smem=1)
    vmem = pl.BlockSpec(memory_space=pltpu.VMEM)
    sent = pl.pallas_call(
        previous_body,
        out_shape=sds(64, 9, 2, LANES),
        in_specs=[pl.BlockSpec(memory_space=pltpu.SMEM)] * 2 + [vmem] * 3,
        out_specs=vmem,
        input_output_aliases={4: 0},
        compiler_params=pltpu.CompilerParams(vmem_limit_bytes=12 * 1024 * 1024),
    )(place, block, prev0, prev1, base)
    strips = lax.all_to_all(sent, BLOCK, 0, 0, tiled=True).reshape(8, 8, 9, 2, LANES)

    def swap(mine):
        return lax.ppermute(mine, "core", [(0, 1), (1, 0)])

    def from_neighbour(mine):
        return lax.ppermute(mine, ("zl", "core", "y"), neighbour_route())

    def exchange(mine, beside):
        got = from_neighbour(mine)
        got, beside = lax.optimization_barrier((got, beside))
        return got, swap(got), beside

    f, k, start, message = call(
        pack_body,
        [sds(8, NZ, STRIP, LANES), sds(NZ, WIN, LANES), sds(1, 8, PAIR, LANES), sds(4, 8, PAIR, LANES)],
        core, flip, strips, swap(strips), smem=2,
    )
    flops = NZ * WIN * LANES * 15
    both_rates = call(
        coefficients_body, [sds(7, NZ, WIN, LANES)] * 2, k, flops=6 * flops,
        scratch=(pltpu.VMEM((NZ + 2, WIN, LANES), F32),),
    )
    got, got2, (fine, coarse) = exchange(message, both_rates)
    v_early, state = call(
        early_body, [sds(6, NZ, STRIP, LANES), sds(3, 8, PAIR, LANES)],
        core, fine, f, start, got, got2, smem=1, flops=12 * flops,
        scratch=SWEEP_SCRATCH + (pltpu.VMEM((6, NZ, WIN, LANES), F32),),
    )
    (start_g,) = call(
        start_body, [sds(NZ, WIN, LANES)],
        core, block, coarse, start, got, got2, smem=2, flops=2 * flops, scratch=SWEEP_SCRATCH,
    )
    state_got, state_got2, start_g = exchange(state, start_g)
    v_late, first_powers, last = call(
        late_body, [sds(NZ, STRIP, LANES), sds(5, NZ, STRIP, LANES), sds(1, 8, PAIR, LANES)],
        core, fine, coarse, state, state_got, state_got2, start_g, smem=1, flops=12 * flops,
        scratch=SWEEP_SCRATCH + (pltpu.VMEM((NZ + 2, WIN, LANES), F32),),
    )
    (powers,) = call(
        powers_body, [sds(NB, 4 * STRIP, LANES)],
        core, side, block, coarse, last, from_neighbour(last), first_powers, smem=3, flops=6 * flops,
        scratch=SWEEP_SCRATCH + (pltpu.VMEM((NB, NZ, STRIP, LANES), F32),),
    )
    arrived = lax.all_to_all(powers, BLOCKS, 0, 0, tiled=True)
    (back,) = call(collect_body, [sds(32, 16, LANES)], core, side, arrived, v_early, v_late, smem=2)
    returned = lax.all_to_all(back, ("zl", "core", "y"), 0, 0, tiled=True)
    (result,) = call(home_body, [sds(2, NY, LANES)], returned)
    return result[None]


def solution(mesh):
    fine = Mesh(mesh.devices.reshape(SIZES), AXES)
    tm = ("x", "zh", "zl", "core")
    space = ("y", "zhi")
    in_specs = (P(tm, space, None, None), P(tm, space, None, None), P(space, None, None), P(space, None, None))
    out_specs = P(tm, space, None, None)
    return jax.shard_map(on_device, mesh=fine, in_specs=in_specs, out_specs=out_specs, check_vma=False)
```

```python
import functools

import jax
import jax.numpy as jnp
from jax import lax
from jax.experimental import pallas as pl
from jax.experimental.pallas import tpu as pltpu
from jax.sharding import Mesh, PartitionSpec as P

F32 = jnp.float32

damping = 0.8
step_size = 0.5
coarse_size = 4.0
z_weight = 8.0

AXES = ("x", "zh", "zl", "core", "y", "zhi")
SIZES = (4, 2, 4, 2, 4, 2)
BLOCK = ("zl", "core", "y", "zhi")
BLOCKS = ("x", "zh")
NB = 8
NZ = 16
NY = 192
CHIPS = 16
STRIP = NY // CHIPS
PAIR = 2 * STRIP
HALF = STRIP // 2
LANES = 128
LAYERS = [(y, p) for y in range(4) for p in range(2)]
LOW, OWN, HIGH, WIN = 4, 16, 28, 40


def chip_order(zl, y):
    return zl * 4 + (y if zl % 2 == 0 else 3 - y)


def neighbour_route():
    place = {chip_order(zl, y): (zl, y) for zl in range(4) for y in range(4)}
    route = []
    for core, step in ((0, 1), (1, -1)):
        for m in range(CHIPS):
            if 0 <= m + step < CHIPS:
                (zl, y), (to_zl, to_y) = place[m], place[m + step]
                route.append(((zl * 2 + core) * 4 + y, (to_zl * 2 + core) * 4 + to_y))
    return route


def at(z, first, last):
    return slice((z % 2) * STRIP + first, (z % 2) * STRIP + last)


def call(body, outs, *args, scratch=(), smem=0, flops=0):
    specs = [pl.BlockSpec(memory_space=pltpu.SMEM)] * smem
    specs += [pl.BlockSpec(memory_space=pltpu.VMEM)] * (len(args) - smem)
    out_specs = [pl.BlockSpec(memory_space=pltpu.VMEM)] * len(outs)
    size = sum(4 * a.size for a in args) + sum(4 * o.size for o in outs)
    return pl.pallas_call(
        body,
        out_shape=list(outs),
        in_specs=specs,
        out_specs=out_specs,
        scratch_shapes=list(scratch),
        compiler_params=pltpu.CompilerParams(vmem_limit_bytes=12 * 1024 * 1024),
        cost_estimate=pl.CostEstimate(flops=flops, bytes_accessed=size, transcendentals=0),
    )(*args)


def sds(*shape):
    return jax.ShapeDtypeStruct(shape, F32)


def targets():
    for zl in range(4):
        for y in range(4):
            for zhi in range(2):
                for core in range(2):
                    yield ((zl * 2 + core) * 4 + y) * 2 + zhi, core, chip_order(zl, y)


def halves_body(guess_ref, half0_ref, half1_ref):
    for core in range(2):
        for m in range(CHIPS):
            for r in range(3):
                row = m * STRIP + 2 * r
                half0_ref[core, m, r] = guess_ref[core, row : row + 2]
                half1_ref[core, m, r] = guess_ref[core, row + 6 : row + 8]


def home_fields_body(j_ref, src_ref, cond_ref, init_ref, out_ref):
    place = j_ref[0]
    for to, core, m in targets():
        for r in range(6):
            row = m * STRIP + 2 * r
            out_ref[to, r] = src_ref[core, row : row + 2]

    def fill(ref, shift, half):
        for to, core, m in targets():
            m = m + shift
            for r in range(3):
                row = m * STRIP + 6 * half + 2 * r
                if 0 <= m < CHIPS:
                    out_ref[to, 6 + r] = ref[core, row : row + 2]
                else:
                    out_ref[to, 6 + r] = jnp.zeros((2, LANES), F32)

    for half in range(2):
        pl.when(place == half)(functools.partial(fill, init_ref, 0, half))
        for n, shift in enumerate((0, 1, -1)):
            pl.when(place == 2 + 2 * n + half)(functools.partial(fill, cond_ref, shift, half))


def previous_body(j_ref, block_ref, prev0_ref, prev1_ref, base_ref, out_ref):
    for half, prev_ref in ((0, prev0_ref), (1, prev1_ref)):

        @pl.when((j_ref[0] == half) & (block_ref[0] > 0))
        def _(prev_ref=prev_ref):
            for to, core, m in targets():
                for r in range(3):
                    out_ref[to, 6 + r] = prev_ref[core, m, r]


def by_core(core_ref, body, mine, other):
    pl.when(core_ref[0] == 0)(functools.partial(body, mine, other))
    pl.when(core_ref[0] == 1)(functools.partial(body, other, mine))


def pack_body(core_ref, flip_ref, own_ref, other_ref, f_ref, k_ref, start_ref, out_ref):
    flip = flip_ref[0]

    def order(*halves):
        for z in range(NZ):
            half, s = halves[z % 2], z // 2
            k_ref[z, 0:LOW] = jnp.zeros((LOW, LANES), F32)
            for r in range(6):
                for n in range(8):
                    f_ref[n, z, 2 * r : 2 * r + 2] = half[n, s, r]
                part, extra = r // 3, 6 + r % 3
                start = half[part, s + (1 - 2 * (s % 2)) * flip, extra]
                start_ref[0, s, at(z, 2 * r, 2 * r + 2)] = start
                out_ref[0, s, at(z, 2 * r, 2 * r + 2)] = start
                for place, base in ((6, LOW), (2, OWN), (4, HIGH)):
                    k_ref[z, base + 2 * r : base + 2 * r + 2] = half[place + part, s, extra]

    by_core(core_ref, order, own_ref, other_ref)

    @pl.when(core_ref[0] == 0)
    def _():
        for z in range(NZ):
            for n in range(3):
                rows = 11 - 2 * n
                out_ref[1 + n, z // 2, at(z, STRIP - rows, STRIP)] = f_ref[n, z, STRIP - rows : STRIP]
                out_ref[1 + n, z // 2, at(z, 0, STRIP - rows)] = f_ref[5 - n, z, rows:STRIP]

    @pl.when(core_ref[0] == 1)
    def _():
        for z in range(NZ):
            for n in range(3):
                rows = 11 - 2 * n
                out_ref[1 + n, z // 2, at(z, 0, rows)] = f_ref[n, z, 0:rows]
                out_ref[1 + n, z // 2, at(z, rows, STRIP)] = f_ref[5 - n, z, 0 : STRIP - rows]


def clear_ends(*refs):
    zero = jnp.zeros((WIN, LANES), F32)
    for ref in refs:
        ref[0] = zero
        ref[NZ + 1] = zero


def load_window(core_ref, a_s, field, own_ref, got_ref, got2_ref):
    def load(below_ref, above_ref):
        zero = jnp.zeros((LOW, LANES), F32)
        for z in range(NZ):
            a_s[z + 1, 0:LOW] = zero
            a_s[z + 1, LOW:OWN] = below_ref[field, z // 2, at(z, 0, STRIP)]
            a_s[z + 1, OWN:HIGH] = own_ref[field, z // 2, at(z, 0, STRIP)]
            a_s[z + 1, HIGH:WIN] = above_ref[field, z // 2, at(z, 0, STRIP)]

    by_core(core_ref, load, got_ref, got2_ref)


def coefficients(rate, k_s, co_s):
    lane = lax.broadcasted_iota(jnp.int32, (WIN, LANES), 1)
    first = lane == 0
    last = lane == LANES - 1

    def layer(z, carry):
        k = k_s[z + 1]
        side = 0.5 * rate
        tall = 0.5 * rate * z_weight
        c = [
            tall * (k + k_s[z]),
            tall * (k + k_s[z + 2]),
            side * (k + pltpu.roll(k, 1, 0)),
            side * (k + pltpu.roll(k, WIN - 1, 0)),
            side * (k + jnp.where(first, 0.0, pltpu.roll(k, 1, 1))),
            side * (k + jnp.where(last, 0.0, pltpu.roll(k, LANES - 1, 1))),
        ]
        total = ((c[0] + c[1]) + (c[2] + c[3])) + (c[4] + c[5])
        d = jnp.where(k > 0.0, damping / (1.0 + total), 0.0)
        co_s[0, z] = c[0] * d
        co_s[1, z] = c[1] * d
        co_s[2, z] = c[2] * d
        co_s[3, z] = c[3] * d
        co_s[4, z] = jnp.where(first, 0.0, c[4] * d)
        co_s[5, z] = jnp.where(last, 0.0, c[5] * d)
        co_s[6, z] = d
        return carry

    lax.fori_loop(0, NZ, layer, 0)


def coefficients_body(k_ref, fine_ref, coarse_ref, k_s):
    clear_ends(k_s)
    for z in range(NZ):
        k_s[z + 1] = k_ref[z]
    coefficients(step_size, k_s, fine_ref)
    coefficients(coarse_size, k_s, coarse_ref)


def one_sweep(src, dst, co_s, db_s, rows):
    tall = rows.stop - rows.start
    under, w = src[0, rows], src[1, rows]
    for z in range(NZ):
        over = src[z + 2, rows]
        acc = (db_s[z, rows] + (1.0 - damping) * w) + (co_s[0, z, rows] * under + co_s[1, z, rows] * over)
        acc = acc + (
            co_s[2, z, rows] * pltpu.roll(w, 1, 0) + co_s[3, z, rows] * pltpu.roll(w, tall - 1, 0)
        )
        acc = acc + (
            co_s[4, z, rows] * pltpu.roll(w, 1, 1) + co_s[5, z, rows] * pltpu.roll(w, LANES - 1, 1)
        )
        dst[z + 1, rows] = acc
        under, w = w, over


def step(halo, a_s, b_s, co_s, db_s, forcing=None):
    rows = slice(8, 32) if halo <= 4 else slice(8, WIN) if halo <= 8 else slice(0, WIN)
    for z in range(NZ):
        target = a_s[z + 1, rows]
        if forcing is not None:
            target = target + step_size * forcing[z, rows]
        db_s[z, rows] = co_s[6, z, rows] * target
    one_sweep(a_s, b_s, co_s, db_s, rows)
    one_sweep(b_s, a_s, co_s, db_s, rows)


def early_body(
    core_ref, co_s, f_ref, own_ref, got_ref, got2_ref, out_ref, next_ref, a_s, b_s, db_s, f_s
):
    clear_ends(a_s, b_s)
    load_window(core_ref, a_s, 0, own_ref, got_ref, got2_ref)
    for n in range(6):
        for z in range(NZ):
            f_s[n, z] = jnp.zeros((WIN, LANES), F32)
            f_s[n, z, OWN:HIGH] = f_ref[n, z]

    def halos(below_ref, above_ref):
        for n in range(3):
            rows = 11 - 2 * n
            for z in range(NZ):
                s = z // 2
                f_s[n, z, OWN - rows : OWN] = below_ref[1 + n, s, at(z, STRIP - rows, STRIP)]
                f_s[n, z, HIGH : HIGH + rows] = above_ref[1 + n, s, at(z, 0, rows)]
                f_s[5 - n, z, OWN - STRIP + rows : OWN] = below_ref[1 + n, s, at(z, 0, STRIP - rows)]
                f_s[5 - n, z, HIGH : HIGH + STRIP - rows] = above_ref[1 + n, s, at(z, rows, STRIP)]

    by_core(core_ref, halos, got_ref, got2_ref)
    for n in range(6):
        step(12 - 2 * n, a_s, b_s, co_s, db_s, f_s.at[n])
        for z in range(NZ):
            out_ref[n, z] = a_s[z + 1, OWN:HIGH]
    for z in range(NZ):
        next_ref[0, z // 2, at(z, 0, STRIP)] = a_s[z + 1, OWN:HIGH]
        for n in range(2):
            next_ref[1 + n, z // 2, at(z, 0, STRIP)] = f_ref[6 + n, z]


def start_body(core_ref, block_ref, co_s, own_ref, got_ref, got2_ref, out_ref, a_s, b_s, db_s):
    clear_ends(a_s, b_s)
    load_window(core_ref, a_s, 0, own_ref, got_ref, got2_ref)
    step(10, a_s, b_s, co_s, db_s)
    later = block_ref[0] > 0
    for z in range(NZ):
        out_ref[z] = jnp.where(later, a_s[z + 1], 0.0)


def late_body(
    core_ref, side_ref, fine_s, co_s, own_ref, got_ref, got2_ref, start_ref,
    out_ref, pow_ref, next_ref, a_s, b_s, db_s, f_s, pow_s,
):
    clear_ends(a_s, b_s)
    load_window(core_ref, a_s, 0, own_ref, got_ref, got2_ref)
    for n in range(2):
        load_window(core_ref, f_s, 1 + n, own_ref, got_ref, got2_ref)
        step(12 - 2 * n, a_s, b_s, fine_s, db_s, f_s.at[pl.ds(1, NZ)])
        if n == 0:
            for z in range(NZ):
                out_ref[z] = a_s[z + 1, OWN:HIGH]
    for z in range(NZ):
        a_s[z + 1] = a_s[z + 1] - start_ref[z]
    for n in range(5):
        if n > 0:
            step(10 - 2 * n, a_s, b_s, co_s, db_s)
        for z in range(NZ):
            pow_s[n, z] = a_s[z + 1, OWN:HIGH]
    for z in range(NZ):
        next_ref[0, z // 2, at(z, 0, STRIP)] = a_s[z + 1, OWN:HIGH]

    def send(m, z, rows):
        for n in range(5):
            pow_ref[n, m * HALF : (m + 1) * HALF] = pow_s[n, z, rows]

    cut(core_ref, side_ref, send)


def powers_body(
    core_ref, side_ref, block_ref, co_s, own_ref, got_ref, early_ref, out_ref, a_s, b_s, db_s, pow_s, late_s
):
    clear_ends(a_s, b_s)
    for z in range(NZ):
        a_s[z + 1] = jnp.zeros((WIN, LANES), F32)
        a_s[z + 1, OWN:HIGH] = own_ref[0, z // 2, at(z, 0, STRIP)]

    def halo(rows):
        for z in range(NZ):
            a_s[z + 1, rows] = got_ref[0, z // 2, at(z, 0, STRIP)]

    pl.when(core_ref[0] == 0)(functools.partial(halo, slice(LOW, OWN)))
    pl.when(core_ref[0] == 1)(functools.partial(halo, slice(HIGH, WIN)))
    for n in range(5):
        pow_s[n] = early_ref[n]
    for n in range(3):
        step(6 - 2 * n, a_s, b_s, co_s, db_s)
        for z in range(NZ):
            late_s[n, z] = a_s[z + 1, OWN:HIGH]

    def send(m, z, rows):
        for n in range(3):
            pow_s[5 + n, m * HALF : (m + 1) * HALF] = late_s[n, z, rows]

    cut(core_ref, side_ref, send)
    for b in range(NB):
        power = jnp.clip(b - block_ref[0], 0, NB - 1)
        out_ref[b] = jnp.where(b >= block_ref[0], pow_s[power], 0.0)


def cut(core_ref, side_ref, body):
    def each(rows):
        for n, (y, p) in enumerate(LAYERS):
            body(n, 2 * (2 * y + side_ref[0]) + p, rows)

    for core in range(2):
        pl.when(core_ref[0] == core)(functools.partial(each, slice(core * HALF, (core + 1) * HALF)))


SWEEP_SCRATCH = (
    pltpu.VMEM((NZ + 2, WIN, LANES), F32),
    pltpu.VMEM((NZ + 2, WIN, LANES), F32),
    pltpu.VMEM((NZ, WIN, LANES), F32),
)


def collect_body(core_ref, side_ref, got_ref, early_ref, late_ref, out_ref):
    def fill(n, z, rows):
        y, p = LAYERS[n]
        total = got_ref[0, n * HALF : (n + 1) * HALF]
        for b in range(1, NB):
            total = total + got_ref[b, n * HALF : (n + 1) * HALF]
        states = [early_ref[t, z, rows] for t in range(6)] + [late_ref[z, rows], total]
        for t in range(8):
            for r in range(3):
                out_ref[t * 4 + y, 3 * p + r] = states[t][2 * r : 2 * r + 2]

    cut(core_ref, side_ref, fill)


def home_body(got_ref, out_ref):
    for zl in range(4):
        for y in range(4):
            for core in range(2):
                for p in range(2):
                    for r in range(3):
                        row = chip_order(zl, y) * STRIP + core * HALF + 2 * r
                        out_ref[p, row : row + 2] = got_ref[(zl * 2 + core) * 4 + y, 3 * p + r]


def on_device(guess, source, diffusivity, initial):
    guess = guess[0]
    source = source[0]
    core = lax.axis_index("core")[None]
    side = lax.axis_index("zhi")[None]
    place = lax.axis_index(("zl", "core"))[None]
    block = lax.axis_index(BLOCKS)[None]

    def onward(mine, place):
        route = []
        for b in range(NB - 1):
            for y in range(4):
                for zhi in range(2):
                    to = zhi if b % 2 == 0 else 1 - zhi
                    route.append((((b * 8 + 7) * 4 + y) * 2 + zhi, (((b + 1) * 8 + place) * 4 + y) * 2 + to))
        return lax.ppermute(mine, AXES, route)

    half0, half1 = call(halves_body, [sds(2, CHIPS, 3, 2, LANES)] * 2, guess)
    prev0, prev1 = onward(half0, 0), onward(half1, 1)
    flip = ((block > 0) & (block % 2 == 0)).astype(jnp.int32)
    (base,) = call(home_fields_body, [sds(64, 9, 2, LANES)], place, source, diffusivity, initial, smem=1)
    vmem = pl.BlockSpec(memory_space=pltpu.VMEM)
    sent = pl.pallas_call(
        previous_body,
        out_shape=sds(64, 9, 2, LANES),
        in_specs=[pl.BlockSpec(memory_space=pltpu.SMEM)] * 2 + [vmem] * 3,
        out_specs=vmem,
        input_output_aliases={4: 0},
        compiler_params=pltpu.CompilerParams(vmem_limit_bytes=12 * 1024 * 1024),
    )(place, block, prev0, prev1, base)
    strips = lax.all_to_all(sent, BLOCK, 0, 0, tiled=True).reshape(8, 8, 9, 2, LANES)

    def swap(mine):
        return lax.ppermute(mine, "core", [(0, 1), (1, 0)])

    def from_neighbour(mine):
        return lax.ppermute(mine, ("zl", "core", "y"), neighbour_route())

    def exchange(mine, beside):
        got = from_neighbour(mine)
        got, beside = lax.optimization_barrier((got, beside))
        return got, swap(got), beside

    f, k, start, message = call(
        pack_body,
        [sds(8, NZ, STRIP, LANES), sds(NZ, WIN, LANES), sds(1, 8, PAIR, LANES), sds(4, 8, PAIR, LANES)],
        core, flip, strips, swap(strips), smem=2,
    )
    flops = NZ * WIN * LANES * 15
    both_rates = call(
        coefficients_body, [sds(7, NZ, WIN, LANES)] * 2, k, flops=6 * flops,
        scratch=(pltpu.VMEM((NZ + 2, WIN, LANES), F32),),
    )
    got, got2, (fine, coarse) = exchange(message, both_rates)
    v_early, state = call(
        early_body, [sds(6, NZ, STRIP, LANES), sds(3, 8, PAIR, LANES)],
        core, fine, f, start, got, got2, smem=1, flops=12 * flops,
        scratch=SWEEP_SCRATCH + (pltpu.VMEM((6, NZ, WIN, LANES), F32),),
    )
    (start_g,) = call(
        start_body, [sds(NZ, WIN, LANES)],
        core, block, coarse, start, got, got2, smem=2, flops=2 * flops, scratch=SWEEP_SCRATCH,
    )
    state_got, state_got2, start_g = exchange(state, start_g)
    v_late, first_powers, last = call(
        late_body, [sds(NZ, STRIP, LANES), sds(5, 8 * HALF, LANES), sds(1, 8, PAIR, LANES)],
        core, side, fine, coarse, state, state_got, state_got2, start_g, smem=2, flops=12 * flops,
        scratch=SWEEP_SCRATCH + (pltpu.VMEM((NZ + 2, WIN, LANES), F32), pltpu.VMEM((5, NZ, STRIP, LANES), F32)),
    )
    (powers,) = call(
        powers_body, [sds(NB, 8 * HALF, LANES)],
        core, side, block, coarse, last, from_neighbour(last), first_powers, smem=3, flops=6 * flops,
        scratch=SWEEP_SCRATCH + (pltpu.VMEM((NB, 8 * HALF, LANES), F32), pltpu.VMEM((3, NZ, STRIP, LANES), F32)),
    )
    arrived = lax.all_to_all(powers, BLOCKS, 0, 0, tiled=True)
    (back,) = call(collect_body, [sds(32, 6, 2, LANES)], core, side, arrived, v_early, v_late, smem=2)
    returned = lax.all_to_all(back, ("zl", "core", "y"), 0, 0, tiled=True)
    (result,) = call(home_body, [sds(2, NY, LANES)], returned)
    return result[None]


def solution(mesh):
    fine = Mesh(mesh.devices.reshape(SIZES), AXES)
    tm = ("x", "zh", "zl", "core")
    space = ("y", "zhi")
    in_specs = (P(tm, space, None, None), P(tm, space, None, None), P(space, None, None), P(space, None, None))
    out_specs = P(tm, space, None, None)
    return jax.shard_map(on_device, mesh=fine, in_specs=in_specs, out_specs=out_specs, check_vma=False)
```

```python
import functools

import jax
import jax.numpy as jnp
from jax import lax
from jax.experimental import pallas as pl
from jax.experimental.pallas import tpu as pltpu
from jax.sharding import Mesh, PartitionSpec as P

F32 = jnp.float32

damping = 0.8
step_size = 0.5
coarse_size = 4.0
z_weight = 8.0

AXES = ("x", "zh", "zl", "core", "y", "zhi")
SIZES = (4, 2, 4, 2, 4, 2)
BLOCK = ("zl", "core", "y", "zhi")
BLOCKS = ("x", "zh")
NB = 8
NZ = 16
NY = 192
CHIPS = 16
STRIP = NY // CHIPS
PAIR = 2 * STRIP
HALF = STRIP // 2
LANES = 128
LAYERS = [(y, p) for y in range(4) for p in range(2)]
LOW, OWN, HIGH, WIN = 4, 16, 28, 40


def chip_order(zl, y):
    return zl * 4 + (y if zl % 2 == 0 else 3 - y)


def neighbour_route():
    place = {chip_order(zl, y): (zl, y) for zl in range(4) for y in range(4)}
    route = []
    for core, step in ((0, 1), (1, -1)):
        for m in range(CHIPS):
            if 0 <= m + step < CHIPS:
                (zl, y), (to_zl, to_y) = place[m], place[m + step]
                route.append(((zl * 2 + core) * 4 + y, (to_zl * 2 + core) * 4 + to_y))
    return route


def at(z, first, last):
    return slice((z % 2) * STRIP + first, (z % 2) * STRIP + last)


def call(body, outs, *args, scratch=(), smem=0, flops=0):
    specs = [pl.BlockSpec(memory_space=pltpu.SMEM)] * smem
    specs += [pl.BlockSpec(memory_space=pltpu.VMEM)] * (len(args) - smem)
    out_specs = [pl.BlockSpec(memory_space=pltpu.VMEM)] * len(outs)
    size = sum(4 * a.size for a in args) + sum(4 * o.size for o in outs)
    return pl.pallas_call(
        body,
        out_shape=list(outs),
        in_specs=specs,
        out_specs=out_specs,
        scratch_shapes=list(scratch),
        compiler_params=pltpu.CompilerParams(vmem_limit_bytes=12 * 1024 * 1024),
        cost_estimate=pl.CostEstimate(flops=flops, bytes_accessed=size, transcendentals=0),
    )(*args)


def sds(*shape):
    return jax.ShapeDtypeStruct(shape, F32)


def targets():
    for zl in range(4):
        for y in range(4):
            for zhi in range(2):
                for core in range(2):
                    yield ((zl * 2 + core) * 4 + y) * 2 + zhi, core, chip_order(zl, y)


def halves_body(guess_ref, half0_ref, half1_ref):
    for core in range(2):
        for m in range(CHIPS):
            for r in range(3):
                row = m * STRIP + 2 * r
                half0_ref[core, m, r] = guess_ref[core, row : row + 2]
                half1_ref[core, m, r] = guess_ref[core, row + 6 : row + 8]


def home_fields_body(j_ref, src_ref, cond_ref, init_ref, out_ref):
    place = j_ref[0]
    for to, core, m in targets():
        for r in range(6):
            row = m * STRIP + 2 * r
            out_ref[to, r] = src_ref[core, row : row + 2]

    def fill(ref, shift, half):
        for to, core, m in targets():
            m = m + shift
            for r in range(3):
                row = m * STRIP + 6 * half + 2 * r
                if 0 <= m < CHIPS:
                    out_ref[to, 6 + r] = ref[core, row : row + 2]
                else:
                    out_ref[to, 6 + r] = jnp.zeros((2, LANES), F32)

    for half in range(2):
        pl.when(place == half)(functools.partial(fill, init_ref, 0, half))
        for n, shift in enumerate((0, 1, -1)):
            pl.when(place == 2 + 2 * n + half)(functools.partial(fill, cond_ref, shift, half))


def previous_body(j_ref, block_ref, prev0_ref, prev1_ref, base_ref, out_ref):
    for half, prev_ref in ((0, prev0_ref), (1, prev1_ref)):

        @pl.when((j_ref[0] == half) & (block_ref[0] > 0))
        def _(prev_ref=prev_ref):
            for to, core, m in targets():
                for r in range(3):
                    out_ref[to, 6 + r] = prev_ref[core, m, r]


def by_core(core_ref, body, mine, other):
    pl.when(core_ref[0] == 0)(functools.partial(body, mine, other))
    pl.when(core_ref[0] == 1)(functools.partial(body, other, mine))


def pack_body(core_ref, flip_ref, own_ref, other_ref, f_ref, k_ref, start_ref, out_ref):
    flip = flip_ref[0]

    def order(*halves):
        for z in range(NZ):
            half, s = halves[z % 2], z // 2
            k_ref[z, 0:LOW] = jnp.zeros((LOW, LANES), F32)
            for r in range(6):
                for n in range(8):
                    f_ref[n, z, 2 * r : 2 * r + 2] = half[n, s, r]
                part, extra = r // 3, 6 + r % 3
                start = half[part, s + (1 - 2 * (s % 2)) * flip, extra]
                start_ref[0, s, at(z, 2 * r, 2 * r + 2)] = start
                out_ref[0, s, at(z, 2 * r, 2 * r + 2)] = start
                for place, base in ((6, LOW), (2, OWN), (4, HIGH)):
                    k_ref[z, base + 2 * r : base + 2 * r + 2] = half[place + part, s, extra]

    by_core(core_ref, order, own_ref, other_ref)

    @pl.when(core_ref[0] == 0)
    def _():
        for z in range(NZ):
            for n in range(3):
                rows = 11 - 2 * n
                out_ref[1 + n, z // 2, at(z, STRIP - rows, STRIP)] = f_ref[n, z, STRIP - rows : STRIP]
                out_ref[1 + n, z // 2, at(z, 0, STRIP - rows)] = f_ref[5 - n, z, rows:STRIP]

    @pl.when(core_ref[0] == 1)
    def _():
        for z in range(NZ):
            for n in range(3):
                rows = 11 - 2 * n
                out_ref[1 + n, z // 2, at(z, 0, rows)] = f_ref[n, z, 0:rows]
                out_ref[1 + n, z // 2, at(z, rows, STRIP)] = f_ref[5 - n, z, 0 : STRIP - rows]


def clear_ends(*refs):
    zero = jnp.zeros((WIN, LANES), F32)
    for ref in refs:
        ref[0] = zero
        ref[NZ + 1] = zero


def load_window(core_ref, a_s, field, own_ref, got_ref, got2_ref):
    def load(below_ref, above_ref):
        zero = jnp.zeros((LOW, LANES), F32)
        for z in range(NZ):
            a_s[z + 1, 0:LOW] = zero
            a_s[z + 1, LOW:OWN] = below_ref[field, z // 2, at(z, 0, STRIP)]
            a_s[z + 1, OWN:HIGH] = own_ref[field, z // 2, at(z, 0, STRIP)]
            a_s[z + 1, HIGH:WIN] = above_ref[field, z // 2, at(z, 0, STRIP)]

    by_core(core_ref, load, got_ref, got2_ref)


def coefficients(rate, k_s, co_s):
    lane = lax.broadcasted_iota(jnp.int32, (WIN, LANES), 1)
    first = lane == 0
    last = lane == LANES - 1

    def layer(z, carry):
        k = k_s[z + 1]
        side = 0.5 * rate
        tall = 0.5 * rate * z_weight
        c = [
            tall * (k + k_s[z]),
            tall * (k + k_s[z + 2]),
            side * (k + pltpu.roll(k, 1, 0)),
            side * (k + pltpu.roll(k, WIN - 1, 0)),
            side * (k + jnp.where(first, 0.0, pltpu.roll(k, 1, 1))),
            side * (k + jnp.where(last, 0.0, pltpu.roll(k, LANES - 1, 1))),
        ]
        total = ((c[0] + c[1]) + (c[2] + c[3])) + (c[4] + c[5])
        d = jnp.where(k > 0.0, damping / (1.0 + total), 0.0)
        co_s[0, z] = c[0] * d
        co_s[1, z] = c[1] * d
        co_s[2, z] = c[2] * d
        co_s[3, z] = c[3] * d
        co_s[4, z] = jnp.where(first, 0.0, c[4] * d)
        co_s[5, z] = jnp.where(last, 0.0, c[5] * d)
        co_s[6, z] = d
        return carry

    lax.fori_loop(0, NZ, layer, 0)


def coefficients_body(k_ref, fine_ref, coarse_ref, k_s):
    clear_ends(k_s)
    for z in range(NZ):
        k_s[z + 1] = k_ref[z]
    coefficients(step_size, k_s, fine_ref)
    coefficients(coarse_size, k_s, coarse_ref)


def one_sweep(src, dst, co_s, db_s, rows):
    tall = rows.stop - rows.start
    under, w = src[0, rows], src[1, rows]
    for z in range(NZ):
        over = src[z + 2, rows]
        acc = (db_s[z, rows] + (1.0 - damping) * w) + (co_s[0, z, rows] * under + co_s[1, z, rows] * over)
        acc = acc + (
            co_s[2, z, rows] * pltpu.roll(w, 1, 0) + co_s[3, z, rows] * pltpu.roll(w, tall - 1, 0)
        )
        acc = acc + (
            co_s[4, z, rows] * pltpu.roll(w, 1, 1) + co_s[5, z, rows] * pltpu.roll(w, LANES - 1, 1)
        )
        dst[z + 1, rows] = acc
        under, w = w, over


def step(halo, a_s, b_s, co_s, db_s, forcing=None):
    rows = slice(8, 32) if halo <= 4 else slice(8, WIN) if halo <= 8 else slice(0, WIN)
    for z in range(NZ):
        target = a_s[z + 1, rows]
        if forcing is not None:
            target = target + step_size * forcing[z, rows]
        db_s[z, rows] = co_s[6, z, rows] * target
    one_sweep(a_s, b_s, co_s, db_s, rows)
    one_sweep(b_s, a_s, co_s, db_s, rows)


def early_body(
    core_ref, co_s, f_ref, own_ref, got_ref, got2_ref, out_ref, next_ref, a_s, b_s, db_s, f_s
):
    clear_ends(a_s, b_s)
    load_window(core_ref, a_s, 0, own_ref, got_ref, got2_ref)
    for n in range(6):
        for z in range(NZ):
            f_s[n, z] = jnp.zeros((WIN, LANES), F32)
            f_s[n, z, OWN:HIGH] = f_ref[n, z]

    def halos(below_ref, above_ref):
        for n in range(3):
            rows = 11 - 2 * n
            for z in range(NZ):
                s = z // 2
                f_s[n, z, OWN - rows : OWN] = below_ref[1 + n, s, at(z, STRIP - rows, STRIP)]
                f_s[n, z, HIGH : HIGH + rows] = above_ref[1 + n, s, at(z, 0, rows)]
                f_s[5 - n, z, OWN - STRIP + rows : OWN] = below_ref[1 + n, s, at(z, 0, STRIP - rows)]
                f_s[5 - n, z, HIGH : HIGH + STRIP - rows] = above_ref[1 + n, s, at(z, rows, STRIP)]

    by_core(core_ref, halos, got_ref, got2_ref)
    for n in range(6):
        step(12 - 2 * n, a_s, b_s, co_s, db_s, f_s.at[n])
        for z in range(NZ):
            out_ref[n, z] = a_s[z + 1, OWN:HIGH]
    for z in range(NZ):
        next_ref[0, z // 2, at(z, 0, STRIP)] = a_s[z + 1, OWN:HIGH]
        for n in range(2):
            next_ref[1 + n, z // 2, at(z, 0, STRIP)] = f_ref[6 + n, z]


def start_body(core_ref, block_ref, co_s, own_ref, got_ref, got2_ref, out_ref, a_s, b_s, db_s):
    clear_ends(a_s, b_s)
    load_window(core_ref, a_s, 0, own_ref, got_ref, got2_ref)
    step(10, a_s, b_s, co_s, db_s)
    later = block_ref[0] > 0
    for z in range(NZ):
        out_ref[z] = jnp.where(later, a_s[z + 1], 0.0)


def late_body(
    core_ref, fine_s, co_s, own_ref, got_ref, got2_ref, start_ref,
    out_ref, pow_ref, next_ref, a_s, b_s, db_s, f_s,
):
    clear_ends(a_s, b_s)
    load_window(core_ref, a_s, 0, own_ref, got_ref, got2_ref)
    for n in range(2):
        load_window(core_ref, f_s, 1 + n, own_ref, got_ref, got2_ref)
        step(12 - 2 * n, a_s, b_s, fine_s, db_s, f_s.at[pl.ds(1, NZ)])
        if n == 0:
            for z in range(NZ):
                out_ref[z] = a_s[z + 1, OWN:HIGH]
    for z in range(NZ):
        a_s[z + 1] = a_s[z + 1] - start_ref[z]
    for n in range(5):
        if n > 0:
            step(10 - 2 * n, a_s, b_s, co_s, db_s)
        for z in range(NZ):
            pow_ref[n, z] = a_s[z + 1, OWN:HIGH]
    for z in range(NZ):
        next_ref[0, z // 2, at(z, 0, STRIP)] = a_s[z + 1, OWN:HIGH]


def early_powers_body(core_ref, side_ref, block_ref, early_ref, out_ref):
    for b in range(NB):
        power = b - block_ref[0]
        live = (power >= 0) & (power < 5)
        power = jnp.clip(power, 0, 4)

        def send(m, z, rows, b=b, power=power, live=live):
            out_ref[b, m * HALF : (m + 1) * HALF] = jnp.where(live, early_ref[power, z, rows], 0.0)

        cut(core_ref, side_ref, send)


def powers_body(
    core_ref, side_ref, block_ref, co_s, own_ref, got_ref, base_ref, out_ref, a_s, b_s, db_s, late_s
):
    clear_ends(a_s, b_s)
    for z in range(NZ):
        a_s[z + 1] = jnp.zeros((WIN, LANES), F32)
        a_s[z + 1, OWN:HIGH] = own_ref[0, z // 2, at(z, 0, STRIP)]

    def halo(rows):
        for z in range(NZ):
            a_s[z + 1, rows] = got_ref[0, z // 2, at(z, 0, STRIP)]

    pl.when(core_ref[0] == 0)(functools.partial(halo, slice(LOW, OWN)))
    pl.when(core_ref[0] == 1)(functools.partial(halo, slice(HIGH, WIN)))
    for n in range(3):
        step(6 - 2 * n, a_s, b_s, co_s, db_s)
        for z in range(NZ):
            late_s[n, z] = a_s[z + 1, OWN:HIGH]
    for n in range(3):
        to = block_ref[0] + 5 + n

        @pl.when(to < NB)
        def _(n=n, to=to):
            to = jnp.minimum(to, NB - 1)

            def send(m, z, rows):
                out_ref[to, m * HALF : (m + 1) * HALF] = late_s[n, z, rows]

            cut(core_ref, side_ref, send)


def cut(core_ref, side_ref, body):
    def each(rows):
        for n, (y, p) in enumerate(LAYERS):
            body(n, 2 * (2 * y + side_ref[0]) + p, rows)

    for core in range(2):
        pl.when(core_ref[0] == core)(functools.partial(each, slice(core * HALF, (core + 1) * HALF)))


SWEEP_SCRATCH = (
    pltpu.VMEM((NZ + 2, WIN, LANES), F32),
    pltpu.VMEM((NZ + 2, WIN, LANES), F32),
    pltpu.VMEM((NZ, WIN, LANES), F32),
)


def collect_body(core_ref, side_ref, got_ref, early_ref, late_ref, out_ref):
    def fill(n, z, rows):
        y, p = LAYERS[n]
        total = got_ref[0, n * HALF : (n + 1) * HALF]
        for b in range(1, NB):
            total = total + got_ref[b, n * HALF : (n + 1) * HALF]
        states = [early_ref[t, z, rows] for t in range(6)] + [late_ref[z, rows], total]
        for t in range(8):
            for r in range(3):
                out_ref[t * 4 + y, 3 * p + r] = states[t][2 * r : 2 * r + 2]

    cut(core_ref, side_ref, fill)


def home_body(got_ref, out_ref):
    for zl in range(4):
        for y in range(4):
            for core in range(2):
                for p in range(2):
                    for r in range(3):
                        row = chip_order(zl, y) * STRIP + core * HALF + 2 * r
                        out_ref[p, row : row + 2] = got_ref[(zl * 2 + core) * 4 + y, 3 * p + r]


def on_device(guess, source, diffusivity, initial):
    guess = guess[0]
    source = source[0]
    core = lax.axis_index("core")[None]
    side = lax.axis_index("zhi")[None]
    place = lax.axis_index(("zl", "core"))[None]
    block = lax.axis_index(BLOCKS)[None]

    def onward(mine, place):
        route = []
        for b in range(NB - 1):
            for y in range(4):
                for zhi in range(2):
                    to = zhi if b % 2 == 0 else 1 - zhi
                    route.append((((b * 8 + 7) * 4 + y) * 2 + zhi, (((b + 1) * 8 + place) * 4 + y) * 2 + to))
        return lax.ppermute(mine, AXES, route)

    half0, half1 = call(halves_body, [sds(2, CHIPS, 3, 2, LANES)] * 2, guess)
    prev0, prev1 = onward(half0, 0), onward(half1, 1)
    flip = ((block > 0) & (block % 2 == 0)).astype(jnp.int32)
    (base,) = call(home_fields_body, [sds(64, 9, 2, LANES)], place, source, diffusivity, initial, smem=1)
    vmem = pl.BlockSpec(memory_space=pltpu.VMEM)
    sent = pl.pallas_call(
        previous_body,
        out_shape=sds(64, 9, 2, LANES),
        in_specs=[pl.BlockSpec(memory_space=pltpu.SMEM)] * 2 + [vmem] * 3,
        out_specs=vmem,
        input_output_aliases={4: 0},
        compiler_params=pltpu.CompilerParams(vmem_limit_bytes=12 * 1024 * 1024),
    )(place, block, prev0, prev1, base)
    strips = lax.all_to_all(sent, BLOCK, 0, 0, tiled=True).reshape(8, 8, 9, 2, LANES)

    def swap(mine):
        return lax.ppermute(mine, "core", [(0, 1), (1, 0)])

    def from_neighbour(mine):
        return lax.ppermute(mine, ("zl", "core", "y"), neighbour_route())

    def exchange(mine, beside):
        got = from_neighbour(mine)
        got, beside = lax.optimization_barrier((got, beside))
        return got, swap(got), beside

    f, k, start, message = call(
        pack_body,
        [sds(8, NZ, STRIP, LANES), sds(NZ, WIN, LANES), sds(1, 8, PAIR, LANES), sds(4, 8, PAIR, LANES)],
        core, flip, strips, swap(strips), smem=2,
    )
    flops = NZ * WIN * LANES * 15
    both_rates = call(
        coefficients_body, [sds(7, NZ, WIN, LANES)] * 2, k, flops=6 * flops,
        scratch=(pltpu.VMEM((NZ + 2, WIN, LANES), F32),),
    )
    got, got2, (fine, coarse) = exchange(message, both_rates)
    v_early, state = call(
        early_body, [sds(6, NZ, STRIP, LANES), sds(3, 8, PAIR, LANES)],
        core, fine, f, start, got, got2, smem=1, flops=12 * flops,
        scratch=SWEEP_SCRATCH + (pltpu.VMEM((6, NZ, WIN, LANES), F32),),
    )
    (start_g,) = call(
        start_body, [sds(NZ, WIN, LANES)],
        core, block, coarse, start, got, got2, smem=2, flops=2 * flops, scratch=SWEEP_SCRATCH,
    )
    state_got, state_got2, start_g = exchange(state, start_g)
    v_late, first_powers, last = call(
        late_body, [sds(NZ, STRIP, LANES), sds(5, NZ, STRIP, LANES), sds(1, 8, PAIR, LANES)],
        core, fine, coarse, state, state_got, state_got2, start_g, smem=1, flops=12 * flops,
        scratch=SWEEP_SCRATCH + (pltpu.VMEM((NZ + 2, WIN, LANES), F32),),
    )
    last_got = from_neighbour(last)
    (base,) = call(early_powers_body, [sds(NB, 8 * HALF, LANES)], core, side, block, first_powers, smem=3)
    last_got, base = lax.optimization_barrier((last_got, base))
    smem = pl.BlockSpec(memory_space=pltpu.SMEM)
    powers = pl.pallas_call(
        powers_body,
        out_shape=sds(NB, 8 * HALF, LANES),
        in_specs=[smem] * 3 + [vmem] * 4,
        out_specs=vmem,
        scratch_shapes=SWEEP_SCRATCH + (pltpu.VMEM((3, NZ, STRIP, LANES), F32),),
        input_output_aliases={6: 0},
        compiler_params=pltpu.CompilerParams(vmem_limit_bytes=12 * 1024 * 1024),
    )(core, side, block, coarse, last, last_got, base)
    arrived = lax.all_to_all(powers, BLOCKS, 0, 0, tiled=True)
    (back,) = call(collect_body, [sds(32, 6, 2, LANES)], core, side, arrived, v_early, v_late, smem=2)
    returned = lax.all_to_all(back, ("zl", "core", "y"), 0, 0, tiled=True)
    (result,) = call(home_body, [sds(2, NY, LANES)], returned)
    return result[None]


def solution(mesh):
    fine = Mesh(mesh.devices.reshape(SIZES), AXES)
    tm = ("x", "zh", "zl", "core")
    space = ("y", "zhi")
    in_specs = (P(tm, space, None, None), P(tm, space, None, None), P(space, None, None), P(space, None, None))
    out_specs = P(tm, space, None, None)
    return jax.shard_map(on_device, mesh=fine, in_specs=in_specs, out_specs=out_specs, check_vma=False)
```

```python
import functools

import jax
import jax.numpy as jnp
from jax import lax
from jax.experimental import pallas as pl
from jax.experimental.pallas import tpu as pltpu
from jax.sharding import Mesh, PartitionSpec as P

F32 = jnp.float32

damping = 0.8
step_size = 0.5
coarse_size = 4.0
z_weight = 8.0

AXES = ("x", "zh", "zl", "core", "y", "zhi")
SIZES = (4, 2, 4, 2, 4, 2)
BLOCK = ("zl", "core", "y", "zhi")
BLOCKS = ("x", "zh")
NB = 8
NZ = 16
NY = 192
CHIPS = 16
STRIP = NY // CHIPS
PAIR = 2 * STRIP
HALF = STRIP // 2
LANES = 128
LAYERS = [(y, p) for y in range(4) for p in range(2)]
LOW, OWN, HIGH, WIN = 4, 16, 28, 40


def chip_order(zl, y):
    return zl * 4 + (y if zl % 2 == 0 else 3 - y)


def neighbour_route():
    place = {chip_order(zl, y): (zl, y) for zl in range(4) for y in range(4)}
    route = []
    for core, step in ((0, 1), (1, -1)):
        for m in range(CHIPS):
            if 0 <= m + step < CHIPS:
                (zl, y), (to_zl, to_y) = place[m], place[m + step]
                route.append(((zl * 2 + core) * 4 + y, (to_zl * 2 + core) * 4 + to_y))
    return route


def at(z, first, last):
    return slice((z % 2) * STRIP + first, (z % 2) * STRIP + last)


def call(body, outs, *args, scratch=(), smem=0, flops=0):
    specs = [pl.BlockSpec(memory_space=pltpu.SMEM)] * smem
    specs += [pl.BlockSpec(memory_space=pltpu.VMEM)] * (len(args) - smem)
    out_specs = [pl.BlockSpec(memory_space=pltpu.VMEM)] * len(outs)
    size = sum(4 * a.size for a in args) + sum(4 * o.size for o in outs)
    return pl.pallas_call(
        body,
        out_shape=list(outs),
        in_specs=specs,
        out_specs=out_specs,
        scratch_shapes=list(scratch),
        compiler_params=pltpu.CompilerParams(vmem_limit_bytes=12 * 1024 * 1024),
        cost_estimate=pl.CostEstimate(flops=flops, bytes_accessed=size, transcendentals=0),
    )(*args)


def sds(*shape):
    return jax.ShapeDtypeStruct(shape, F32)


def targets():
    for zl in range(4):
        for y in range(4):
            for zhi in range(2):
                for core in range(2):
                    yield ((zl * 2 + core) * 4 + y) * 2 + zhi, core, chip_order(zl, y)


def halves_body(guess_ref, half0_ref, half1_ref):
    for core in range(2):
        for m in range(CHIPS):
            for r in range(3):
                row = m * STRIP + 2 * r
                half0_ref[core, m, r] = guess_ref[core, row : row + 2]
                half1_ref[core, m, r] = guess_ref[core, row + 6 : row + 8]


def home_fields_body(j_ref, src_ref, cond_ref, init_ref, out_ref):
    place = j_ref[0]
    for to, core, m in targets():
        for r in range(6):
            row = m * STRIP + 2 * r
            out_ref[to, r] = src_ref[core, row : row + 2]

    def fill(ref, shift, half):
        for to, core, m in targets():
            m = m + shift
            for r in range(3):
                row = m * STRIP + 6 * half + 2 * r
                if 0 <= m < CHIPS:
                    out_ref[to, 6 + r] = ref[core, row : row + 2]
                else:
                    out_ref[to, 6 + r] = jnp.zeros((2, LANES), F32)

    for half in range(2):
        pl.when(place == half)(functools.partial(fill, init_ref, 0, half))
        for n, shift in enumerate((0, 1, -1)):
            pl.when(place == 2 + 2 * n + half)(functools.partial(fill, cond_ref, shift, half))


def previous_body(j_ref, block_ref, prev0_ref, prev1_ref, base_ref, out_ref):
    for half, prev_ref in ((0, prev0_ref), (1, prev1_ref)):

        @pl.when((j_ref[0] == half) & (block_ref[0] > 0))
        def _(prev_ref=prev_ref):
            for to, core, m in targets():
                for r in range(3):
                    out_ref[to, 6 + r] = prev_ref[core, m, r]


def by_core(core_ref, body, mine, other):
    pl.when(core_ref[0] == 0)(functools.partial(body, mine, other))
    pl.when(core_ref[0] == 1)(functools.partial(body, other, mine))


def pack_body(core_ref, flip_ref, own_ref, other_ref, f_ref, k_ref, start_ref, out_ref):
    flip = flip_ref[0]

    def order(*halves):
        for z in range(NZ):
            half, s = halves[z % 2], z // 2
            k_ref[z, 0:LOW] = jnp.zeros((LOW, LANES), F32)
            for r in range(6):
                for n in range(8):
                    f_ref[n, z, 2 * r : 2 * r + 2] = half[n, s, r]
                part, extra = r // 3, 6 + r % 3
                start = half[part, s + (1 - 2 * (s % 2)) * flip, extra]
                start_ref[0, s, at(z, 2 * r, 2 * r + 2)] = start
                out_ref[0, s, at(z, 2 * r, 2 * r + 2)] = start
                for place, base in ((6, LOW), (2, OWN), (4, HIGH)):
                    k_ref[z, base + 2 * r : base + 2 * r + 2] = half[place + part, s, extra]

    by_core(core_ref, order, own_ref, other_ref)

    @pl.when(core_ref[0] == 0)
    def _():
        for z in range(NZ):
            for n in range(3):
                rows = 11 - 2 * n
                out_ref[1 + n, z // 2, at(z, STRIP - rows, STRIP)] = f_ref[n, z, STRIP - rows : STRIP]
                out_ref[1 + n, z // 2, at(z, 0, STRIP - rows)] = f_ref[5 - n, z, rows:STRIP]

    @pl.when(core_ref[0] == 1)
    def _():
        for z in range(NZ):
            for n in range(3):
                rows = 11 - 2 * n
                out_ref[1 + n, z // 2, at(z, 0, rows)] = f_ref[n, z, 0:rows]
                out_ref[1 + n, z // 2, at(z, rows, STRIP)] = f_ref[5 - n, z, 0 : STRIP - rows]


def clear_ends(*refs):
    zero = jnp.zeros((WIN, LANES), F32)
    for ref in refs:
        ref[0] = zero
        ref[NZ + 1] = zero


def load_window(core_ref, a_s, field, own_ref, got_ref, got2_ref):
    def load(below_ref, above_ref):
        zero = jnp.zeros((LOW, LANES), F32)
        for z in range(NZ):
            a_s[z + 1, 0:LOW] = zero
            a_s[z + 1, LOW:OWN] = below_ref[field, z // 2, at(z, 0, STRIP)]
            a_s[z + 1, OWN:HIGH] = own_ref[field, z // 2, at(z, 0, STRIP)]
            a_s[z + 1, HIGH:WIN] = above_ref[field, z // 2, at(z, 0, STRIP)]

    by_core(core_ref, load, got_ref, got2_ref)


def coefficients(rate, k_s, co_s):
    lane = lax.broadcasted_iota(jnp.int32, (WIN, LANES), 1)
    first = lane == 0
    last = lane == LANES - 1

    def layer(z, carry):
        k = k_s[z + 1]
        side = 0.5 * rate
        tall = 0.5 * rate * z_weight
        c = [
            tall * (k + k_s[z]),
            tall * (k + k_s[z + 2]),
            side * (k + pltpu.roll(k, 1, 0)),
            side * (k + pltpu.roll(k, WIN - 1, 0)),
            side * (k + jnp.where(first, 0.0, pltpu.roll(k, 1, 1))),
            side * (k + jnp.where(last, 0.0, pltpu.roll(k, LANES - 1, 1))),
        ]
        total = ((c[0] + c[1]) + (c[2] + c[3])) + (c[4] + c[5])
        d = jnp.where(k > 0.0, damping / (1.0 + total), 0.0)
        co_s[0, z] = c[0] * d
        co_s[1, z] = c[1] * d
        co_s[2, z] = c[2] * d
        co_s[3, z] = c[3] * d
        co_s[4, z] = jnp.where(first, 0.0, c[4] * d)
        co_s[5, z] = jnp.where(last, 0.0, c[5] * d)
        co_s[6, z] = d
        return carry

    lax.fori_loop(0, NZ, layer, 0)


def coefficients_body(k_ref, fine_ref, coarse_ref, k_s):
    clear_ends(k_s)
    for z in range(NZ):
        k_s[z + 1] = k_ref[z]
    coefficients(step_size, k_s, fine_ref)
    coefficients(coarse_size, k_s, coarse_ref)


def one_sweep(src, dst, co_s, db_s, rows):
    tall = rows.stop - rows.start
    under, w = src[0, rows], src[1, rows]
    for z in range(NZ):
        over = src[z + 2, rows]
        acc = (db_s[z, rows] + (1.0 - damping) * w) + (co_s[0, z, rows] * under + co_s[1, z, rows] * over)
        acc = acc + (
            co_s[2, z, rows] * pltpu.roll(w, 1, 0) + co_s[3, z, rows] * pltpu.roll(w, tall - 1, 0)
        )
        acc = acc + (
            co_s[4, z, rows] * pltpu.roll(w, 1, 1) + co_s[5, z, rows] * pltpu.roll(w, LANES - 1, 1)
        )
        dst[z + 1, rows] = acc
        under, w = w, over


def step(halo, a_s, b_s, co_s, db_s, forcing=None):
    rows = slice(8, 32) if halo <= 4 else slice(8, WIN) if halo <= 8 else slice(0, WIN)
    for z in range(NZ):
        target = a_s[z + 1, rows]
        if forcing is not None:
            target = target + step_size * forcing[z, rows]
        db_s[z, rows] = co_s[6, z, rows] * target
    one_sweep(a_s, b_s, co_s, db_s, rows)
    one_sweep(b_s, a_s, co_s, db_s, rows)


def early_body(
    core_ref, co_s, f_ref, own_ref, got_ref, got2_ref, out_ref, next_ref, a_s, b_s, db_s, f_s
):
    clear_ends(a_s, b_s)
    load_window(core_ref, a_s, 0, own_ref, got_ref, got2_ref)
    for n in range(6):
        for z in range(NZ):
            f_s[n, z, OWN:HIGH] = f_ref[n, z]

    def halos(below_ref, above_ref):
        for n in range(3):
            rows = 11 - 2 * n
            for z in range(NZ):
                s = z // 2
                f_s[n, z, OWN - rows : OWN] = below_ref[1 + n, s, at(z, STRIP - rows, STRIP)]
                f_s[n, z, HIGH : HIGH + rows] = above_ref[1 + n, s, at(z, 0, rows)]
                f_s[5 - n, z, OWN - STRIP + rows : OWN] = below_ref[1 + n, s, at(z, 0, STRIP - rows)]
                f_s[5 - n, z, HIGH : HIGH + STRIP - rows] = above_ref[1 + n, s, at(z, rows, STRIP)]

    by_core(core_ref, halos, got_ref, got2_ref)
    for n in range(6):
        step(12 - 2 * n, a_s, b_s, co_s, db_s, f_s.at[n])
        for z in range(NZ):
            out_ref[n, z] = a_s[z + 1, OWN:HIGH]
    for z in range(NZ):
        next_ref[0, z // 2, at(z, 0, STRIP)] = a_s[z + 1, OWN:HIGH]
        for n in range(2):
            next_ref[1 + n, z // 2, at(z, 0, STRIP)] = f_ref[6 + n, z]


def start_body(core_ref, block_ref, co_s, own_ref, got_ref, got2_ref, out_ref, a_s, b_s, db_s):
    clear_ends(a_s, b_s)
    load_window(core_ref, a_s, 0, own_ref, got_ref, got2_ref)
    step(10, a_s, b_s, co_s, db_s)
    later = block_ref[0] > 0
    for z in range(NZ):
        out_ref[z] = jnp.where(later, a_s[z + 1], 0.0)


def late_body(
    core_ref, fine_s, co_s, own_ref, got_ref, got2_ref, start_ref,
    out_ref, pow_ref, next_ref, a_s, b_s, db_s, f_s,
):
    clear_ends(a_s, b_s)
    load_window(core_ref, a_s, 0, own_ref, got_ref, got2_ref)
    for n in range(2):
        load_window(core_ref, f_s, 1 + n, own_ref, got_ref, got2_ref)
        step(12 - 2 * n, a_s, b_s, fine_s, db_s, f_s.at[pl.ds(1, NZ)])
        if n == 0:
            for z in range(NZ):
                out_ref[z] = a_s[z + 1, OWN:HIGH]
    for z in range(NZ):
        a_s[z + 1] = a_s[z + 1] - start_ref[z]
    for n in range(5):
        if n > 0:
            step(10 - 2 * n, a_s, b_s, co_s, db_s)
        for z in range(NZ):
            pow_ref[n, z] = a_s[z + 1, OWN:HIGH]
    for z in range(NZ):
        next_ref[0, z // 2, at(z, 0, STRIP)] = a_s[z + 1, OWN:HIGH]


def early_powers_body(core_ref, side_ref, block_ref, early_ref, out_ref):
    for b in range(NB):
        power = b - block_ref[0]
        live = (power >= 0) & (power < 5)
        power = jnp.clip(power, 0, 4)

        def send(m, z, rows, b=b, power=power, live=live):
            out_ref[b, m * HALF : (m + 1) * HALF] = jnp.where(live, early_ref[power, z, rows], 0.0)

        cut(core_ref, side_ref, send)


def powers_body(
    core_ref, side_ref, block_ref, co_s, own_ref, got_ref, base_ref, out_ref, a_s, b_s, db_s, late_s
):
    clear_ends(a_s, b_s)
    for z in range(NZ):
        a_s[z + 1] = jnp.zeros((WIN, LANES), F32)
        a_s[z + 1, OWN:HIGH] = own_ref[0, z // 2, at(z, 0, STRIP)]

    def halo(rows):
        for z in range(NZ):
            a_s[z + 1, rows] = got_ref[0, z // 2, at(z, 0, STRIP)]

    pl.when(core_ref[0] == 0)(functools.partial(halo, slice(LOW, OWN)))
    pl.when(core_ref[0] == 1)(functools.partial(halo, slice(HIGH, WIN)))
    for n in range(3):
        step(6 - 2 * n, a_s, b_s, co_s, db_s)
        for z in range(NZ):
            late_s[n, z] = a_s[z + 1, OWN:HIGH]
    for n in range(3):
        to = block_ref[0] + 5 + n

        @pl.when(to < NB)
        def _(n=n, to=to):
            to = jnp.minimum(to, NB - 1)

            def send(m, z, rows):
                out_ref[to, m * HALF : (m + 1) * HALF] = late_s[n, z, rows]

            cut(core_ref, side_ref, send)


def cut(core_ref, side_ref, body):
    def each(rows):
        for n, (y, p) in enumerate(LAYERS):
            body(n, 2 * (2 * y + side_ref[0]) + p, rows)

    for core in range(2):
        pl.when(core_ref[0] == core)(functools.partial(each, slice(core * HALF, (core + 1) * HALF)))


SWEEP_SCRATCH = (
    pltpu.VMEM((NZ + 2, WIN, LANES), F32),
    pltpu.VMEM((NZ + 2, WIN, LANES), F32),
    pltpu.VMEM((NZ, WIN, LANES), F32),
)


def collect_body(core_ref, side_ref, got_ref, early_ref, late_ref, out_ref):
    def fill(n, z, rows):
        y, p = LAYERS[n]
        total = got_ref[0, n * HALF : (n + 1) * HALF]
        for b in range(1, NB):
            total = total + got_ref[b, n * HALF : (n + 1) * HALF]
        states = [early_ref[t, z, rows] for t in range(6)] + [late_ref[z, rows], total]
        for t in range(8):
            for r in range(3):
                out_ref[t * 4 + y, 3 * p + r] = states[t][2 * r : 2 * r + 2]

    cut(core_ref, side_ref, fill)


def home_body(got_ref, out_ref):
    for zl in range(4):
        for y in range(4):
            for core in range(2):
                for p in range(2):
                    for r in range(3):
                        row = chip_order(zl, y) * STRIP + core * HALF + 2 * r
                        out_ref[p, row : row + 2] = got_ref[(zl * 2 + core) * 4 + y, 3 * p + r]


def on_device(guess, source, diffusivity, initial):
    guess = guess[0]
    source = source[0]
    core = lax.axis_index("core")[None]
    side = lax.axis_index("zhi")[None]
    place = lax.axis_index(("zl", "core"))[None]
    block = lax.axis_index(BLOCKS)[None]

    def onward(mine, place):
        route = []
        for b in range(NB - 1):
            for y in range(4):
                for zhi in range(2):
                    to = zhi if b % 2 == 0 else 1 - zhi
                    route.append((((b * 8 + 7) * 4 + y) * 2 + zhi, (((b + 1) * 8 + place) * 4 + y) * 2 + to))
        return lax.ppermute(mine, AXES, route)

    half0, half1 = call(halves_body, [sds(2, CHIPS, 3, 2, LANES)] * 2, guess)
    prev0, prev1 = onward(half0, 0), onward(half1, 1)
    flip = ((block > 0) & (block % 2 == 0)).astype(jnp.int32)
    (base,) = call(home_fields_body, [sds(64, 9, 2, LANES)], place, source, diffusivity, initial, smem=1)
    vmem = pl.BlockSpec(memory_space=pltpu.VMEM)
    sent = pl.pallas_call(
        previous_body,
        out_shape=sds(64, 9, 2, LANES),
        in_specs=[pl.BlockSpec(memory_space=pltpu.SMEM)] * 2 + [vmem] * 3,
        out_specs=vmem,
        input_output_aliases={4: 0},
        compiler_params=pltpu.CompilerParams(vmem_limit_bytes=12 * 1024 * 1024),
    )(place, block, prev0, prev1, base)
    strips = lax.all_to_all(sent, BLOCK, 0, 0, tiled=True).reshape(8, 8, 9, 2, LANES)

    def swap(mine):
        return lax.ppermute(mine, "core", [(0, 1), (1, 0)])

    def from_neighbour(mine):
        return lax.ppermute(mine, ("zl", "core", "y"), neighbour_route())

    def exchange(mine, beside):
        got = from_neighbour(mine)
        got, beside = lax.optimization_barrier((got, beside))
        return got, swap(got), beside

    f, k, start, message = call(
        pack_body,
        [sds(8, NZ, STRIP, LANES), sds(NZ, WIN, LANES), sds(1, 8, PAIR, LANES), sds(4, 8, PAIR, LANES)],
        core, flip, strips, swap(strips), smem=2,
    )
    flops = NZ * WIN * LANES * 15
    both_rates = call(
        coefficients_body, [sds(7, NZ, WIN, LANES)] * 2, k, flops=6 * flops,
        scratch=(pltpu.VMEM((NZ + 2, WIN, LANES), F32),),
    )
    got, got2, (fine, coarse) = exchange(message, both_rates)
    v_early, state = call(
        early_body, [sds(6, NZ, STRIP, LANES), sds(3, 8, PAIR, LANES)],
        core, fine, f, start, got, got2, smem=1, flops=12 * flops,
        scratch=SWEEP_SCRATCH + (pltpu.VMEM((6, NZ, WIN, LANES), F32),),
    )
    (start_g,) = call(
        start_body, [sds(NZ, WIN, LANES)],
        core, block, coarse, start, got, got2, smem=2, flops=2 * flops, scratch=SWEEP_SCRATCH,
    )
    state_got, state_got2, start_g = exchange(state, start_g)
    v_late, first_powers, last = call(
        late_body, [sds(NZ, STRIP, LANES), sds(5, NZ, STRIP, LANES), sds(1, 8, PAIR, LANES)],
        core, fine, coarse, state, state_got, state_got2, start_g, smem=1, flops=12 * flops,
        scratch=SWEEP_SCRATCH + (pltpu.VMEM((NZ + 2, WIN, LANES), F32),),
    )
    last_got = from_neighbour(last)
    (base,) = call(early_powers_body, [sds(NB, 8 * HALF, LANES)], core, side, block, first_powers, smem=3)
    last_got, base = lax.optimization_barrier((last_got, base))
    smem = pl.BlockSpec(memory_space=pltpu.SMEM)
    powers = pl.pallas_call(
        powers_body,
        out_shape=sds(NB, 8 * HALF, LANES),
        in_specs=[smem] * 3 + [vmem] * 4,
        out_specs=vmem,
        scratch_shapes=SWEEP_SCRATCH + (pltpu.VMEM((3, NZ, STRIP, LANES), F32),),
        input_output_aliases={6: 0},
        compiler_params=pltpu.CompilerParams(vmem_limit_bytes=12 * 1024 * 1024),
    )(core, side, block, coarse, last, last_got, base)
    arrived = lax.all_to_all(powers, BLOCKS, 0, 0, tiled=True)
    (back,) = call(collect_body, [sds(32, 6, 2, LANES)], core, side, arrived, v_early, v_late, smem=2)
    returned = lax.all_to_all(back, ("zl", "core", "y"), 0, 0, tiled=True)
    (result,) = call(home_body, [sds(2, NY, LANES)], returned)
    return result[None]


def solution(mesh):
    fine = Mesh(mesh.devices.reshape(SIZES), AXES)
    tm = ("x", "zh", "zl", "core")
    space = ("y", "zhi")
    in_specs = (P(tm, space, None, None), P(tm, space, None, None), P(space, None, None), P(space, None, None))
    out_specs = P(tm, space, None, None)
    return jax.shard_map(on_device, mesh=fine, in_specs=in_specs, out_specs=out_specs, check_vma=False)
```

```python
import functools

import jax
import jax.numpy as jnp
from jax import lax
from jax.experimental import pallas as pl
from jax.experimental.pallas import tpu as pltpu
from jax.sharding import Mesh, PartitionSpec as P

F32 = jnp.float32

damping = 0.8
step_size = 0.5
coarse_size = 4.0
z_weight = 8.0

AXES = ("x", "zh", "zl", "core", "y", "zhi")
SIZES = (4, 2, 4, 2, 4, 2)
BLOCK = ("zl", "core", "y", "zhi")
BLOCKS = ("x", "zh")
NB = 8
NZ = 16
NY = 192
CHIPS = 16
STRIP = NY // CHIPS
PAIR = 2 * STRIP
HALF = STRIP // 2
LANES = 128
LAYERS = [(y, p) for y in range(4) for p in range(2)]
LOW, OWN, HIGH, WIN = 4, 16, 28, 40


def chip_order(zl, y):
    return zl * 4 + (y if zl % 2 == 0 else 3 - y)


def neighbour_route():
    place = {chip_order(zl, y): (zl, y) for zl in range(4) for y in range(4)}
    route = []
    for core, step in ((0, 1), (1, -1)):
        for m in range(CHIPS):
            if 0 <= m + step < CHIPS:
                (zl, y), (to_zl, to_y) = place[m], place[m + step]
                route.append(((zl * 2 + core) * 4 + y, (to_zl * 2 + core) * 4 + to_y))
    return route


def at(z, first, last):
    return slice((z % 2) * STRIP + first, (z % 2) * STRIP + last)


def call(body, outs, *args, scratch=(), smem=0, flops=0):
    specs = [pl.BlockSpec(memory_space=pltpu.SMEM)] * smem
    specs += [pl.BlockSpec(memory_space=pltpu.VMEM)] * (len(args) - smem)
    out_specs = [pl.BlockSpec(memory_space=pltpu.VMEM)] * len(outs)
    size = sum(4 * a.size for a in args) + sum(4 * o.size for o in outs)
    return pl.pallas_call(
        body,
        out_shape=list(outs),
        in_specs=specs,
        out_specs=out_specs,
        scratch_shapes=list(scratch),
        compiler_params=pltpu.CompilerParams(vmem_limit_bytes=12 * 1024 * 1024),
        cost_estimate=pl.CostEstimate(flops=flops, bytes_accessed=size, transcendentals=0),
    )(*args)


def sds(*shape):
    return jax.ShapeDtypeStruct(shape, F32)


def targets():
    for zl in range(4):
        for y in range(4):
            for zhi in range(2):
                for core in range(2):
                    yield ((zl * 2 + core) * 4 + y) * 2 + zhi, core, chip_order(zl, y)


def halves_body(guess_ref, half0_ref, half1_ref):
    for core in range(2):
        for m in range(CHIPS):
            for r in range(3):
                row = m * STRIP + 2 * r
                half0_ref[core, m, r] = guess_ref[core, row : row + 2]
                half1_ref[core, m, r] = guess_ref[core, row + 6 : row + 8]


def home_fields_body(j_ref, src_ref, cond_ref, init_ref, out_ref):
    place = j_ref[0]
    for to, core, m in targets():
        for r in range(6):
            row = m * STRIP + 2 * r
            out_ref[to, r] = src_ref[core, row : row + 2]

    def fill(ref, shift, half):
        for to, core, m in targets():
            m = m + shift
            for r in range(3):
                row = m * STRIP + 6 * half + 2 * r
                if 0 <= m < CHIPS:
                    out_ref[to, 6 + r] = ref[core, row : row + 2]
                else:
                    out_ref[to, 6 + r] = jnp.zeros((2, LANES), F32)

    for half in range(2):
        pl.when(place == half)(functools.partial(fill, init_ref, 0, half))
        for n, shift in enumerate((0, 1, -1)):
            pl.when(place == 2 + 2 * n + half)(functools.partial(fill, cond_ref, shift, half))


def previous_body(j_ref, block_ref, prev0_ref, prev1_ref, base_ref, out_ref):
    for half, prev_ref in ((0, prev0_ref), (1, prev1_ref)):

        @pl.when((j_ref[0] == half) & (block_ref[0] > 0))
        def _(prev_ref=prev_ref):
            for to, core, m in targets():
                for r in range(3):
                    out_ref[to, 6 + r] = prev_ref[core, m, r]


def by_core(core_ref, body, mine, other):
    pl.when(core_ref[0] == 0)(functools.partial(body, mine, other))
    pl.when(core_ref[0] == 1)(functools.partial(body, other, mine))


def pack_body(core_ref, flip_ref, own_ref, other_ref, f_ref, k_ref, start_ref, out_ref):
    flip = flip_ref[0]

    def order(*halves):
        for z in range(NZ):
            half, s = halves[z % 2], z // 2
            k_ref[z, 0:LOW] = jnp.zeros((LOW, LANES), F32)
            for r in range(6):
                for n in range(8):
                    f_ref[n, z, 2 * r : 2 * r + 2] = half[n, s, r]
                part, extra = r // 3, 6 + r % 3
                start = half[part, s + (1 - 2 * (s % 2)) * flip, extra]
                start_ref[0, s, at(z, 2 * r, 2 * r + 2)] = start
                out_ref[0, s, at(z, 2 * r, 2 * r + 2)] = start
                for place, base in ((6, LOW), (2, OWN), (4, HIGH)):
                    k_ref[z, base + 2 * r : base + 2 * r + 2] = half[place + part, s, extra]

    by_core(core_ref, order, own_ref, other_ref)

    @pl.when(core_ref[0] == 0)
    def _():
        for z in range(NZ):
            for n in range(3):
                rows = 11 - 2 * n
                out_ref[1 + n, z // 2, at(z, STRIP - rows, STRIP)] = f_ref[n, z, STRIP - rows : STRIP]
                out_ref[1 + n, z // 2, at(z, 0, STRIP - rows)] = f_ref[5 - n, z, rows:STRIP]

    @pl.when(core_ref[0] == 1)
    def _():
        for z in range(NZ):
            for n in range(3):
                rows = 11 - 2 * n
                out_ref[1 + n, z // 2, at(z, 0, rows)] = f_ref[n, z, 0:rows]
                out_ref[1 + n, z // 2, at(z, rows, STRIP)] = f_ref[5 - n, z, 0 : STRIP - rows]


def clear_ends(*refs):
    zero = jnp.zeros((WIN, LANES), F32)
    for ref in refs:
        ref[0] = zero
        ref[NZ + 1] = zero


def load_window(core_ref, a_s, field, own_ref, got_ref, got2_ref):
    def load(below_ref, above_ref):
        zero = jnp.zeros((LOW, LANES), F32)
        for z in range(NZ):
            a_s[z + 1, 0:LOW] = zero
            a_s[z + 1, LOW:OWN] = below_ref[field, z // 2, at(z, 0, STRIP)]
            a_s[z + 1, OWN:HIGH] = own_ref[field, z // 2, at(z, 0, STRIP)]
            a_s[z + 1, HIGH:WIN] = above_ref[field, z // 2, at(z, 0, STRIP)]

    by_core(core_ref, load, got_ref, got2_ref)


def coefficients(rate, k_s, co_s):
    lane = lax.broadcasted_iota(jnp.int32, (WIN, LANES), 1)
    first = lane == 0
    last = lane == LANES - 1

    def layer(z, carry):
        k = k_s[z + 1]
        side = 0.5 * rate
        tall = 0.5 * rate * z_weight
        c = [
            tall * (k + k_s[z]),
            tall * (k + k_s[z + 2]),
            side * (k + pltpu.roll(k, 1, 0)),
            side * (k + pltpu.roll(k, WIN - 1, 0)),
            side * (k + jnp.where(first, 0.0, pltpu.roll(k, 1, 1))),
            side * (k + jnp.where(last, 0.0, pltpu.roll(k, LANES - 1, 1))),
        ]
        total = ((c[0] + c[1]) + (c[2] + c[3])) + (c[4] + c[5])
        d = jnp.where(k > 0.0, damping / (1.0 + total), 0.0)
        co_s[0, z] = c[0] * d
        co_s[1, z] = c[1] * d
        co_s[2, z] = c[2] * d
        co_s[3, z] = c[3] * d
        co_s[4, z] = jnp.where(first, 0.0, c[4] * d)
        co_s[5, z] = jnp.where(last, 0.0, c[5] * d)
        co_s[6, z] = d
        return carry

    lax.fori_loop(0, NZ, layer, 0)


def coefficients_body(k_ref, fine_ref, coarse_ref, k_s):
    clear_ends(k_s)
    for z in range(NZ):
        k_s[z + 1] = k_ref[z]
    coefficients(step_size, k_s, fine_ref)
    coefficients(coarse_size, k_s, coarse_ref)


def one_sweep(src, dst, co_s, db_s, rows):
    tall = rows.stop - rows.start
    under, w = src[0, rows], src[1, rows]
    for z in range(NZ):
        over = src[z + 2, rows]
        acc = (db_s[z, rows] + (1.0 - damping) * w) + (co_s[0, z, rows] * under + co_s[1, z, rows] * over)
        acc = acc + (
            co_s[2, z, rows] * pltpu.roll(w, 1, 0) + co_s[3, z, rows] * pltpu.roll(w, tall - 1, 0)
        )
        acc = acc + (
            co_s[4, z, rows] * pltpu.roll(w, 1, 1) + co_s[5, z, rows] * pltpu.roll(w, LANES - 1, 1)
        )
        dst[z + 1, rows] = acc
        under, w = w, over


def step(halo, a_s, b_s, co_s, db_s, forcing=None):
    rows = slice(8, 32) if halo <= 4 else slice(8, WIN) if halo <= 8 else slice(0, WIN)
    for z in range(NZ):
        target = a_s[z + 1, rows]
        if forcing is not None:
            target = target + step_size * forcing[z, rows]
        db_s[z, rows] = co_s[6, z, rows] * target
    one_sweep(a_s, b_s, co_s, db_s, rows)
    one_sweep(b_s, a_s, co_s, db_s, rows)


def early_body(
    core_ref, co_s, f_ref, own_ref, got_ref, got2_ref, out_ref, next_ref, a_s, b_s, db_s, f_s
):
    clear_ends(a_s, b_s)
    load_window(core_ref, a_s, 0, own_ref, got_ref, got2_ref)
    for n in range(6):
        for z in range(NZ):
            f_s[n, z] = jnp.zeros((WIN, LANES), F32)
            f_s[n, z, OWN:HIGH] = f_ref[n, z]

    def halos(below_ref, above_ref):
        for n in range(3):
            rows = 11 - 2 * n
            for z in range(NZ):
                s = z // 2
                f_s[n, z, OWN - rows : OWN] = below_ref[1 + n, s, at(z, STRIP - rows, STRIP)]
                f_s[n, z, HIGH : HIGH + rows] = above_ref[1 + n, s, at(z, 0, rows)]
                f_s[5 - n, z, OWN - STRIP + rows : OWN] = below_ref[1 + n, s, at(z, 0, STRIP - rows)]
                f_s[5 - n, z, HIGH : HIGH + STRIP - rows] = above_ref[1 + n, s, at(z, rows, STRIP)]

    by_core(core_ref, halos, got_ref, got2_ref)
    for n in range(6):
        step(12 - 2 * n, a_s, b_s, co_s, db_s, f_s.at[n])
        for z in range(NZ):
            out_ref[n, z] = a_s[z + 1, OWN:HIGH]
    for z in range(NZ):
        next_ref[0, z // 2, at(z, 0, STRIP)] = a_s[z + 1, OWN:HIGH]
        for n in range(2):
            next_ref[1 + n, z // 2, at(z, 0, STRIP)] = f_ref[6 + n, z]


def start_body(core_ref, block_ref, co_s, own_ref, got_ref, got2_ref, out_ref, a_s, b_s, db_s):
    clear_ends(a_s, b_s)
    load_window(core_ref, a_s, 0, own_ref, got_ref, got2_ref)
    step(10, a_s, b_s, co_s, db_s)
    later = block_ref[0] > 0
    for z in range(NZ):
        out_ref[z] = jnp.where(later, a_s[z + 1], 0.0)


def late_body(
    core_ref, fine_s, co_s, own_ref, got_ref, got2_ref, start_ref,
    out_ref, pow_ref, next_ref, edge_ref, a_s, b_s, db_s, f_s,
):
    clear_ends(a_s, b_s)
    load_window(core_ref, a_s, 0, own_ref, got_ref, got2_ref)
    for n in range(2):
        load_window(core_ref, f_s, 1 + n, own_ref, got_ref, got2_ref)
        step(12 - 2 * n, a_s, b_s, fine_s, db_s, f_s.at[pl.ds(1, NZ)])
        if n == 0:
            for z in range(NZ):
                out_ref[z] = a_s[z + 1, OWN:HIGH]
    for z in range(NZ):
        a_s[z + 1] = a_s[z + 1] - start_ref[z]
    for n in range(5):
        if n > 0:
            step(10 - 2 * n, a_s, b_s, co_s, db_s)
        for z in range(NZ):
            pow_ref[n, z] = a_s[z + 1, OWN:HIGH]
    for z in range(NZ):
        next_ref[0, z // 2, at(z, 0, STRIP)] = a_s[z + 1, OWN:HIGH]

    def edge(rows):
        for z in range(NZ):
            edge_ref[z // 4, HALF * (z % 4) : HALF * (z % 4) + HALF] = a_s[z + 1, rows]

    pl.when(core_ref[0] == 0)(functools.partial(edge, slice(HIGH - HALF, HIGH)))
    pl.when(core_ref[0] == 1)(functools.partial(edge, slice(OWN, OWN + HALF)))


def early_powers_body(core_ref, side_ref, block_ref, early_ref, out_ref):
    for b in range(NB):
        power = b - block_ref[0]
        live = (power >= 0) & (power < 5)
        power = jnp.clip(power, 0, 4)

        def send(m, z, rows, b=b, power=power, live=live):
            out_ref[b, m * HALF : (m + 1) * HALF] = jnp.where(live, early_ref[power, z, rows], 0.0)

        cut(core_ref, side_ref, send)


def powers_body(
    core_ref, side_ref, block_ref, co_s, own_ref, got_ref, base_ref, out_ref, a_s, b_s, db_s, late_s
):
    clear_ends(a_s, b_s)
    for z in range(NZ):
        a_s[z + 1] = jnp.zeros((WIN, LANES), F32)
        a_s[z + 1, OWN:HIGH] = own_ref[0, z // 2, at(z, 0, STRIP)]

    def halo(rows):
        for z in range(NZ):
            a_s[z + 1, rows] = got_ref[z // 4, HALF * (z % 4) : HALF * (z % 4) + HALF]

    pl.when(core_ref[0] == 0)(functools.partial(halo, slice(OWN - HALF, OWN)))
    pl.when(core_ref[0] == 1)(functools.partial(halo, slice(HIGH, HIGH + HALF)))
    for n in range(3):
        step(6 - 2 * n, a_s, b_s, co_s, db_s)
        for z in range(NZ):
            late_s[n, z] = a_s[z + 1, OWN:HIGH]
    for n in range(3):
        to = block_ref[0] + 5 + n

        @pl.when(to < NB)
        def _(n=n, to=to):
            to = jnp.minimum(to, NB - 1)

            def send(m, z, rows):
                out_ref[to, m * HALF : (m + 1) * HALF] = late_s[n, z, rows]

            cut(core_ref, side_ref, send)


def cut(core_ref, side_ref, body):
    def each(rows):
        for n, (y, p) in enumerate(LAYERS):
            body(n, 2 * (2 * y + side_ref[0]) + p, rows)

    for core in range(2):
        pl.when(core_ref[0] == core)(functools.partial(each, slice(core * HALF, (core + 1) * HALF)))


SWEEP_SCRATCH = (
    pltpu.VMEM((NZ + 2, WIN, LANES), F32),
    pltpu.VMEM((NZ + 2, WIN, LANES), F32),
    pltpu.VMEM((NZ, WIN, LANES), F32),
)


def collect_body(core_ref, side_ref, got_ref, early_ref, late_ref, out_ref):
    def fill(n, z, rows):
        y, p = LAYERS[n]
        total = got_ref[0, n * HALF : (n + 1) * HALF]
        for b in range(1, NB):
            total = total + got_ref[b, n * HALF : (n + 1) * HALF]
        states = [early_ref[t, z, rows] for t in range(6)] + [late_ref[z, rows], total]
        for t in range(8):
            for r in range(3):
                out_ref[t * 4 + y, 3 * p + r] = states[t][2 * r : 2 * r + 2]

    cut(core_ref, side_ref, fill)


def home_body(got_ref, out_ref):
    for zl in range(4):
        for y in range(4):
            for core in range(2):
                for p in range(2):
                    for r in range(3):
                        row = chip_order(zl, y) * STRIP + core * HALF + 2 * r
                        out_ref[p, row : row + 2] = got_ref[(zl * 2 + core) * 4 + y, 3 * p + r]


def on_device(guess, source, diffusivity, initial):
    guess = guess[0]
    source = source[0]
    core = lax.axis_index("core")[None]
    side = lax.axis_index("zhi")[None]
    place = lax.axis_index(("zl", "core"))[None]
    block = lax.axis_index(BLOCKS)[None]

    def onward(mine, place):
        route = []
        for b in range(NB - 1):
            for y in range(4):
                for zhi in range(2):
                    to = zhi if b % 2 == 0 else 1 - zhi
                    route.append((((b * 8 + 7) * 4 + y) * 2 + zhi, (((b + 1) * 8 + place) * 4 + y) * 2 + to))
        return lax.ppermute(mine, AXES, route)

    half0, half1 = call(halves_body, [sds(2, CHIPS, 3, 2, LANES)] * 2, guess)
    prev0, prev1 = onward(half0, 0), onward(half1, 1)
    flip = ((block > 0) & (block % 2 == 0)).astype(jnp.int32)
    (base,) = call(home_fields_body, [sds(64, 9, 2, LANES)], place, source, diffusivity, initial, smem=1)
    vmem = pl.BlockSpec(memory_space=pltpu.VMEM)
    sent = pl.pallas_call(
        previous_body,
        out_shape=sds(64, 9, 2, LANES),
        in_specs=[pl.BlockSpec(memory_space=pltpu.SMEM)] * 2 + [vmem] * 3,
        out_specs=vmem,
        input_output_aliases={4: 0},
        compiler_params=pltpu.CompilerParams(vmem_limit_bytes=12 * 1024 * 1024),
    )(place, block, prev0, prev1, base)
    strips = lax.all_to_all(sent, BLOCK, 0, 0, tiled=True).reshape(8, 8, 9, 2, LANES)

    def swap(mine):
        return lax.ppermute(mine, "core", [(0, 1), (1, 0)])

    def from_neighbour(mine):
        return lax.ppermute(mine, ("zl", "core", "y"), neighbour_route())

    def exchange(mine, beside):
        got = from_neighbour(mine)
        got, beside = lax.optimization_barrier((got, beside))
        return got, swap(got), beside

    f, k, start, message = call(
        pack_body,
        [sds(8, NZ, STRIP, LANES), sds(NZ, WIN, LANES), sds(1, 8, PAIR, LANES), sds(4, 8, PAIR, LANES)],
        core, flip, strips, swap(strips), smem=2,
    )
    flops = NZ * WIN * LANES * 15
    both_rates = call(
        coefficients_body, [sds(7, NZ, WIN, LANES)] * 2, k, flops=6 * flops,
        scratch=(pltpu.VMEM((NZ + 2, WIN, LANES), F32),),
    )
    got, got2, (fine, coarse) = exchange(message, both_rates)
    v_early, state = call(
        early_body, [sds(6, NZ, STRIP, LANES), sds(3, 8, PAIR, LANES)],
        core, fine, f, start, got, got2, smem=1, flops=12 * flops,
        scratch=SWEEP_SCRATCH + (pltpu.VMEM((6, NZ, WIN, LANES), F32),),
    )
    (start_g,) = call(
        start_body, [sds(NZ, WIN, LANES)],
        core, block, coarse, start, got, got2, smem=2, flops=2 * flops, scratch=SWEEP_SCRATCH,
    )
    state_got, state_got2, start_g = exchange(state, start_g)
    v_late, first_powers, last, edge = call(
        late_body, [sds(NZ, STRIP, LANES), sds(5, NZ, STRIP, LANES), sds(1, 8, PAIR, LANES), sds(4, 4 * HALF, LANES)],
        core, fine, coarse, state, state_got, state_got2, start_g, smem=1, flops=12 * flops,
        scratch=SWEEP_SCRATCH + (pltpu.VMEM((NZ + 2, WIN, LANES), F32),),
    )
    last_got = from_neighbour(edge)
    (base,) = call(early_powers_body, [sds(NB, 8 * HALF, LANES)], core, side, block, first_powers, smem=3)
    last_got, base = lax.optimization_barrier((last_got, base))
    smem = pl.BlockSpec(memory_space=pltpu.SMEM)
    powers = pl.pallas_call(
        powers_body,
        out_shape=sds(NB, 8 * HALF, LANES),
        in_specs=[smem] * 3 + [vmem] * 4,
        out_specs=vmem,
        scratch_shapes=SWEEP_SCRATCH + (pltpu.VMEM((3, NZ, STRIP, LANES), F32),),
        input_output_aliases={6: 0},
        compiler_params=pltpu.CompilerParams(vmem_limit_bytes=12 * 1024 * 1024),
    )(core, side, block, coarse, last, last_got, base)
    arrived = lax.all_to_all(powers, BLOCKS, 0, 0, tiled=True)
    (back,) = call(collect_body, [sds(32, 6, 2, LANES)], core, side, arrived, v_early, v_late, smem=2)
    returned = lax.all_to_all(back, ("zl", "core", "y"), 0, 0, tiled=True)
    (result,) = call(home_body, [sds(2, NY, LANES)], returned)
    return result[None]


def solution(mesh):
    fine = Mesh(mesh.devices.reshape(SIZES), AXES)
    tm = ("x", "zh", "zl", "core")
    space = ("y", "zhi")
    in_specs = (P(tm, space, None, None), P(tm, space, None, None), P(space, None, None), P(space, None, None))
    out_specs = P(tm, space, None, None)
    return jax.shard_map(on_device, mesh=fine, in_specs=in_specs, out_specs=out_specs, check_vma=False)
```
